32 devices in a mesh: ifg: 8 (over z, x), tile: 4 (over y, core).
Axes of the slice: x: 2, y: 2, z: 4, core: 2. Of those that a mesh axis runs over, the one named last changes fastest.
Arguments:
- ifgs: bfloat16 [1152, 8, 1024], P('ifg', 'tile'), may hold values from -12 to 12
- pairs: int32 [1152, 2], replicated, may hold values from 0 to 299, as said below
- pseudo_inverse: bfloat16 [300, 1152], P(None, 'ifg'), may hold values from -0.1875 to 0.1875
- ref_pixels: int32 [64], replicated, may hold values from 0 to 8191
- epochs: int32 [8], replicated, may hold values from 8 to 291
Outputs:
- coefficients: float32 [16, 8, 1024], P(None, 'tile', 'ifg')
- misfit_rms: float32 [8, 1024], P('tile', 'ifg')
The draws below stay inside these ranges and needn't reach their ends.
Inputs may be any that keep to these rules, and one draw needn't show every extreme that they name: pairs[k, 0] < pairs[k, 1] <= pairs[k, 0] + 6.
All inputs are finite; a program needn't handle non-finite values.
Results may differ from the reference program's by a relative error of at most 0.0029.
Values may be sent and summed in bfloat16 or wider, within the bound.
No kernel may reach another device: no remote copies, remote signals or barrier semaphores. Data moves between devices by JAX's collectives and lax.ppermute only.
A program may use at most 64 MiB of HBM per device.

```python
import math
import jax
import jax.numpy as jnp
from jax import lax

DATES = 300
PAIRS = 1152
EPOCHS = 8
TERMS = 16
REF = 64
COL_DEV = 128
ROWS = 8
COLS = 1024
N_IFG = 8


def draw_pairs(key, part):
    first_key = jax.random.fold_in(key, 11)
    gap_key = jax.random.fold_in(key, 23)
    first = jax.random.randint(first_key, (PAIRS,), 0, DATES - 1, dtype=jnp.int32)
    gap = jax.random.randint(gap_key, (PAIRS,), 1, 7, dtype=jnp.int32)
    second = jnp.minimum(first + gap, DATES - 1)
    return jnp.stack([first, second], axis=1)


def with_ends(drawn, stream_key, low, largest):
    place = [jax.random.randint(jax.random.fold_in(stream_key, axis), (), 0, length) for axis, length in enumerate(drawn.shape)]
    main_axis = drawn.shape.index(max(drawn.shape))
    neighbour = place[:main_axis] + [(place[main_axis] + 1) % drawn.shape[main_axis]] + place[main_axis + 1:]
    return drawn.at[tuple(place)].set(low).at[tuple(neighbour)].set(largest)


def level_of(own_key, dims, cuts, smallest, high):
    factor_of, own = 1.0, jax.random.fold_in(own_key, 6)
    for position, parts in cuts:
        heights = jnp.exp(jax.random.uniform(jax.random.fold_in(own, position), (parts,), jnp.float32, smallest / len(cuts), high / len(cuts)))
        factor_of = factor_of * jnp.repeat(heights, dims[position] // parts).reshape([-1 if axis == position else 1 for axis in range(len(dims))])
    return factor_of


def bell_draw(stream_key, dims, scale, bound, split=(), held_as=jnp.bfloat16):
    array = jax.random.normal(stream_key, dims, jnp.float32) * scale
    if len(split) > 0:
        array = level_of(stream_key, dims, split, -0.22, 0.18) * array
    return jnp.clip(array, min=-bound, max=bound).astype(held_as)


def setup_inputs(seed: int = 0) -> dict:
    seeds = jax.random.split(jax.random.key(seed), 6)
    ifgs = bell_draw(seeds[0], (PAIRS, ROWS, COLS), 2.0, 12.0, ((0, 8), (1, 4)))
    pairs = draw_pairs(jax.random.fold_in(seeds[5], 71), 0)
    pseudo_inverse = bell_draw(seeds[2], (DATES, PAIRS), PAIRS ** -0.5, 0.1875, ((1, 8),))
    ref_pixels = with_ends(jax.random.randint(seeds[3], (REF,), 0, ROWS * COLS), jax.random.fold_in(seeds[3], 1), 0, (ROWS * COLS) - 1).astype(jnp.int32)
    epochs = with_ends(jax.random.randint(seeds[4], (EPOCHS,), 8, DATES - 8), jax.random.fold_in(seeds[4], 1), 8, (DATES - 8) - 1).astype(jnp.int32)
    return dict(ifgs=ifgs, pairs=pairs, pseudo_inverse=pseudo_inverse, ref_pixels=ref_pixels, epochs=epochs)


EPS = 1e-06
RIDGE = 1.0

def design(epochs, count):
    index = jnp.arange(count, dtype=jnp.int32)
    days = index.astype(jnp.float32)
    scaled = 2.0 * days / (count - 1) - 1.0
    years = days * 12.0 / 365.25
    smooth = jnp.stack([jnp.ones_like(days), scaled, scaled * scaled, scaled * scaled * scaled, jnp.sin(2.0 * math.pi * years), jnp.cos(2.0 * math.pi * years), jnp.sin(4.0 * math.pi * years), jnp.cos(4.0 * math.pi * years)], axis=1)
    jumps = (index[:, None] >= epochs[None, :]).astype(jnp.float32)
    return jnp.concatenate([smooth, jumps], axis=1)

def fit_operator(epochs, count):
    matrix = design(epochs, count)
    normal = jnp.dot(matrix.T.astype(jnp.float32), matrix.astype(jnp.float32), precision=lax.Precision.HIGHEST, preferred_element_type=jnp.float32)
    normal = normal + RIDGE * jnp.eye(matrix.shape[1], dtype=jnp.float32)
    return jnp.linalg.solve(normal, matrix.T)

def incidence_matrix(pairs, count):
    dates = jnp.arange(count, dtype=jnp.int32)
    later = (pairs[:, 1:2] == dates[None, :]).astype(jnp.float32)
    earlier = (pairs[:, 0:1] == dates[None, :]).astype(jnp.float32)
    return later - earlier

def reference(ifgs, pairs, pseudo_inverse, ref_pixels, epochs):
    flat_view = ifgs.reshape(PAIRS, ROWS * COLS)
    region = jnp.take(flat_view, ref_pixels, axis=1).astype(jnp.float32)
    means = lax.optimization_barrier(jnp.sum(region, axis=1)) / REF
    operator = fit_operator(epochs, DATES)
    incidence = incidence_matrix(pairs, DATES)

    def block(index):
        piece = lax.dynamic_slice_in_dim(ifgs, index * COL_DEV, COL_DEV, 2)
        corrected = (piece.astype(jnp.float32) - means[:, None, None]).astype(jnp.bfloat16).reshape(PAIRS, ROWS * COL_DEV)
        displacement = jnp.dot(pseudo_inverse.astype(jnp.float32), corrected.astype(jnp.float32), preferred_element_type=jnp.float32)
        coeffs = jnp.dot(operator.astype(jnp.float32), displacement.astype(jnp.float32), precision=lax.Precision.HIGHEST, preferred_element_type=jnp.float32)
        predicted = jnp.dot(incidence.astype(jnp.float32), displacement.astype(jnp.float32), precision=lax.Precision.HIGHEST, preferred_element_type=jnp.float32)
        misfit = corrected.astype(jnp.float32) - predicted
        spread = jnp.sqrt(lax.optimization_barrier(jnp.mean(misfit * misfit, axis=0)) + EPS)
        return (coeffs.reshape(TERMS, ROWS, COL_DEV), spread.reshape(ROWS, COL_DEV))
    coeff_blocks, spread_blocks = lax.map(block, jnp.arange(N_IFG, dtype=jnp.int32))
    coefficients = jnp.transpose(coeff_blocks, (1, 2, 0, 3)).reshape(TERMS, ROWS, COLS)
    misfit_rms = jnp.transpose(spread_blocks, (1, 0, 2)).reshape(ROWS, COLS)
    return (coefficients, misfit_rms)
```

```python
import functools
import math

import jax
import jax.numpy as jnp
from jax import lax
from jax.experimental import pallas as pl
from jax.experimental.pallas import tpu as pltpu
from jax.sharding import PartitionSpec as P

EPS = 1e-06
RIDGE = 1.0
VMEM = pl.BlockSpec(memory_space=pltpu.VMEM)
SMEM = pl.BlockSpec(memory_space=pltpu.SMEM)


def design(epochs, count):
    index = jnp.arange(count, dtype=jnp.int32)
    days = index.astype(jnp.float32)
    scaled = 2.0 * days / (count - 1) - 1.0
    years = days * 12.0 / 365.25
    smooth = jnp.stack(
        [
            jnp.ones_like(days),
            scaled,
            scaled * scaled,
            scaled * scaled * scaled,
            jnp.sin(2.0 * math.pi * years),
            jnp.cos(2.0 * math.pi * years),
            jnp.sin(4.0 * math.pi * years),
            jnp.cos(4.0 * math.pi * years),
        ],
        axis=1,
    )
    jumps = (index[:, None] >= epochs[None, :]).astype(jnp.float32)
    return jnp.concatenate([smooth, jumps], axis=1)


def fit_operator(epochs, count):
    matrix = design(epochs, count)
    normal = jnp.dot(
        matrix.T, matrix, precision=lax.Precision.HIGHEST, preferred_element_type=jnp.float32
    )
    normal = normal + RIDGE * jnp.eye(matrix.shape[1], dtype=jnp.float32)
    factor = jnp.linalg.cholesky(normal)
    return jax.scipy.linalg.cho_solve((factor, True), matrix.T)


def incidence_matrix(pairs, count):
    dates = jnp.arange(count, dtype=jnp.int32)
    later = (pairs[:, 1:2] == dates[None, :]).astype(jnp.bfloat16)
    earlier = (pairs[:, 0:1] == dates[None, :]).astype(jnp.bfloat16)
    return later - earlier


def sums_kernel(row_count, ref_ref, send_ref, out_ref, acc_ref):
    blocks, rows, width = send_ref.shape
    ifg_count = rows // row_count
    cols = blocks * width
    first = lax.axis_index("tile") * row_count
    row = lax.broadcasted_iota(jnp.int32, (8, cols), 0) % row_count + first
    flat = row * cols + lax.broadcasted_iota(jnp.int32, (8, cols), 1)

    def count(i, weight):
        return weight + jnp.where(flat == ref_ref[i], 1.0, 0.0)

    weight = lax.fori_loop(
        0, ref_ref.shape[0], count, jnp.zeros((8, cols), jnp.float32), unroll=8
    )
    acc = jnp.zeros((rows // 8, 8, width), jnp.float32)
    for j in range(blocks):
        values = send_ref[j].astype(jnp.float32).reshape(rows // 8, 8, width)
        acc = acc + values * weight[None, :, j * width : (j + 1) * width]
    acc_ref[...] = acc.reshape(rows, width)
    per_ifg = acc_ref[pl.ds(0, ifg_count, stride=row_count), :]
    for r in range(1, row_count):
        per_ifg = per_ifg + acc_ref[pl.ds(r, ifg_count, stride=row_count), :]
    out_ref[...] = lax.dot_general(
        jnp.ones((8, width), jnp.float32),
        per_ifg,
        (((1,), (1,)), ((), ())),
        precision=lax.Precision.HIGHEST,
        preferred_element_type=jnp.float32,
    )


def partial_sums(ifgs, send, ref_pixels):
    ifg_count, row_count, cols = ifgs.shape
    if send.shape[1] % 16:
        tile = lax.axis_index("tile")
        pixel = jnp.arange(row_count * cols, dtype=jnp.int32) + tile * row_count * cols
        weight = jnp.sum((ref_pixels[:, None] == pixel[None, :]).astype(jnp.float32), axis=0)
        weight = weight.reshape(1, row_count, cols)
        return jnp.sum(ifgs.astype(jnp.float32) * weight, axis=(1, 2))
    sums = pl.pallas_call(
        functools.partial(sums_kernel, row_count),
        out_shape=jax.ShapeDtypeStruct((8, ifg_count), jnp.float32),
        in_specs=[SMEM, VMEM],
        out_specs=VMEM,
        scratch_shapes=[pltpu.VMEM(send.shape[1:], jnp.float32)],
        name="region_sums",
    )(ref_pixels, send)
    return sums[0]


def post_kernel(row_count, recv_ref, mean_ref, inverse_ref, incidence_ref, fit_ref,
                coeff_ref, spread_ref, wide_ref, corr_ref):
    pairs, dates = incidence_ref.shape
    width = recv_ref.shape[1]
    step = 128 if pairs % 128 == 0 else pairs
    for k in range(0, pairs, step):
        wide_ref[...] = recv_ref[row_count * k : row_count * (k + step), :].astype(jnp.float32)
        mean = mean_ref[k : k + step, :]
        for r in range(row_count):
            values = wide_ref[pl.ds(r, step, stride=row_count), :]
            corr_ref[k : k + step, r * width : (r + 1) * width] = (values - mean).astype(
                jnp.bfloat16
            )
    displacement = jnp.dot(
        inverse_ref[...], corr_ref[...], preferred_element_type=jnp.float32
    )
    coeffs = jnp.dot(
        fit_ref[...],
        displacement,
        precision=lax.Precision.HIGHEST,
        preferred_element_type=jnp.float32,
    )
    high = displacement.astype(jnp.bfloat16)
    low = (displacement - high.astype(jnp.float32)).astype(jnp.bfloat16)
    total = jnp.zeros((8, row_count * width), jnp.float32)
    for k in range(0, pairs, step):
        incidence = incidence_ref[k : k + step, :]
        predicted = jnp.dot(incidence, high, preferred_element_type=jnp.float32) + jnp.dot(
            incidence, low, preferred_element_type=jnp.float32
        )
        misfit = corr_ref[k : k + step, :].astype(jnp.float32) - predicted
        total = total + jnp.sum((misfit * misfit).reshape(step // 8, 8, -1), axis=0)
    spread = jnp.sqrt(jnp.sum(total, axis=0, keepdims=True) / pairs + EPS)
    for r in range(row_count):
        coeff_ref[:, r, :] = coeffs[:, r * width : (r + 1) * width]
        spread_ref[r : r + 1, :] = spread[:, r * width : (r + 1) * width]


def swap(array, bit):
    size = lax.axis_size("tile")
    return lax.ppermute(array, "tile", [(i, i ^ bit) for i in range(size)])


def tile_gather(array):
    size = lax.axis_size("tile")
    tile = lax.axis_index("tile")
    parts = [array]
    bit = size // 2
    order = []
    while bit:
        parts = parts + [swap(part, bit) for part in parts]
        order.append(bit)
        bit //= 2
    stacked = jnp.stack(parts)
    offset = [0] * size
    for position in range(size):
        mask = 0
        for place, bit in enumerate(order):
            if position >> place & 1:
                mask |= bit
        offset[mask] = position
    stacked = jnp.stack([parts[offset[m]] for m in range(size)])
    for bit in order:
        swapped = stacked.reshape((size // (2 * bit), 2, bit) + array.shape)
        swapped = jnp.flip(swapped, axis=1).reshape(stacked.shape)
        stacked = jnp.where((tile & bit) != 0, swapped, stacked)
    return stacked


def split_sum(value):
    high = lax.reduce_precision(value, 8, 7)
    middle = lax.reduce_precision(value - high, 8, 7)
    low = lax.reduce_precision(value - high - middle, 8, 7)
    return jnp.stack([high, middle, low]).astype(jnp.bfloat16)


def shards(ifgs, pairs, pseudo_inverse, ref_pixels, epochs):
    ifg_count, row_count, cols = ifgs.shape
    blocks = lax.axis_size("ifg")
    tiles = lax.axis_size("tile")
    width = cols // blocks
    date_count = pseudo_inverse.shape[0]
    pair_count = blocks * ifg_count
    dates = -(-date_count // 16) * 16
    tile = lax.axis_index("tile")

    send = ifgs.reshape(ifg_count, row_count, blocks, width).transpose(2, 0, 1, 3)
    send = send.reshape(blocks, ifg_count * row_count, width)

    share = -(-ifg_count // tiles)
    columns = jnp.pad(pseudo_inverse.T, ((0, share * tiles - ifg_count), (0, 0)))
    columns = lax.dynamic_slice_in_dim(columns, tile * share, share, 0)
    lanes = max(date_count, ifg_count)
    sums = split_sum(partial_sums(ifgs, send, ref_pixels))
    payload = jnp.concatenate(
        [
            jnp.pad(columns, ((0, 0), (0, lanes - date_count))),
            jnp.pad(sums, ((0, 0), (0, lanes - ifg_count))),
        ]
    )
    payload = jnp.broadcast_to(payload[None], (blocks,) + payload.shape)
    payload = lax.all_to_all(payload, "ifg", 0, 0, tiled=True)
    recv = lax.all_to_all(send, "ifg", 0, 0, tiled=True)
    gathered = tile_gather(payload)

    inverse = gathered[:, :, :share, :date_count].transpose(3, 1, 0, 2)
    inverse = inverse.reshape(date_count, blocks, tiles * share)[:, :, :ifg_count]
    inverse = jnp.pad(
        inverse.reshape(date_count, pair_count), ((0, dates - date_count), (0, 0))
    )
    totals = jnp.sum(gathered[:, :, share:, :ifg_count].astype(jnp.float32), axis=(0, 2))
    means = (totals / ref_pixels.shape[0]).reshape(pair_count, 1)
    means = jnp.broadcast_to(means, (pair_count, width))
    incidence = incidence_matrix(pairs, dates)
    fit = jnp.pad(fit_operator(epochs, date_count), ((0, 0), (0, dates - date_count)))

    terms = fit.shape[0]
    return pl.pallas_call(
        functools.partial(post_kernel, row_count),
        out_shape=(
            jax.ShapeDtypeStruct((terms, row_count, width), jnp.float32),
            jax.ShapeDtypeStruct((row_count, width), jnp.float32),
        ),
        in_specs=[VMEM] * 5,
        out_specs=(VMEM, VMEM),
        scratch_shapes=[
            pltpu.VMEM(
                (row_count * (128 if pair_count % 128 == 0 else pair_count), width), jnp.float32
            ),
            pltpu.VMEM((pair_count, row_count * width), jnp.bfloat16),
        ],
        compiler_params=pltpu.CompilerParams(vmem_limit_bytes=32 * 1024 * 1024),
        name="invert",
    )(recv.reshape(pair_count * row_count, width), means, inverse, incidence, fit)


def solution(mesh):
    in_specs = (P("ifg", "tile", None), P(), P(None, "ifg"), P(), P())
    out_specs = (P(None, "tile", "ifg"), P("tile", "ifg"))
    return jax.shard_map(shards, mesh=mesh, in_specs=in_specs, out_specs=out_specs, check_vma=False)
```

```python
import functools
import math

import jax
import jax.numpy as jnp
from jax import lax
from jax.experimental import pallas as pl
from jax.experimental.pallas import tpu as pltpu
from jax.sharding import PartitionSpec as P

EPS = 1e-06
RIDGE = 1.0
VMEM = pl.BlockSpec(memory_space=pltpu.VMEM)
SMEM = pl.BlockSpec(memory_space=pltpu.SMEM)


def design(epochs, count):
    index = jnp.arange(count, dtype=jnp.int32)
    days = index.astype(jnp.float32)
    scaled = 2.0 * days / (count - 1) - 1.0
    years = days * 12.0 / 365.25
    smooth = jnp.stack(
        [
            jnp.ones_like(days),
            scaled,
            scaled * scaled,
            scaled * scaled * scaled,
            jnp.sin(2.0 * math.pi * years),
            jnp.cos(2.0 * math.pi * years),
            jnp.sin(4.0 * math.pi * years),
            jnp.cos(4.0 * math.pi * years),
        ],
        axis=1,
    )
    jumps = (index[:, None] >= epochs[None, :]).astype(jnp.float32)
    return jnp.concatenate([smooth, jumps], axis=1)


def fit_operator(epochs, count):
    matrix = design(epochs, count)
    normal = jnp.dot(
        matrix.T, matrix, precision=lax.Precision.HIGHEST, preferred_element_type=jnp.float32
    )
    normal = normal + RIDGE * jnp.eye(matrix.shape[1], dtype=jnp.float32)
    factor = jnp.linalg.cholesky(normal)
    return jax.scipy.linalg.cho_solve((factor, True), matrix.T)


def incidence_matrix(pairs, count):
    dates = jnp.arange(count, dtype=jnp.int32)
    later = (pairs[:, 1:2] == dates[None, :]).astype(jnp.bfloat16)
    earlier = (pairs[:, 0:1] == dates[None, :]).astype(jnp.bfloat16)
    return later - earlier


def sums_kernel(row_count, ref_ref, send_ref, out_ref, acc_ref):
    blocks, rows, width = send_ref.shape
    ifg_count = rows // row_count
    cols = blocks * width
    first = lax.axis_index("tile") * row_count
    row = lax.broadcasted_iota(jnp.int32, (8, cols), 0) % row_count + first
    flat = row * cols + lax.broadcasted_iota(jnp.int32, (8, cols), 1)

    def count(i, weight):
        return weight + jnp.where(flat == ref_ref[i], 1.0, 0.0)

    weight = lax.fori_loop(
        0, ref_ref.shape[0], count, jnp.zeros((8, cols), jnp.float32), unroll=8
    )
    acc = jnp.zeros((rows // 8, 8, width), jnp.float32)
    for j in range(blocks):
        values = send_ref[j].astype(jnp.float32).reshape(rows // 8, 8, width)
        acc = acc + values * weight[None, :, j * width : (j + 1) * width]
    acc_ref[...] = acc.reshape(rows, width)
    per_ifg = acc_ref[pl.ds(0, ifg_count, stride=row_count), :]
    for r in range(1, row_count):
        per_ifg = per_ifg + acc_ref[pl.ds(r, ifg_count, stride=row_count), :]
    out_ref[...] = lax.dot_general(
        jnp.ones((8, width), jnp.float32),
        per_ifg,
        (((1,), (1,)), ((), ())),
        precision=lax.Precision.HIGHEST,
        preferred_element_type=jnp.float32,
    )


def partial_sums(ifgs, send, ref_pixels):
    ifg_count, row_count, cols = ifgs.shape
    if send.shape[1] % 16:
        tile = lax.axis_index("tile")
        pixel = jnp.arange(row_count * cols, dtype=jnp.int32) + tile * row_count * cols
        weight = jnp.sum((ref_pixels[:, None] == pixel[None, :]).astype(jnp.float32), axis=0)
        weight = weight.reshape(1, row_count, cols)
        return jnp.sum(ifgs.astype(jnp.float32) * weight, axis=(1, 2))
    sums = pl.pallas_call(
        functools.partial(sums_kernel, row_count),
        out_shape=jax.ShapeDtypeStruct((8, ifg_count), jnp.float32),
        in_specs=[SMEM, VMEM],
        out_specs=VMEM,
        scratch_shapes=[pltpu.VMEM(send.shape[1:], jnp.float32)],
        name="region_sums",
    )(ref_pixels, send)
    return sums[0]


def post_kernel(row_count, recv_ref, mean_ref, inverse_ref, incidence_ref, fit_ref,
                coeff_ref, spread_ref, wide_ref, corr_ref):
    pairs, dates = incidence_ref.shape
    width = recv_ref.shape[1]
    step = 128 if pairs % 128 == 0 else pairs
    for k in range(0, pairs, step):
        wide_ref[...] = recv_ref[row_count * k : row_count * (k + step), :].astype(jnp.float32)
        mean = mean_ref[k : k + step, :]
        for r in range(row_count):
            values = wide_ref[pl.ds(r, step, stride=row_count), :]
            corr_ref[k : k + step, r * width : (r + 1) * width] = (values - mean).astype(
                jnp.bfloat16
            )
    displacement = jnp.dot(
        inverse_ref[...], corr_ref[...], preferred_element_type=jnp.float32
    )
    finish(row_count, displacement, incidence_ref, fit_ref, coeff_ref, spread_ref, corr_ref)


ANY = pl.BlockSpec(memory_space=pl.ANY)
PAD = 16


def pack_kernel(row_count, ref_hbm, ifgs_hbm, columns_hbm, send_hbm, share_hbm,
                refs, columns, blocks, share, acc_ref, in_sems, out_sems, misc_sems):
    ifg_count, _, cols = ifgs_hbm.shape
    count, width = blocks.shape[0], blocks.shape[3]
    date_count = columns.shape[1]
    half = share.shape[0] - PAD
    ref_copy = pltpu.make_async_copy(ref_hbm, refs, misc_sems.at[0])
    ref_copy.start()
    ins = [
        pltpu.make_async_copy(
            ifgs_hbm.at[:, :, pl.ds(j * width, width)], blocks.at[j], in_sems.at[j]
        )
        for j in range(count)
    ]
    outs = [
        pltpu.make_async_copy(blocks.at[j], send_hbm.at[j], out_sems.at[j]) for j in range(count)
    ]
    for copy in ins:
        copy.start()
    columns_copy = pltpu.make_async_copy(columns_hbm, columns, misc_sems.at[1])
    columns_copy.start()
    tile = lax.axis_index("tile")
    place = lax.axis_index("ifg") // 2
    flat = lax.broadcasted_iota(jnp.int32, (8, cols), 1) + cols * (
        lax.broadcasted_iota(jnp.int32, (8, cols), 0) % row_count + tile * row_count
    )
    share[...] = jnp.zeros(share.shape, jnp.bfloat16)
    ref_copy.wait()
    weight = jnp.zeros((8, cols), jnp.float32)
    for i in range(refs.shape[0]):
        weight = weight + jnp.where(flat == refs[i], 1.0, 0.0)
    flat_blocks = blocks.reshape(count, ifg_count * row_count, width)
    acc = jnp.zeros((ifg_count * row_count // 8, 8, width), jnp.float32)
    for j in range(count):
        ins[j].wait()
        outs[j].start()
        values = flat_blocks[j].astype(jnp.float32).reshape(acc.shape)
        acc = acc + values * weight[None, :, j * width : (j + 1) * width]
    acc_ref[...] = acc.reshape(ifg_count * row_count, width)
    per_ifg = acc_ref[pl.ds(0, ifg_count, stride=row_count), :]
    for r in range(1, row_count):
        per_ifg = per_ifg + acc_ref[pl.ds(r, ifg_count, stride=row_count), :]
    columns_copy.wait()
    first = pl.multiple_of((tile % 2) * (ifg_count - half), 16)
    share[:half, :date_count] = columns[pl.ds(first, half), :]
    sums = lax.dot_general(
        jnp.ones((8, width), jnp.float32),
        per_ifg,
        (((1,), (1,)), ((), ())),
        precision=lax.Precision.HIGHEST,
        preferred_element_type=jnp.float32,
    )
    high = sums.astype(jnp.bfloat16).astype(jnp.float32)
    middle = (sums - high).astype(jnp.bfloat16).astype(jnp.float32)
    low = sums - high - middle
    row = lax.broadcasted_iota(jnp.int32, (8, ifg_count), 0)
    terms = jnp.where(row % 4 == 0, high, jnp.where(row % 4 == 1, middle, low))
    terms = jnp.concatenate([terms, terms], axis=0)
    row = lax.broadcasted_iota(jnp.int32, (PAD, ifg_count), 0)
    terms = jnp.where((row // 4 == place) & (row % 4 < 3), terms, 0.0)
    share[half:, :ifg_count] = terms.astype(jnp.bfloat16)
    share_copy = pltpu.make_async_copy(share, share_hbm, misc_sems.at[2])
    share_copy.start()
    for copy in outs:
        copy.wait()
    share_copy.wait()


def pack(ref_pixels, ifgs, columns, blocks, half, lanes):
    ifg_count, row_count, cols = ifgs.shape
    shape = (blocks, ifg_count, row_count, cols // blocks)
    share = (half + PAD, lanes)
    return pl.pallas_call(
        functools.partial(pack_kernel, row_count),
        out_shape=(
            jax.ShapeDtypeStruct(shape, jnp.bfloat16),
            jax.ShapeDtypeStruct(share, jnp.bfloat16),
        ),
        in_specs=[ANY] * 3,
        out_specs=(ANY, ANY),
        scratch_shapes=[
            pltpu.SMEM(ref_pixels.shape, jnp.int32),
            pltpu.VMEM(columns.shape, jnp.bfloat16),
            pltpu.VMEM(shape, jnp.bfloat16),
            pltpu.VMEM(share, jnp.bfloat16),
            pltpu.VMEM((ifg_count * row_count, shape[3]), jnp.float32),
            pltpu.SemaphoreType.DMA((blocks,)),
            pltpu.SemaphoreType.DMA((blocks,)),
            pltpu.SemaphoreType.DMA((3,)),
        ],
        name="pack",
    )(ref_pixels, ifgs, columns)


def invert_kernel(row_count, region_size, recv_ref, own_ref, across_ref, own_core_ref,
                  across_core_ref, sums_ref, sums_core_ref, incidence_ref, fit_ref,
                  coeff_ref, spread_ref, wide_ref, corr_ref, operator_ref):
    blocks, rows, width = recv_ref.shape
    ifg_count = rows // row_count
    planes = blocks // 2
    pairs = blocks * ifg_count
    half = own_ref.shape[1]
    ifg = lax.axis_index("ifg")
    core = lax.axis_index("tile") % 2
    place, side = ifg // 2, ifg % 2
    for away, (near, far) in enumerate(((own_ref, own_core_ref), (across_ref, across_core_ref))):
        for m in range(planes):
            first = (2 * (place ^ m) + (side ^ away)) * ifg_count
            shift = ifg_count - half
            operator_ref[pl.ds(pl.multiple_of(first + core * shift, 16), half), :] = near[m]
            operator_ref[pl.ds(pl.multiple_of(first + (1 - core) * shift, 16), half), :] = far[m]
    row = lax.broadcasted_iota(jnp.int32, (PAD, planes * width), 0)
    lane = lax.broadcasted_iota(jnp.int32, (PAD, planes * width), 1)
    select = jnp.where(row // 4 == lane // width, 1.0, 0.0).astype(jnp.bfloat16)
    for away in range(2):
        totals = 0.0
        for part in (sums_ref[0, away], sums_ref[1, away], sums_core_ref[0, away], sums_core_ref[1, away]):
            totals = totals + lax.dot_general(
                part, select, (((0,), (0,)), ((), ())), preferred_element_type=jnp.float32
            )
        means = totals[:ifg_count] / region_size
        for plane in range(planes):
            block = 2 * plane + (side ^ away)
            wide_ref[...] = recv_ref[block].astype(jnp.float32)
            mean = means[:, plane * width : (plane + 1) * width]
            first = pl.multiple_of(block * ifg_count, 16)
            for r in range(row_count):
                values = wide_ref[pl.ds(r, ifg_count, stride=row_count), :]
                corr_ref[pl.ds(first, ifg_count), r * width : (r + 1) * width] = (
                    values - mean
                ).astype(jnp.bfloat16)
    displacement = lax.dot_general(
        operator_ref[...],
        corr_ref[...],
        (((0,), (0,)), ((), ())),
        preferred_element_type=jnp.float32,
    )
    finish(row_count, displacement, incidence_ref, fit_ref, coeff_ref, spread_ref, corr_ref)


def finish(row_count, displacement, incidence_ref, fit_ref, coeff_ref, spread_ref, corr_ref):
    pairs = incidence_ref.shape[0]
    width = corr_ref.shape[1] // row_count
    step = 128 if pairs % 128 == 0 else pairs
    coeffs = jnp.dot(
        fit_ref[...],
        displacement,
        precision=lax.Precision.HIGHEST,
        preferred_element_type=jnp.float32,
    )
    high = displacement.astype(jnp.bfloat16)
    low = (displacement - high.astype(jnp.float32)).astype(jnp.bfloat16)
    total = jnp.zeros((8, row_count * width), jnp.float32)
    for k in range(0, pairs, step):
        incidence = incidence_ref[k : k + step, :]
        predicted = jnp.dot(incidence, high, preferred_element_type=jnp.float32) + jnp.dot(
            incidence, low, preferred_element_type=jnp.float32
        )
        misfit = corr_ref[k : k + step, :].astype(jnp.float32) - predicted
        total = total + jnp.sum((misfit * misfit).reshape(step // 8, 8, -1), axis=0)
    spread = jnp.sqrt(jnp.sum(total, axis=0, keepdims=True) / pairs + EPS)
    for r in range(row_count):
        coeff_ref[:, r, :] = coeffs[:, r * width : (r + 1) * width]
        spread_ref[r : r + 1, :] = spread[:, r * width : (r + 1) * width]


def trade(array, bit):
    size = lax.axis_size("ifg")
    return lax.ppermute(array, "ifg", [(i, i ^ bit) for i in range(size)])


def small_slice(ifgs, pairs, pseudo_inverse, ref_pixels, epochs):
    ifg_count, row_count, cols = ifgs.shape
    blocks = lax.axis_size("ifg")
    width = cols // blocks
    date_count = pseudo_inverse.shape[0]
    pair_count = blocks * ifg_count
    lanes = -(-max(date_count, ifg_count) // 128) * 128
    half = -(-ifg_count // 32) * 16

    send, share = pack(ref_pixels, ifgs, pseudo_inverse.T, blocks, half, lanes)
    shares = [share] + [trade(share, 2 * m) for m in range(1, blocks // 2)]
    recv = lax.all_to_all(
        send.reshape(blocks, ifg_count * row_count, width), "ifg", 0, 0, tiled=True
    )
    sum_lanes = -(-ifg_count // 128) * 128
    sums = sum(part[half:, :sum_lanes] for part in shares)
    sums = jnp.stack([sums, trade(sums, 1)])
    sums = jnp.stack([sums, swap(sums, 2)])
    sums_core = swap(sums, 1)
    own = jnp.stack([part[:half] for part in shares])
    across = trade(own, 1)
    own_core = swap(own, 1)
    across_core = swap(across, 1)

    incidence = incidence_matrix(pairs, lanes)
    fit = jnp.pad(fit_operator(epochs, date_count), ((0, 0), (0, lanes - date_count)))
    terms = fit.shape[0]
    return pl.pallas_call(
        functools.partial(invert_kernel, row_count, ref_pixels.shape[0]),
        out_shape=(
            jax.ShapeDtypeStruct((terms, row_count, width), jnp.float32),
            jax.ShapeDtypeStruct((row_count, width), jnp.float32),
        ),
        in_specs=[VMEM] * 9,
        out_specs=(VMEM, VMEM),
        scratch_shapes=[
            pltpu.VMEM((row_count * ifg_count, width), jnp.float32),
            pltpu.VMEM((pair_count, row_count * width), jnp.bfloat16),
            pltpu.VMEM((pair_count, lanes), jnp.bfloat16),
        ],
        compiler_params=pltpu.CompilerParams(vmem_limit_bytes=32 * 1024 * 1024),
        name="invert",
    )(recv, own, across, own_core, across_core, sums, sums_core, incidence, fit)


def swap(array, bit):
    size = lax.axis_size("tile")
    return lax.ppermute(array, "tile", [(i, i ^ bit) for i in range(size)])


def tile_gather(array):
    size = lax.axis_size("tile")
    tile = lax.axis_index("tile")
    parts = [array]
    bit = size // 2
    order = []
    while bit:
        parts = parts + [swap(part, bit) for part in parts]
        order.append(bit)
        bit //= 2
    stacked = jnp.stack(parts)
    offset = [0] * size
    for position in range(size):
        mask = 0
        for place, bit in enumerate(order):
            if position >> place & 1:
                mask |= bit
        offset[mask] = position
    stacked = jnp.stack([parts[offset[m]] for m in range(size)])
    for bit in order:
        swapped = stacked.reshape((size // (2 * bit), 2, bit) + array.shape)
        swapped = jnp.flip(swapped, axis=1).reshape(stacked.shape)
        stacked = jnp.where((tile & bit) != 0, swapped, stacked)
    return stacked


def split_sum(value):
    high = lax.reduce_precision(value, 8, 7)
    middle = lax.reduce_precision(value - high, 8, 7)
    low = lax.reduce_precision(value - high - middle, 8, 7)
    return jnp.stack([high, middle, low]).astype(jnp.bfloat16)


def shards(ifgs, pairs, pseudo_inverse, ref_pixels, epochs):
    ifg_count, row_count, cols = ifgs.shape
    blocks = lax.axis_size("ifg")
    tiles = lax.axis_size("tile")
    if blocks == 8 and tiles == 4 and ifg_count % 16 == 0:
        return small_slice(ifgs, pairs, pseudo_inverse, ref_pixels, epochs)
    width = cols // blocks
    date_count = pseudo_inverse.shape[0]
    pair_count = blocks * ifg_count
    dates = -(-date_count // 16) * 16
    tile = lax.axis_index("tile")

    send = ifgs.reshape(ifg_count, row_count, blocks, width).transpose(2, 0, 1, 3)
    send = send.reshape(blocks, ifg_count * row_count, width)

    share = -(-ifg_count // tiles)
    columns = jnp.pad(pseudo_inverse.T, ((0, share * tiles - ifg_count), (0, 0)))
    columns = lax.dynamic_slice_in_dim(columns, tile * share, share, 0)
    lanes = max(date_count, ifg_count)
    sums = split_sum(partial_sums(ifgs, send, ref_pixels))
    payload = jnp.concatenate(
        [
            jnp.pad(columns, ((0, 0), (0, lanes - date_count))),
            jnp.pad(sums, ((0, 0), (0, lanes - ifg_count))),
        ]
    )
    payload = jnp.broadcast_to(payload[None], (blocks,) + payload.shape)
    payload = lax.all_to_all(payload, "ifg", 0, 0, tiled=True)
    recv = lax.all_to_all(send, "ifg", 0, 0, tiled=True)
    gathered = tile_gather(payload)

    inverse = gathered[:, :, :share, :date_count].transpose(3, 1, 0, 2)
    inverse = inverse.reshape(date_count, blocks, tiles * share)[:, :, :ifg_count]
    inverse = jnp.pad(
        inverse.reshape(date_count, pair_count), ((0, dates - date_count), (0, 0))
    )
    totals = jnp.sum(gathered[:, :, share:, :ifg_count].astype(jnp.float32), axis=(0, 2))
    means = (totals / ref_pixels.shape[0]).reshape(pair_count, 1)
    means = jnp.broadcast_to(means, (pair_count, width))
    incidence = incidence_matrix(pairs, dates)
    fit = jnp.pad(fit_operator(epochs, date_count), ((0, 0), (0, dates - date_count)))

    terms = fit.shape[0]
    return pl.pallas_call(
        functools.partial(post_kernel, row_count),
        out_shape=(
            jax.ShapeDtypeStruct((terms, row_count, width), jnp.float32),
            jax.ShapeDtypeStruct((row_count, width), jnp.float32),
        ),
        in_specs=[VMEM] * 5,
        out_specs=(VMEM, VMEM),
        scratch_shapes=[
            pltpu.VMEM(
                (row_count * (128 if pair_count % 128 == 0 else pair_count), width), jnp.float32
            ),
            pltpu.VMEM((pair_count, row_count * width), jnp.bfloat16),
        ],
        compiler_params=pltpu.CompilerParams(vmem_limit_bytes=32 * 1024 * 1024),
        name="invert",
    )(recv.reshape(pair_count * row_count, width), means, inverse, incidence, fit)


def solution(mesh):
    in_specs = (P("ifg", "tile", None), P(), P(None, "ifg"), P(), P())
    out_specs = (P(None, "tile", "ifg"), P("tile", "ifg"))
    return jax.shard_map(shards, mesh=mesh, in_specs=in_specs, out_specs=out_specs, check_vma=False)
```

```python
import functools
import math

import jax
import jax.numpy as jnp
from jax import lax
from jax.experimental import pallas as pl
from jax.experimental.pallas import tpu as pltpu
from jax.sharding import PartitionSpec as P

EPS = 1e-06
RIDGE = 1.0
VMEM = pl.BlockSpec(memory_space=pltpu.VMEM)
SMEM = pl.BlockSpec(memory_space=pltpu.SMEM)


def design(epochs, count):
    index = jnp.arange(count, dtype=jnp.int32)
    days = index.astype(jnp.float32)
    scaled = 2.0 * days / (count - 1) - 1.0
    years = days * 12.0 / 365.25
    smooth = jnp.stack(
        [
            jnp.ones_like(days),
            scaled,
            scaled * scaled,
            scaled * scaled * scaled,
            jnp.sin(2.0 * math.pi * years),
            jnp.cos(2.0 * math.pi * years),
            jnp.sin(4.0 * math.pi * years),
            jnp.cos(4.0 * math.pi * years),
        ],
        axis=1,
    )
    jumps = (index[:, None] >= epochs[None, :]).astype(jnp.float32)
    return jnp.concatenate([smooth, jumps], axis=1)


def fit_operator(epochs, count):
    matrix = design(epochs, count)
    normal = jnp.dot(
        matrix.T, matrix, precision=lax.Precision.HIGHEST, preferred_element_type=jnp.float32
    )
    normal = normal + RIDGE * jnp.eye(matrix.shape[1], dtype=jnp.float32)
    factor = jnp.linalg.cholesky(normal)
    return jax.scipy.linalg.cho_solve((factor, True), matrix.T)


def incidence_matrix(pairs, count):
    dates = jnp.arange(count, dtype=jnp.int32)
    later = (pairs[:, 1:2] == dates[None, :]).astype(jnp.bfloat16)
    earlier = (pairs[:, 0:1] == dates[None, :]).astype(jnp.bfloat16)
    return later - earlier


def sums_kernel(row_count, ref_ref, send_ref, out_ref, acc_ref):
    blocks, rows, width = send_ref.shape
    ifg_count = rows // row_count
    cols = blocks * width
    first = lax.axis_index("tile") * row_count
    row = lax.broadcasted_iota(jnp.int32, (8, cols), 0) % row_count + first
    flat = row * cols + lax.broadcasted_iota(jnp.int32, (8, cols), 1)

    def count(i, weight):
        return weight + jnp.where(flat == ref_ref[i], 1.0, 0.0)

    weight = lax.fori_loop(
        0, ref_ref.shape[0], count, jnp.zeros((8, cols), jnp.float32), unroll=8
    )
    acc = jnp.zeros((rows // 8, 8, width), jnp.float32)
    for j in range(blocks):
        values = send_ref[j].astype(jnp.float32).reshape(rows // 8, 8, width)
        acc = acc + values * weight[None, :, j * width : (j + 1) * width]
    acc_ref[...] = acc.reshape(rows, width)
    per_ifg = acc_ref[pl.ds(0, ifg_count, stride=row_count), :]
    for r in range(1, row_count):
        per_ifg = per_ifg + acc_ref[pl.ds(r, ifg_count, stride=row_count), :]
    out_ref[...] = lax.dot_general(
        jnp.ones((8, width), jnp.float32),
        per_ifg,
        (((1,), (1,)), ((), ())),
        precision=lax.Precision.HIGHEST,
        preferred_element_type=jnp.float32,
    )


def partial_sums(ifgs, send, ref_pixels):
    ifg_count, row_count, cols = ifgs.shape
    if send.shape[1] % 16:
        tile = lax.axis_index("tile")
        pixel = jnp.arange(row_count * cols, dtype=jnp.int32) + tile * row_count * cols
        weight = jnp.sum((ref_pixels[:, None] == pixel[None, :]).astype(jnp.float32), axis=0)
        weight = weight.reshape(1, row_count, cols)
        return jnp.sum(ifgs.astype(jnp.float32) * weight, axis=(1, 2))
    sums = pl.pallas_call(
        functools.partial(sums_kernel, row_count),
        out_shape=jax.ShapeDtypeStruct((8, ifg_count), jnp.float32),
        in_specs=[SMEM, VMEM],
        out_specs=VMEM,
        scratch_shapes=[pltpu.VMEM(send.shape[1:], jnp.float32)],
        name="region_sums",
    )(ref_pixels, send)
    return sums[0]


def post_kernel(row_count, recv_ref, mean_ref, inverse_ref, incidence_ref, fit_ref,
                coeff_ref, spread_ref, wide_ref, corr_ref):
    pairs, dates = incidence_ref.shape
    width = recv_ref.shape[1]
    step = 128 if pairs % 128 == 0 else pairs
    for k in range(0, pairs, step):
        wide_ref[...] = recv_ref[row_count * k : row_count * (k + step), :].astype(jnp.float32)
        mean = mean_ref[k : k + step, :]
        for r in range(row_count):
            values = wide_ref[pl.ds(r, step, stride=row_count), :]
            corr_ref[k : k + step, r * width : (r + 1) * width] = (values - mean).astype(
                jnp.bfloat16
            )
    displacement = jnp.dot(
        inverse_ref[...], corr_ref[...], preferred_element_type=jnp.float32
    )
    spans = [(slice(k, k + step), slice(k, k + step)) for k in range(0, pairs, step)]
    finish(row_count, displacement, spans, incidence_ref, fit_ref, coeff_ref, spread_ref, corr_ref)


ANY = pl.BlockSpec(memory_space=pl.ANY)
PAD = 16
PLANES = 4
SMALL = pltpu.CompilerParams(vmem_limit_bytes=16 * 1024 * 1024)


def pack_kernel(row_count, ref_hbm, ifgs_hbm, blocks, share, refs, acc_ref, in_sems, ref_sem):
    ifg_count, _, cols = ifgs_hbm.shape
    count, width = blocks.shape[0], blocks.shape[3]
    ref_copy = pltpu.make_async_copy(ref_hbm, refs, ref_sem)
    ref_copy.start()
    ins = [
        pltpu.make_async_copy(
            ifgs_hbm.at[:, :, pl.ds(j * width, width)], blocks.at[j], in_sems.at[j]
        )
        for j in range(count)
    ]
    for copy in ins:
        copy.start()
    tile = lax.axis_index("tile")
    place = lax.axis_index("ifg") // 2
    flat = lax.broadcasted_iota(jnp.int32, (8, cols), 1) + cols * (
        lax.broadcasted_iota(jnp.int32, (8, cols), 0) % row_count + tile * row_count
    )
    share[...] = jnp.zeros(share.shape, jnp.bfloat16)
    ref_copy.wait()
    weight = jnp.zeros((8, cols), jnp.float32)
    for i in range(refs.shape[0]):
        weight = weight + jnp.where(flat == refs[i], 1.0, 0.0)
    flat_blocks = blocks.reshape(count, ifg_count * row_count, width)
    acc = jnp.zeros((ifg_count * row_count // 8, 8, width), jnp.float32)
    for j in range(count):
        ins[j].wait()
        values = flat_blocks[j].astype(jnp.float32).reshape(acc.shape)
        acc = acc + values * weight[None, :, j * width : (j + 1) * width]
    acc_ref[...] = acc.reshape(ifg_count * row_count, width)
    per_ifg = acc_ref[pl.ds(0, ifg_count, stride=row_count), :]
    for r in range(1, row_count):
        per_ifg = per_ifg + acc_ref[pl.ds(r, ifg_count, stride=row_count), :]
    sums = lax.dot_general(
        jnp.ones((8, width), jnp.float32),
        per_ifg,
        (((1,), (1,)), ((), ())),
        precision=lax.Precision.HIGHEST,
        preferred_element_type=jnp.float32,
    )
    high = sums.astype(jnp.bfloat16).astype(jnp.float32)
    middle = (sums - high).astype(jnp.bfloat16).astype(jnp.float32)
    low = sums - high - middle
    row = lax.broadcasted_iota(jnp.int32, (8, ifg_count), 0)
    terms = jnp.where(row % 4 == 0, high, jnp.where(row % 4 == 1, middle, low))
    terms = jnp.concatenate([terms, terms], axis=0)
    row = lax.broadcasted_iota(jnp.int32, (PAD, ifg_count), 0)
    terms = jnp.where((row // 4 == place) & (row % 4 < 3), terms, 0.0)
    share[:, :ifg_count] = terms.astype(jnp.bfloat16)


def pack(ref_pixels, ifgs, blocks, lanes):
    ifg_count, row_count, cols = ifgs.shape
    shape = (blocks, ifg_count, row_count, cols // blocks)
    return pl.pallas_call(
        functools.partial(pack_kernel, row_count),
        out_shape=(pltpu.VMEM(shape, jnp.bfloat16), pltpu.VMEM((PAD, lanes), jnp.bfloat16)),
        in_specs=[ANY] * 2,
        out_specs=(VMEM, VMEM),
        scratch_shapes=[
            pltpu.SMEM(ref_pixels.shape, jnp.int32),
            pltpu.VMEM((ifg_count * row_count, shape[3]), jnp.float32),
            pltpu.SemaphoreType.DMA((blocks,)),
            pltpu.SemaphoreType.DMA(()),
        ],
        name="pack",
    )(ref_pixels, ifgs)


def fit_kernel(date_count, epochs_ref, fit_ref):
    terms, lanes = fit_ref.shape
    index = lax.broadcasted_iota(jnp.int32, (terms, lanes), 1)
    row = lax.broadcasted_iota(jnp.int32, (terms, lanes), 0)
    days = index.astype(jnp.float32)
    scaled = 2.0 * days / (date_count - 1) - 1.0
    years = days * 12.0 / 365.25
    smooth = [
        jnp.ones_like(days),
        scaled,
        scaled * scaled,
        scaled * scaled * scaled,
        jnp.sin(2.0 * math.pi * years),
        jnp.cos(2.0 * math.pi * years),
        jnp.sin(4.0 * math.pi * years),
        jnp.cos(4.0 * math.pi * years),
    ]
    matrix = jnp.zeros((terms, lanes), jnp.float32)
    for r, values in enumerate(smooth):
        matrix = jnp.where(row == r, values, matrix)
    for e in range(epochs_ref.shape[0]):
        step = jnp.where(index >= epochs_ref[e], 1.0, 0.0)
        matrix = jnp.where(row == len(smooth) + e, step, matrix)
    matrix = jnp.where(index < date_count, matrix, 0.0)
    normal = lax.dot_general(
        matrix,
        matrix,
        (((1,), (1,)), ((), ())),
        precision=lax.Precision.HIGHEST,
        preferred_element_type=jnp.float32,
    )
    place = lax.broadcasted_iota(jnp.int32, (terms, terms), 0)
    diagonal = place == lax.broadcasted_iota(jnp.int32, (terms, terms), 1)
    normal = normal + jnp.where(diagonal, RIDGE, 0.0)
    for j in range(terms):
        scale = 1.0 / normal[j : j + 1, j : j + 1]
        pivot, right = normal[j : j + 1, :] * scale, matrix[j : j + 1, :] * scale
        factor = normal[:, j : j + 1]
        normal = jnp.where(place == j, pivot, normal - factor * pivot)
        matrix = jnp.where(row == j, right, matrix - factor * right)
    fit_ref[...] = matrix


def prepare_kernel(region_size, own_ref, up_ref, core_ref, up_core_ref, sums_ref, sums_tile_ref,
                   operator_ref, mean_ref):
    pairs, width = mean_ref.shape
    ifg_count = pairs // (2 * PLANES)
    share = own_ref.shape[0] // (2 * PLANES)
    shift = (ifg_count - share) // 3
    ifg, tile = lax.axis_index("ifg"), lax.axis_index("tile")
    for flip, part_ref in enumerate((own_ref, core_ref, up_ref, up_core_ref)):
        for m in range(PLANES):
            for away in range(2):
                first = (ifg ^ (2 * m + away)) * ifg_count + (tile ^ flip) * shift
                rows = (2 * m + away) * share
                operator_ref[pl.ds(pl.multiple_of(first, 16), share), :] = part_ref[
                    rows : rows + share, :
                ]
    row = lax.broadcasted_iota(jnp.int32, (4 * PAD, PLANES * width), 0) % PAD
    lane = lax.broadcasted_iota(jnp.int32, (4 * PAD, PLANES * width), 1)
    select = jnp.where(row // 4 == lane // width, 1.0, 0.0).astype(jnp.bfloat16)
    for away in range(2):
        terms = [sums_ref[away]] + [sums_tile_ref[other, away] for other in range(3)]
        totals = lax.dot_general(
            jnp.concatenate(terms),
            select,
            (((0,), (0,)), ((), ())),
            preferred_element_type=jnp.float32,
        )
        means = totals[:ifg_count] / region_size
        for plane in range(PLANES):
            first = (2 * plane + (ifg % 2 ^ away)) * ifg_count
            mean_ref[pl.ds(pl.multiple_of(first, 16), ifg_count), :] = means[
                :, plane * width : (plane + 1) * width
            ]


def invert_kernel(row_count, recv_ref, operator_ref, mean_ref, incidence_ref, fit_ref,
                  coeff_ref, spread_ref, wide_ref, corr_ref):
    blocks, rows, width = recv_ref.shape
    ifg_count = rows // row_count
    spans = []
    for block in range(blocks):
        span = slice(block * ifg_count, (block + 1) * ifg_count)
        spans.append((span, span))
        wide_ref[...] = recv_ref[block].astype(jnp.float32)
        mean = mean_ref[span, :]
        for r in range(row_count):
            values = wide_ref[pl.ds(r, ifg_count, stride=row_count), :]
            corr_ref[span, r * width : (r + 1) * width] = (values - mean).astype(jnp.bfloat16)
    displacement = lax.dot_general(
        operator_ref[...],
        corr_ref[...],
        (((0,), (0,)), ((), ())),
        preferred_element_type=jnp.float32,
    )
    finish(row_count, displacement, spans, incidence_ref, fit_ref, coeff_ref, spread_ref, corr_ref)


def finish(row_count, displacement, spans, incidence_ref, fit_ref, coeff_ref, spread_ref, corr_ref):
    pairs = incidence_ref.shape[0]
    width = corr_ref.shape[1] // row_count
    coeffs = jnp.dot(
        fit_ref[...],
        displacement,
        precision=lax.Precision.HIGHEST,
        preferred_element_type=jnp.float32,
    )
    high = displacement.astype(jnp.bfloat16)
    low = (displacement - high.astype(jnp.float32)).astype(jnp.bfloat16)
    total = jnp.zeros((8, row_count * width), jnp.float32)
    for span, rows in spans:
        incidence = incidence_ref[span, :]
        predicted = jnp.dot(incidence, high, preferred_element_type=jnp.float32) + jnp.dot(
            incidence, low, preferred_element_type=jnp.float32
        )
        misfit = corr_ref[rows, :].astype(jnp.float32) - predicted
        total = total + jnp.sum((misfit * misfit).reshape(-1, 8, misfit.shape[1]), axis=0)
    spread = jnp.sqrt(jnp.sum(total, axis=0, keepdims=True) / pairs + EPS)
    for r in range(row_count):
        coeff_ref[:, r, :] = coeffs[:, r * width : (r + 1) * width]
        spread_ref[r : r + 1, :] = spread[:, r * width : (r + 1) * width]


def trade(array, bit):
    size = lax.axis_size("ifg")
    return lax.ppermute(array, "ifg", [(i, i ^ bit) for i in range(size)])


def small_slice(ifgs, pairs, pseudo_inverse, ref_pixels, epochs):
    ifg_count, row_count, cols = ifgs.shape
    blocks = lax.axis_size("ifg")
    width = cols // blocks
    date_count = pseudo_inverse.shape[0]
    pair_count = blocks * ifg_count
    lanes = -(-max(date_count, ifg_count) // 128) * 128
    sum_lanes = -(-ifg_count // 128) * 128

    rows = -(-ifg_count // 64) * 16
    first = lax.axis_index("tile") * ((ifg_count - rows) // 3)
    share = lax.dynamic_slice_in_dim(pseudo_inverse.T, first, rows, 0)
    share = jnp.pad(share, ((0, 0), (0, lanes - date_count)))
    other = trade(share, 1)
    send, sums = pack(ref_pixels, ifgs, blocks, lanes)
    payload = jnp.concatenate([share, other, sums])
    send, payload = lax.optimization_barrier((send, payload))
    payloads = [payload] + [trade(payload, 2 * m) for m in range(1, PLANES)]
    recv = lax.all_to_all(
        send.reshape(blocks, ifg_count * row_count, width), "ifg", 0, 0, tiled=True
    )
    sums = sum(part[2 * rows :, :sum_lanes] for part in payloads)
    own = jnp.concatenate([part[: 2 * rows] for part in payloads])
    own, sums, pairs, epochs = lax.optimization_barrier((own, sums, pairs, epochs))
    up = swap(own, 2)
    sums = jnp.stack([sums, trade(sums, 1)])
    sums_tile = jnp.stack([swap(sums, other) for other in (1, 2, 3)])
    core = swap(own, 1)
    up_core = swap(up, 1)
    operator, means = pl.pallas_call(
        functools.partial(prepare_kernel, ref_pixels.shape[0]),
        out_shape=(
            pltpu.VMEM((pair_count, lanes), jnp.bfloat16),
            pltpu.VMEM((pair_count, width), jnp.float32),
        ),
        in_specs=[VMEM] * 6,
        out_specs=(VMEM, VMEM),
        compiler_params=SMALL,
        name="prepare",
    )(own, up, core, up_core, sums, sums_tile)
    incidence = incidence_matrix(pairs, lanes)
    terms = 8 + epochs.shape[0]
    fit = pl.pallas_call(
        functools.partial(fit_kernel, date_count),
        out_shape=pltpu.VMEM((terms, lanes), jnp.float32),
        in_specs=[SMEM],
        out_specs=VMEM,
        compiler_params=SMALL,
        name="fit",
    )(epochs)
    return pl.pallas_call(
        functools.partial(invert_kernel, row_count),
        out_shape=(
            jax.ShapeDtypeStruct((terms, row_count, width), jnp.float32),
            jax.ShapeDtypeStruct((row_count, width), jnp.float32),
        ),
        in_specs=[VMEM] * 5,
        out_specs=(VMEM, VMEM),
        scratch_shapes=[
            pltpu.VMEM((row_count * ifg_count, width), jnp.float32),
            pltpu.VMEM((pair_count, row_count * width), jnp.bfloat16),
        ],
        compiler_params=SMALL,
        name="invert",
    )(recv, operator, means, incidence, fit)


def swap(array, bit):
    size = lax.axis_size("tile")
    return lax.ppermute(array, "tile", [(i, i ^ bit) for i in range(size)])


def tile_gather(array):
    size = lax.axis_size("tile")
    tile = lax.axis_index("tile")
    parts = [array]
    bit = size // 2
    order = []
    while bit:
        parts = parts + [swap(part, bit) for part in parts]
        order.append(bit)
        bit //= 2
    stacked = jnp.stack(parts)
    offset = [0] * size
    for position in range(size):
        mask = 0
        for place, bit in enumerate(order):
            if position >> place & 1:
                mask |= bit
        offset[mask] = position
    stacked = jnp.stack([parts[offset[m]] for m in range(size)])
    for bit in order:
        swapped = stacked.reshape((size // (2 * bit), 2, bit) + array.shape)
        swapped = jnp.flip(swapped, axis=1).reshape(stacked.shape)
        stacked = jnp.where((tile & bit) != 0, swapped, stacked)
    return stacked


def split_sum(value):
    high = lax.reduce_precision(value, 8, 7)
    middle = lax.reduce_precision(value - high, 8, 7)
    low = lax.reduce_precision(value - high - middle, 8, 7)
    return jnp.stack([high, middle, low]).astype(jnp.bfloat16)


def shards(ifgs, pairs, pseudo_inverse, ref_pixels, epochs):
    ifg_count, row_count, cols = ifgs.shape
    blocks = lax.axis_size("ifg")
    tiles = lax.axis_size("tile")
    if blocks == 2 * PLANES and tiles == 4 and ifg_count % 48 == 0:
        return small_slice(ifgs, pairs, pseudo_inverse, ref_pixels, epochs)
    width = cols // blocks
    date_count = pseudo_inverse.shape[0]
    pair_count = blocks * ifg_count
    dates = -(-date_count // 16) * 16
    tile = lax.axis_index("tile")

    send = ifgs.reshape(ifg_count, row_count, blocks, width).transpose(2, 0, 1, 3)
    send = send.reshape(blocks, ifg_count * row_count, width)

    share = -(-ifg_count // tiles)
    columns = jnp.pad(pseudo_inverse.T, ((0, share * tiles - ifg_count), (0, 0)))
    columns = lax.dynamic_slice_in_dim(columns, tile * share, share, 0)
    lanes = max(date_count, ifg_count)
    sums = split_sum(partial_sums(ifgs, send, ref_pixels))
    payload = jnp.concatenate(
        [
            jnp.pad(columns, ((0, 0), (0, lanes - date_count))),
            jnp.pad(sums, ((0, 0), (0, lanes - ifg_count))),
        ]
    )
    payload = jnp.broadcast_to(payload[None], (blocks,) + payload.shape)
    payload = lax.all_to_all(payload, "ifg", 0, 0, tiled=True)
    recv = lax.all_to_all(send, "ifg", 0, 0, tiled=True)
    gathered = tile_gather(payload)

    inverse = gathered[:, :, :share, :date_count].transpose(3, 1, 0, 2)
    inverse = inverse.reshape(date_count, blocks, tiles * share)[:, :, :ifg_count]
    inverse = jnp.pad(
        inverse.reshape(date_count, pair_count), ((0, dates - date_count), (0, 0))
    )
    totals = jnp.sum(gathered[:, :, share:, :ifg_count].astype(jnp.float32), axis=(0, 2))
    means = (totals / ref_pixels.shape[0]).reshape(pair_count, 1)
    means = jnp.broadcast_to(means, (pair_count, width))
    incidence = incidence_matrix(pairs, dates)
    fit = jnp.pad(fit_operator(epochs, date_count), ((0, 0), (0, dates - date_count)))

    terms = fit.shape[0]
    return pl.pallas_call(
        functools.partial(post_kernel, row_count),
        out_shape=(
            jax.ShapeDtypeStruct((terms, row_count, width), jnp.float32),
            jax.ShapeDtypeStruct((row_count, width), jnp.float32),
        ),
        in_specs=[VMEM] * 5,
        out_specs=(VMEM, VMEM),
        scratch_shapes=[
            pltpu.VMEM(
                (row_count * (128 if pair_count % 128 == 0 else pair_count), width), jnp.float32
            ),
            pltpu.VMEM((pair_count, row_count * width), jnp.bfloat16),
        ],
        compiler_params=pltpu.CompilerParams(vmem_limit_bytes=32 * 1024 * 1024),
        name="invert",
    )(recv.reshape(pair_count * row_count, width), means, inverse, incidence, fit)


def solution(mesh):
    in_specs = (P("ifg", "tile", None), P(), P(None, "ifg"), P(), P())
    out_specs = (P(None, "tile", "ifg"), P("tile", "ifg"))
    return jax.shard_map(shards, mesh=mesh, in_specs=in_specs, out_specs=out_specs, check_vma=False)
```

```python
import functools
import math

import jax
import jax.numpy as jnp
from jax import lax
from jax.experimental import pallas as pl
from jax.experimental.pallas import tpu as pltpu
from jax.sharding import PartitionSpec as P

EPS = 1e-06
RIDGE = 1.0
VMEM = pl.BlockSpec(memory_space=pltpu.VMEM)
SMEM = pl.BlockSpec(memory_space=pltpu.SMEM)


def design(epochs, count):
    index = jnp.arange(count, dtype=jnp.int32)
    days = index.astype(jnp.float32)
    scaled = 2.0 * days / (count - 1) - 1.0
    years = days * 12.0 / 365.25
    smooth = jnp.stack(
        [
            jnp.ones_like(days),
            scaled,
            scaled * scaled,
            scaled * scaled * scaled,
            jnp.sin(2.0 * math.pi * years),
            jnp.cos(2.0 * math.pi * years),
            jnp.sin(4.0 * math.pi * years),
            jnp.cos(4.0 * math.pi * years),
        ],
        axis=1,
    )
    jumps = (index[:, None] >= epochs[None, :]).astype(jnp.float32)
    return jnp.concatenate([smooth, jumps], axis=1)


def fit_operator(epochs, count):
    matrix = design(epochs, count)
    normal = jnp.dot(
        matrix.T, matrix, precision=lax.Precision.HIGHEST, preferred_element_type=jnp.float32
    )
    normal = normal + RIDGE * jnp.eye(matrix.shape[1], dtype=jnp.float32)
    factor = jnp.linalg.cholesky(normal)
    return jax.scipy.linalg.cho_solve((factor, True), matrix.T)


def incidence_matrix(pairs, count):
    dates = jnp.arange(count, dtype=jnp.int32)
    later = (pairs[:, 1:2] == dates[None, :]).astype(jnp.bfloat16)
    earlier = (pairs[:, 0:1] == dates[None, :]).astype(jnp.bfloat16)
    return later - earlier


def sums_kernel(row_count, ref_ref, send_ref, out_ref, acc_ref):
    blocks, rows, width = send_ref.shape
    ifg_count = rows // row_count
    cols = blocks * width
    first = lax.axis_index("tile") * row_count
    row = lax.broadcasted_iota(jnp.int32, (8, cols), 0) % row_count + first
    flat = row * cols + lax.broadcasted_iota(jnp.int32, (8, cols), 1)

    def count(i, weight):
        return weight + jnp.where(flat == ref_ref[i], 1.0, 0.0)

    weight = lax.fori_loop(
        0, ref_ref.shape[0], count, jnp.zeros((8, cols), jnp.float32), unroll=8
    )
    acc = jnp.zeros((rows // 8, 8, width), jnp.float32)
    for j in range(blocks):
        values = send_ref[j].astype(jnp.float32).reshape(rows // 8, 8, width)
        acc = acc + values * weight[None, :, j * width : (j + 1) * width]
    acc_ref[...] = acc.reshape(rows, width)
    per_ifg = acc_ref[pl.ds(0, ifg_count, stride=row_count), :]
    for r in range(1, row_count):
        per_ifg = per_ifg + acc_ref[pl.ds(r, ifg_count, stride=row_count), :]
    out_ref[...] = lax.dot_general(
        jnp.ones((8, width), jnp.float32),
        per_ifg,
        (((1,), (1,)), ((), ())),
        precision=lax.Precision.HIGHEST,
        preferred_element_type=jnp.float32,
    )


def partial_sums(ifgs, send, ref_pixels):
    ifg_count, row_count, cols = ifgs.shape
    if send.shape[1] % 16:
        tile = lax.axis_index("tile")
        pixel = jnp.arange(row_count * cols, dtype=jnp.int32) + tile * row_count * cols
        weight = jnp.sum((ref_pixels[:, None] == pixel[None, :]).astype(jnp.float32), axis=0)
        weight = weight.reshape(1, row_count, cols)
        return jnp.sum(ifgs.astype(jnp.float32) * weight, axis=(1, 2))
    sums = pl.pallas_call(
        functools.partial(sums_kernel, row_count),
        out_shape=jax.ShapeDtypeStruct((8, ifg_count), jnp.float32),
        in_specs=[SMEM, VMEM],
        out_specs=VMEM,
        scratch_shapes=[pltpu.VMEM(send.shape[1:], jnp.float32)],
        name="region_sums",
    )(ref_pixels, send)
    return sums[0]


def post_kernel(row_count, recv_ref, mean_ref, inverse_ref, incidence_ref, fit_ref,
                coeff_ref, spread_ref, wide_ref, corr_ref):
    pairs, dates = incidence_ref.shape
    width = recv_ref.shape[1]
    step = 128 if pairs % 128 == 0 else pairs
    for k in range(0, pairs, step):
        wide_ref[...] = recv_ref[row_count * k : row_count * (k + step), :].astype(jnp.float32)
        mean = mean_ref[k : k + step, :]
        for r in range(row_count):
            values = wide_ref[pl.ds(r, step, stride=row_count), :]
            corr_ref[k : k + step, r * width : (r + 1) * width] = (values - mean).astype(
                jnp.bfloat16
            )
    displacement = jnp.dot(
        inverse_ref[...], corr_ref[...], preferred_element_type=jnp.float32
    )
    spans = [(slice(k, k + step), slice(k, k + step)) for k in range(0, pairs, step)]
    finish(row_count, displacement, spans, incidence_ref, fit_ref, coeff_ref, spread_ref, corr_ref)


ANY = pl.BlockSpec(memory_space=pl.ANY)
PAD = 16
PLANES = 4
COST = 6_000_000_000
LANES = 128
SMALL = pltpu.CompilerParams(vmem_limit_bytes=16 * 1024 * 1024)


def pack_kernel(row_count, ref_hbm, ifgs_hbm, columns_hbm, blocks, share,
                refs, columns, in_sems, misc_sems):
    ifg_count, _, cols = ifgs_hbm.shape
    count, width = blocks.shape[0], blocks.shape[3]
    rest = columns.shape[1] - 2 * LANES
    ref_copy = pltpu.make_async_copy(ref_hbm, refs, misc_sems.at[0])
    ref_copy.start()
    ins = [
        pltpu.make_async_copy(
            ifgs_hbm.at[:, :, pl.ds(j * width, width)], blocks.at[j], in_sems.at[j]
        )
        for j in range(count)
    ]
    for copy in ins:
        copy.start()
    columns_copy = pltpu.make_async_copy(columns_hbm, columns, misc_sems.at[1])
    columns_copy.start()
    tile = lax.axis_index("tile")
    flat = lax.broadcasted_iota(jnp.int32, (8, cols), 1) + cols * (
        lax.broadcasted_iota(jnp.int32, (8, cols), 0) % row_count + tile * row_count
    )
    ref_copy.wait()
    weight = jnp.zeros((8, cols), jnp.float32)
    for i in range(refs.shape[0]):
        weight = weight + jnp.where(flat == refs[i], 1.0, 0.0)
    weight = weight.astype(jnp.bfloat16)
    columns_copy.wait()

    @pl.when(tile == 0)
    def _():
        share[:96, :] = columns[:96, :LANES]

    @pl.when(tile == 1)
    def _():
        share[:48, :] = columns[96:, :LANES]
        share[48:96, :] = columns[:48, LANES : 2 * LANES]

    @pl.when(tile == 2)
    def _():
        share[:96, :] = columns[48:, LANES : 2 * LANES]

    @pl.when(tile == 3)
    def _():
        left = columns[:80, 2 * LANES :].astype(jnp.float32)
        right = columns[80:, 2 * LANES :].astype(jnp.float32)
        left = jnp.pad(left, ((0, 16), (0, LANES // 2 - rest)))
        right = jnp.pad(right, ((0, 32), (0, LANES // 2 - rest)))
        share[:96, :] = jnp.concatenate([left, right], axis=1).astype(jnp.bfloat16)

    for copy in ins:
        copy.wait()
    flat_blocks = blocks.reshape(count, ifg_count * row_count, width)
    totals = 0.0
    for j in range(count):
        totals = totals + lax.dot_general(
            weight[:, j * width : (j + 1) * width],
            flat_blocks[j],
            (((1,), (1,)), ((), ())),
            preferred_element_type=jnp.float32,
        )
    row = lax.broadcasted_iota(jnp.int32, totals.shape, 0)
    lane = lax.broadcasted_iota(jnp.int32, totals.shape, 1)
    totals = jnp.sum(jnp.where(row == lane % row_count, totals, 0.0), axis=0, keepdims=True)
    totals = jnp.pad(totals, ((0, 0), (0, 3 * LANES - totals.shape[1])))
    high = totals.astype(jnp.bfloat16).astype(jnp.float32)
    middle = (totals - high).astype(jnp.bfloat16).astype(jnp.float32)
    terms = (high, middle, totals - high - middle)
    row = lax.broadcasted_iota(jnp.int32, (PAD, LANES), 0)
    under = jnp.zeros((PAD, LANES), jnp.float32)
    for t, term in enumerate(terms):
        for c in range(3):
            under = jnp.where(row == 3 * t + c, term[:, c * LANES : (c + 1) * LANES], under)
    share[96:, :] = under.astype(jnp.bfloat16)


def pack(ref_pixels, ifgs, columns, blocks):
    ifg_count, row_count, cols = ifgs.shape
    shape = (blocks, ifg_count, row_count, cols // blocks)
    return pl.pallas_call(
        functools.partial(pack_kernel, row_count),
        out_shape=(pltpu.VMEM(shape, jnp.bfloat16), pltpu.VMEM((96 + PAD, LANES), jnp.bfloat16)),
        in_specs=[ANY] * 3,
        out_specs=(VMEM, VMEM),
        scratch_shapes=[
            pltpu.SMEM(ref_pixels.shape, jnp.int32),
            pltpu.VMEM(columns.shape, jnp.bfloat16),
            pltpu.SemaphoreType.DMA((blocks,)),
            pltpu.SemaphoreType.DMA((2,)),
        ],
        name="pack",
    )(ref_pixels, ifgs, columns)


def fit_kernel(date_count, epochs_ref, fit_ref):
    terms, lanes = fit_ref.shape
    index = lax.broadcasted_iota(jnp.int32, (terms, lanes), 1)
    row = lax.broadcasted_iota(jnp.int32, (terms, lanes), 0)
    days = index.astype(jnp.float32)
    scaled = 2.0 * days / (date_count - 1) - 1.0
    years = days * 12.0 / 365.25
    smooth = [
        jnp.ones_like(days),
        scaled,
        scaled * scaled,
        scaled * scaled * scaled,
        jnp.sin(2.0 * math.pi * years),
        jnp.cos(2.0 * math.pi * years),
        jnp.sin(4.0 * math.pi * years),
        jnp.cos(4.0 * math.pi * years),
    ]
    matrix = jnp.zeros((terms, lanes), jnp.float32)
    for r, values in enumerate(smooth):
        matrix = jnp.where(row == r, values, matrix)
    for e in range(epochs_ref.shape[0]):
        step = jnp.where(index >= epochs_ref[e], 1.0, 0.0)
        matrix = jnp.where(row == len(smooth) + e, step, matrix)
    matrix = jnp.where(index < date_count, matrix, 0.0)
    normal = lax.dot_general(
        matrix,
        matrix,
        (((1,), (1,)), ((), ())),
        precision=lax.Precision.HIGHEST,
        preferred_element_type=jnp.float32,
    )
    place = lax.broadcasted_iota(jnp.int32, (terms, terms), 0)
    diagonal = place == lax.broadcasted_iota(jnp.int32, (terms, terms), 1)
    normal = normal + jnp.where(diagonal, RIDGE, 0.0)
    for j in range(terms):
        scale = 1.0 / normal[j : j + 1, j : j + 1]
        pivot, right = normal[j : j + 1, :] * scale, matrix[j : j + 1, :] * scale
        factor = normal[:, j : j + 1]
        normal = jnp.where(place == j, pivot, normal - factor * pivot)
        matrix = jnp.where(row == j, right, matrix - factor * right)
    fit_ref[...] = matrix


def prepare_kernel(row_count, region_size, *refs):
    *part_refs, operator_ref, mean_ref, all_ref, sums_ref = refs
    pairs, width = mean_ref.shape
    ifg, tile = lax.axis_index("ifg"), lax.axis_index("tile")
    blocks = 2 * PLANES
    ifg_count = pairs // blocks
    for position, part_ref in enumerate(part_refs):
        flip, away = position // 2, position % 2
        for m in range(PLANES):
            all_ref[tile ^ flip, ifg ^ (2 * m + away)] = part_ref[m]
    row = lax.broadcasted_iota(jnp.int32, (4 * PAD, 3 * width), 0) % PAD
    lane = lax.broadcasted_iota(jnp.int32, (4 * PAD, 3 * width), 1)
    select = jnp.where((row < 9) & (row % 3 == lane // width), 1.0, 0.0).astype(jnp.bfloat16)
    for block in range(blocks):
        top = block * ifg_count
        operator_ref[top : top + 96, :LANES] = all_ref[0, block, :96, :]
        operator_ref[top + 96 : top + 144, :LANES] = all_ref[1, block, :48, :]
        operator_ref[top : top + 48, LANES : 2 * LANES] = all_ref[1, block, 48:96, :]
        operator_ref[top + 48 : top + 144, LANES : 2 * LANES] = all_ref[2, block, :96, :]
        rest = all_ref[3, block, :80, :].astype(jnp.float32)
        blank = jnp.zeros((80, LANES // 2), jnp.float32)
        left = jnp.concatenate([rest[:, : LANES // 2], blank], axis=1)
        right = jnp.concatenate([rest[:, LANES // 2 :], blank], axis=1)
        operator_ref[top : top + 80, 2 * LANES :] = left.astype(jnp.bfloat16)
        operator_ref[top + 80 : top + 144, 2 * LANES :] = right[:64].astype(jnp.bfloat16)
        totals = lax.dot_general(
            jnp.concatenate([all_ref[t, block, 96:, :] for t in range(4)]),
            select,
            (((0,), (0,)), ((), ())),
            preferred_element_type=jnp.float32,
        )
        for c in range(3):
            sums_ref[c * LANES : (c + 1) * LANES, :] = totals[:, c * width : (c + 1) * width]
        total = sums_ref[pl.ds(0, ifg_count, stride=row_count), :]
        for r in range(1, row_count):
            total = total + sums_ref[pl.ds(r, ifg_count, stride=row_count), :]
        mean_ref[top : top + ifg_count, :] = total / region_size


def invert_kernel(row_count, recv_ref, operator_ref, mean_ref, incidence_ref, fit_ref,
                  coeff_ref, spread_ref, wide_ref, corr_ref):
    blocks, rows, width = recv_ref.shape
    ifg_count = rows // row_count
    spans = []
    for block in range(blocks):
        span = slice(block * ifg_count, (block + 1) * ifg_count)
        spans.append((span, span))
        wide_ref[...] = recv_ref[block].astype(jnp.float32)
        mean = mean_ref[span, :]
        for r in range(row_count):
            values = wide_ref[pl.ds(r, ifg_count, stride=row_count), :]
            corr_ref[span, r * width : (r + 1) * width] = (values - mean).astype(jnp.bfloat16)
    displacement = lax.dot_general(
        operator_ref[...],
        corr_ref[...],
        (((0,), (0,)), ((), ())),
        preferred_element_type=jnp.float32,
    )
    finish(row_count, displacement, spans, incidence_ref, fit_ref, coeff_ref, spread_ref, corr_ref)


def finish(row_count, displacement, spans, incidence_ref, fit_ref, coeff_ref, spread_ref, corr_ref):
    pairs = incidence_ref.shape[0]
    width = corr_ref.shape[1] // row_count
    coeffs = jnp.dot(
        fit_ref[...],
        displacement,
        precision=lax.Precision.HIGHEST,
        preferred_element_type=jnp.float32,
    )
    high = displacement.astype(jnp.bfloat16)
    low = (displacement - high.astype(jnp.float32)).astype(jnp.bfloat16)
    total = jnp.zeros((8, row_count * width), jnp.float32)
    for span, rows in spans:
        incidence = incidence_ref[span, :]
        predicted = jnp.dot(incidence, high, preferred_element_type=jnp.float32) + jnp.dot(
            incidence, low, preferred_element_type=jnp.float32
        )
        misfit = corr_ref[rows, :].astype(jnp.float32) - predicted
        total = total + jnp.sum((misfit * misfit).reshape(-1, 8, misfit.shape[1]), axis=0)
    spread = jnp.sqrt(jnp.sum(total, axis=0, keepdims=True) / pairs + EPS)
    for r in range(row_count):
        coeff_ref[:, r, :] = coeffs[:, r * width : (r + 1) * width]
        spread_ref[r : r + 1, :] = spread[:, r * width : (r + 1) * width]


def trade(array, bit):
    size = lax.axis_size("ifg")
    return lax.ppermute(array, "ifg", [(i, i ^ bit) for i in range(size)])


def trade_and_swap(array, bit, other):
    size, tiles = lax.axis_size("ifg"), lax.axis_size("tile")
    moves = [
        (i * tiles + t, (i ^ bit) * tiles + (t ^ other)) for i in range(size) for t in range(tiles)
    ]
    return lax.ppermute(array, ("ifg", "tile"), moves)


def small_slice(ifgs, pairs, pseudo_inverse, ref_pixels, epochs):
    ifg_count, row_count, cols = ifgs.shape
    blocks = lax.axis_size("ifg")
    width = cols // blocks
    date_count = pseudo_inverse.shape[0]
    pair_count = blocks * ifg_count
    lanes = 3 * LANES

    send, share = pack(ref_pixels, ifgs, pseudo_inverse.T, blocks)
    shares = [share] + [trade(share, 2 * m) for m in range(1, PLANES)]
    recv = lax.all_to_all(
        send.reshape(blocks, ifg_count * row_count, width), "ifg", 0, 0, tiled=True
    )
    own = jnp.stack(shares)
    own, pairs, epochs = lax.optimization_barrier((own, pairs, epochs))
    across = trade(own, 1)
    up = swap(own, 2)
    across_up = trade_and_swap(own, 1, 2)
    incidence = incidence_matrix(pairs, lanes)
    terms = 8 + epochs.shape[0]
    fit = pl.pallas_call(
        functools.partial(fit_kernel, date_count),
        out_shape=pltpu.VMEM((terms, lanes), jnp.float32),
        in_specs=[SMEM],
        out_specs=VMEM,
        compiler_params=SMALL,
        name="fit",
    )(epochs)
    across, incidence, fit = lax.optimization_barrier((across, incidence, fit))
    parts = [own, across, swap(own, 1), swap(across, 1)]
    parts = parts + [up, across_up, swap(up, 1), swap(across_up, 1)]
    operator, means = pl.pallas_call(
        functools.partial(prepare_kernel, row_count, ref_pixels.shape[0]),
        out_shape=(
            pltpu.VMEM((pair_count, lanes), jnp.bfloat16),
            pltpu.VMEM((pair_count, width), jnp.float32),
        ),
        in_specs=[VMEM] * 8,
        out_specs=(VMEM, VMEM),
        scratch_shapes=[
            pltpu.VMEM((4, blocks) + share.shape, jnp.bfloat16),
            pltpu.VMEM((3 * LANES, width), jnp.float32),
        ],
        compiler_params=SMALL,
        cost_estimate=pl.CostEstimate(flops=COST, bytes_accessed=0, transcendentals=0),
        name="prepare",
    )(*parts)
    return pl.pallas_call(
        functools.partial(invert_kernel, row_count),
        out_shape=(
            jax.ShapeDtypeStruct((terms, row_count, width), jnp.float32),
            jax.ShapeDtypeStruct((row_count, width), jnp.float32),
        ),
        in_specs=[VMEM] * 5,
        out_specs=(VMEM, VMEM),
        scratch_shapes=[
            pltpu.VMEM((row_count * ifg_count, width), jnp.float32),
            pltpu.VMEM((pair_count, row_count * width), jnp.bfloat16),
        ],
        compiler_params=SMALL,
        name="invert",
    )(recv, operator, means, incidence, fit)


def swap(array, bit):
    size = lax.axis_size("tile")
    return lax.ppermute(array, "tile", [(i, i ^ bit) for i in range(size)])


def tile_gather(array):
    size = lax.axis_size("tile")
    tile = lax.axis_index("tile")
    parts = [array]
    bit = size // 2
    order = []
    while bit:
        parts = parts + [swap(part, bit) for part in parts]
        order.append(bit)
        bit //= 2
    stacked = jnp.stack(parts)
    offset = [0] * size
    for position in range(size):
        mask = 0
        for place, bit in enumerate(order):
            if position >> place & 1:
                mask |= bit
        offset[mask] = position
    stacked = jnp.stack([parts[offset[m]] for m in range(size)])
    for bit in order:
        swapped = stacked.reshape((size // (2 * bit), 2, bit) + array.shape)
        swapped = jnp.flip(swapped, axis=1).reshape(stacked.shape)
        stacked = jnp.where((tile & bit) != 0, swapped, stacked)
    return stacked


def split_sum(value):
    high = lax.reduce_precision(value, 8, 7)
    middle = lax.reduce_precision(value - high, 8, 7)
    low = lax.reduce_precision(value - high - middle, 8, 7)
    return jnp.stack([high, middle, low]).astype(jnp.bfloat16)


def shards(ifgs, pairs, pseudo_inverse, ref_pixels, epochs):
    ifg_count, row_count, cols = ifgs.shape
    blocks = lax.axis_size("ifg")
    tiles = lax.axis_size("tile")
    shape = (blocks, tiles, ifg_count, row_count, cols // blocks)
    dates = pseudo_inverse.shape[0]
    if shape == (2 * PLANES, 4, 144, 2, LANES) and 2 * LANES < dates <= 320:
        return small_slice(ifgs, pairs, pseudo_inverse, ref_pixels, epochs)
    width = cols // blocks
    date_count = pseudo_inverse.shape[0]
    pair_count = blocks * ifg_count
    dates = -(-date_count // 16) * 16
    tile = lax.axis_index("tile")

    send = ifgs.reshape(ifg_count, row_count, blocks, width).transpose(2, 0, 1, 3)
    send = send.reshape(blocks, ifg_count * row_count, width)

    share = -(-ifg_count // tiles)
    columns = jnp.pad(pseudo_inverse.T, ((0, share * tiles - ifg_count), (0, 0)))
    columns = lax.dynamic_slice_in_dim(columns, tile * share, share, 0)
    lanes = max(date_count, ifg_count)
    sums = split_sum(partial_sums(ifgs, send, ref_pixels))
    payload = jnp.concatenate(
        [
            jnp.pad(columns, ((0, 0), (0, lanes - date_count))),
            jnp.pad(sums, ((0, 0), (0, lanes - ifg_count))),
        ]
    )
    payload = jnp.broadcast_to(payload[None], (blocks,) + payload.shape)
    payload = lax.all_to_all(payload, "ifg", 0, 0, tiled=True)
    recv = lax.all_to_all(send, "ifg", 0, 0, tiled=True)
    gathered = tile_gather(payload)

    inverse = gathered[:, :, :share, :date_count].transpose(3, 1, 0, 2)
    inverse = inverse.reshape(date_count, blocks, tiles * share)[:, :, :ifg_count]
    inverse = jnp.pad(
        inverse.reshape(date_count, pair_count), ((0, dates - date_count), (0, 0))
    )
    totals = jnp.sum(gathered[:, :, share:, :ifg_count].astype(jnp.float32), axis=(0, 2))
    means = (totals / ref_pixels.shape[0]).reshape(pair_count, 1)
    means = jnp.broadcast_to(means, (pair_count, width))
    incidence = incidence_matrix(pairs, dates)
    fit = jnp.pad(fit_operator(epochs, date_count), ((0, 0), (0, dates - date_count)))

    terms = fit.shape[0]
    return pl.pallas_call(
        functools.partial(post_kernel, row_count),
        out_shape=(
            jax.ShapeDtypeStruct((terms, row_count, width), jnp.float32),
            jax.ShapeDtypeStruct((row_count, width), jnp.float32),
        ),
        in_specs=[VMEM] * 5,
        out_specs=(VMEM, VMEM),
        scratch_shapes=[
            pltpu.VMEM(
                (row_count * (128 if pair_count % 128 == 0 else pair_count), width), jnp.float32
            ),
            pltpu.VMEM((pair_count, row_count * width), jnp.bfloat16),
        ],
        compiler_params=pltpu.CompilerParams(vmem_limit_bytes=32 * 1024 * 1024),
        name="invert",
    )(recv.reshape(pair_count * row_count, width), means, inverse, incidence, fit)


def solution(mesh):
    in_specs = (P("ifg", "tile", None), P(), P(None, "ifg"), P(), P())
    out_specs = (P(None, "tile", "ifg"), P("tile", "ifg"))
    return jax.shard_map(shards, mesh=mesh, in_specs=in_specs, out_specs=out_specs, check_vma=False)
```

```python
import functools
import math

import jax
import jax.numpy as jnp
from jax import lax
from jax.experimental import pallas as pl
from jax.experimental.pallas import tpu as pltpu
from jax.sharding import PartitionSpec as P

EPS = 1e-06
RIDGE = 1.0
VMEM = pl.BlockSpec(memory_space=pltpu.VMEM)
SMEM = pl.BlockSpec(memory_space=pltpu.SMEM)


def design(epochs, count):
    index = jnp.arange(count, dtype=jnp.int32)
    days = index.astype(jnp.float32)
    scaled = 2.0 * days / (count - 1) - 1.0
    years = days * 12.0 / 365.25
    smooth = jnp.stack(
        [
            jnp.ones_like(days),
            scaled,
            scaled * scaled,
            scaled * scaled * scaled,
            jnp.sin(2.0 * math.pi * years),
            jnp.cos(2.0 * math.pi * years),
            jnp.sin(4.0 * math.pi * years),
            jnp.cos(4.0 * math.pi * years),
        ],
        axis=1,
    )
    jumps = (index[:, None] >= epochs[None, :]).astype(jnp.float32)
    return jnp.concatenate([smooth, jumps], axis=1)


def fit_operator(epochs, count):
    matrix = design(epochs, count)
    normal = jnp.dot(
        matrix.T, matrix, precision=lax.Precision.HIGHEST, preferred_element_type=jnp.float32
    )
    normal = normal + RIDGE * jnp.eye(matrix.shape[1], dtype=jnp.float32)
    factor = jnp.linalg.cholesky(normal)
    return jax.scipy.linalg.cho_solve((factor, True), matrix.T)


def incidence_matrix(pairs, count):
    dates = jnp.arange(-(-(2 * count - 256) // 128) * 128, dtype=jnp.int32)
    dates = jnp.where(dates < count, dates, jnp.where(dates < 2 * count - 256, dates - count + 256, -1))
    later = (pairs[:, 1:2] == dates[None, :]).astype(jnp.bfloat16)
    earlier = (pairs[:, 0:1] == dates[None, :]).astype(jnp.bfloat16)
    return later - earlier


def sums_kernel(row_count, ref_ref, send_ref, out_ref, acc_ref):
    blocks, rows, width = send_ref.shape
    ifg_count = rows // row_count
    cols = blocks * width
    first = lax.axis_index("tile") * row_count
    row = lax.broadcasted_iota(jnp.int32, (8, cols), 0) % row_count + first
    flat = row * cols + lax.broadcasted_iota(jnp.int32, (8, cols), 1)

    def count(i, weight):
        return weight + jnp.where(flat == ref_ref[i], 1.0, 0.0)

    weight = lax.fori_loop(
        0, ref_ref.shape[0], count, jnp.zeros((8, cols), jnp.float32), unroll=8
    )
    acc = jnp.zeros((rows // 8, 8, width), jnp.float32)
    for j in range(blocks):
        values = send_ref[j].astype(jnp.float32).reshape(rows // 8, 8, width)
        acc = acc + values * weight[None, :, j * width : (j + 1) * width]
    acc_ref[...] = acc.reshape(rows, width)
    per_ifg = acc_ref[pl.ds(0, ifg_count, stride=row_count), :]
    for r in range(1, row_count):
        per_ifg = per_ifg + acc_ref[pl.ds(r, ifg_count, stride=row_count), :]
    out_ref[...] = lax.dot_general(
        jnp.ones((8, width), jnp.float32),
        per_ifg,
        (((1,), (1,)), ((), ())),
        precision=lax.Precision.HIGHEST,
        preferred_element_type=jnp.float32,
    )


def partial_sums(ifgs, send, ref_pixels):
    ifg_count, row_count, cols = ifgs.shape
    if send.shape[1] % 16:
        tile = lax.axis_index("tile")
        pixel = jnp.arange(row_count * cols, dtype=jnp.int32) + tile * row_count * cols
        weight = jnp.sum((ref_pixels[:, None] == pixel[None, :]).astype(jnp.float32), axis=0)
        weight = weight.reshape(1, row_count, cols)
        return jnp.sum(ifgs.astype(jnp.float32) * weight, axis=(1, 2))
    sums = pl.pallas_call(
        functools.partial(sums_kernel, row_count),
        out_shape=jax.ShapeDtypeStruct((8, ifg_count), jnp.float32),
        in_specs=[SMEM, VMEM],
        out_specs=VMEM,
        scratch_shapes=[pltpu.VMEM(send.shape[1:], jnp.float32)],
        name="region_sums",
    )(ref_pixels, send)
    return sums[0]


def post_kernel(row_count, recv_ref, mean_ref, inverse_ref, incidence_ref, fit_ref,
                coeff_ref, spread_ref, wide_ref, corr_ref):
    pairs = incidence_ref.shape[0]
    width = recv_ref.shape[1]
    step = 128 if pairs % 128 == 0 else pairs
    for k in range(0, pairs, step):
        wide_ref[...] = recv_ref[row_count * k : row_count * (k + step), :].astype(jnp.float32)
        mean = mean_ref[k : k + step, :]
        for r in range(row_count):
            values = wide_ref[pl.ds(r, step, stride=row_count), :]
            corr_ref[k : k + step, r * width : (r + 1) * width] = (values - mean).astype(
                jnp.bfloat16
            )
    displacement = jnp.dot(
        inverse_ref[...], corr_ref[...], preferred_element_type=jnp.float32
    )
    spans = [(slice(k, k + step), slice(k, k + step)) for k in range(0, pairs, step)]
    finish(row_count, displacement, spans, incidence_ref, fit_ref, coeff_ref, spread_ref, corr_ref)


ANY = pl.BlockSpec(memory_space=pl.ANY)
PAD = 16
PLANES = 4
COST = 6_000_000_000
LANES = 128
SMALL = pltpu.CompilerParams(vmem_limit_bytes=16 * 1024 * 1024)


def pack_kernel(row_count, ref_hbm, ifgs_hbm, columns_hbm, blocks, share,
                refs, columns, weight_ref, in_sems, misc_sems):
    ifg_count, _, cols = ifgs_hbm.shape
    count, width = blocks.shape[0], blocks.shape[3]
    rest = columns.shape[1] - 2 * LANES
    ref_copy = pltpu.make_async_copy(ref_hbm, refs, misc_sems.at[0])
    ref_copy.start()
    ins = [
        pltpu.make_async_copy(
            ifgs_hbm.at[:, :, pl.ds(j * width, width)], blocks.at[j], in_sems.at[j]
        )
        for j in range(count)
    ]
    for copy in ins:
        copy.start()
    columns_copy = pltpu.make_async_copy(columns_hbm, columns, misc_sems.at[1])
    columns_copy.start()
    tile = lax.axis_index("tile")
    flat = lax.broadcasted_iota(jnp.int32, (8, cols), 1) + cols * (
        lax.broadcasted_iota(jnp.int32, (8, cols), 0) % row_count + tile * row_count
    )
    ref_copy.wait()
    weight = jnp.zeros((8, cols), jnp.float32)
    for i in range(refs.shape[0]):
        weight = weight + jnp.where(flat == refs[i], 1.0, 0.0)
    weight_ref[...] = weight
    columns_copy.wait()

    @pl.when(tile == 0)
    def _():
        share[:96, :] = columns[:96, :LANES]

    @pl.when(tile == 1)
    def _():
        share[:48, :] = columns[96:, :LANES]
        share[48:96, :] = columns[:48, LANES : 2 * LANES]

    @pl.when(tile == 2)
    def _():
        share[:96, :] = columns[48:, LANES : 2 * LANES]

    @pl.when(tile == 3)
    def _():
        left = columns[:80, 2 * LANES :].astype(jnp.float32)
        right = columns[80:, 2 * LANES :].astype(jnp.float32)
        left = jnp.pad(left, ((0, 16), (0, LANES // 2 - rest)))
        right = jnp.pad(right, ((0, 32), (0, LANES // 2 - rest)))
        share[:96, :] = jnp.concatenate([left, right], axis=1).astype(jnp.bfloat16)

    for copy in ins:
        copy.wait()
    flat_blocks = blocks.reshape(count, ifg_count * row_count, width)
    totals = 0.0
    for j in range(count):
        totals = totals + lax.dot_general(
            weight_ref[:, j * width : (j + 1) * width].astype(jnp.bfloat16),
            flat_blocks[j],
            (((1,), (1,)), ((), ())),
            preferred_element_type=jnp.float32,
        )
    row = lax.broadcasted_iota(jnp.int32, totals.shape, 0)
    lane = lax.broadcasted_iota(jnp.int32, totals.shape, 1)
    totals = jnp.sum(jnp.where(row == lane % row_count, totals, 0.0), axis=0, keepdims=True)
    totals = jnp.pad(totals, ((0, 0), (0, 3 * LANES - totals.shape[1])))
    high = totals.astype(jnp.bfloat16).astype(jnp.float32)
    middle = (totals - high).astype(jnp.bfloat16).astype(jnp.float32)
    terms = (high, middle, totals - high - middle)
    row = lax.broadcasted_iota(jnp.int32, (PAD, LANES), 0)
    under = jnp.zeros((PAD, LANES), jnp.float32)
    for t, term in enumerate(terms):
        for c in range(3):
            under = jnp.where(row == 3 * t + c, term[:, c * LANES : (c + 1) * LANES], under)
    share[96:, :] = under.astype(jnp.bfloat16)


def pack(ref_pixels, ifgs, columns, blocks):
    ifg_count, row_count, cols = ifgs.shape
    shape = (blocks, ifg_count, row_count, cols // blocks)
    return pl.pallas_call(
        functools.partial(pack_kernel, row_count),
        out_shape=(pltpu.VMEM(shape, jnp.bfloat16), pltpu.VMEM((96 + PAD, LANES), jnp.bfloat16)),
        in_specs=[ANY] * 3,
        out_specs=(VMEM, VMEM),
        scratch_shapes=[
            pltpu.SMEM(ref_pixels.shape, jnp.int32),
            pltpu.VMEM(columns.shape, jnp.bfloat16),
            pltpu.VMEM((8, cols), jnp.float32),
            pltpu.SemaphoreType.DMA((blocks,)),
            pltpu.SemaphoreType.DMA((2,)),
        ],
        name="pack",
    )(ref_pixels, ifgs, columns)


def fit_kernel(date_count, epochs_ref, fit_ref):
    terms, lanes = fit_ref.shape
    index = lax.broadcasted_iota(jnp.int32, (terms, lanes), 1)
    row = lax.broadcasted_iota(jnp.int32, (terms, lanes), 0)
    days = index.astype(jnp.float32)
    scaled = 2.0 * days / (date_count - 1) - 1.0
    years = days * 12.0 / 365.25
    smooth = [
        jnp.ones_like(days),
        scaled,
        scaled * scaled,
        scaled * scaled * scaled,
        jnp.sin(2.0 * math.pi * years),
        jnp.cos(2.0 * math.pi * years),
        jnp.sin(4.0 * math.pi * years),
        jnp.cos(4.0 * math.pi * years),
    ]
    matrix = jnp.zeros((terms, lanes), jnp.float32)
    for r, values in enumerate(smooth):
        matrix = jnp.where(row == r, values, matrix)
    for e in range(epochs_ref.shape[0]):
        step = jnp.where(index >= epochs_ref[e], 1.0, 0.0)
        matrix = jnp.where(row == len(smooth) + e, step, matrix)
    matrix = jnp.where(index < date_count, matrix, 0.0)
    normal = lax.dot_general(
        matrix,
        matrix,
        (((1,), (1,)), ((), ())),
        precision=lax.Precision.HIGHEST,
        preferred_element_type=jnp.float32,
    )
    place = lax.broadcasted_iota(jnp.int32, (terms, terms), 0)
    diagonal = place == lax.broadcasted_iota(jnp.int32, (terms, terms), 1)
    normal = normal + jnp.where(diagonal, RIDGE, 0.0)
    for j in range(terms):
        scale = 1.0 / normal[j : j + 1, j : j + 1]
        pivot, right = normal[j : j + 1, :] * scale, matrix[j : j + 1, :] * scale
        factor = normal[:, j : j + 1]
        normal = jnp.where(place == j, pivot, normal - factor * pivot)
        matrix = jnp.where(row == j, right, matrix - factor * right)
    fit_ref[...] = matrix


def prepare_kernel(row_count, region_size, *refs):
    *part_refs, operator_ref, mean_ref, all_ref, sums_ref = refs
    pairs, width = mean_ref.shape
    ifg, tile = lax.axis_index("ifg"), lax.axis_index("tile")
    blocks = 2 * PLANES
    ifg_count = pairs // blocks
    for position, part_ref in enumerate(part_refs):
        flip, away = position // 2, position % 2
        for m in range(PLANES):
            all_ref[tile ^ flip, ifg ^ (2 * m + away)] = part_ref[m]
    row = lax.broadcasted_iota(jnp.int32, (4 * PAD, 3 * width), 0) % PAD
    lane = lax.broadcasted_iota(jnp.int32, (4 * PAD, 3 * width), 1)
    select = jnp.where((row < 9) & (row % 3 == lane // width), 1.0, 0.0).astype(jnp.bfloat16)
    for block in range(blocks):
        top = block * ifg_count
        operator_ref[top : top + 96, :LANES] = all_ref[0, block, :96, :]
        operator_ref[top + 96 : top + 144, :LANES] = all_ref[1, block, :48, :]
        operator_ref[top : top + 48, LANES : 2 * LANES] = all_ref[1, block, 48:96, :]
        operator_ref[top + 48 : top + 144, LANES : 2 * LANES] = all_ref[2, block, :96, :]
        rest = all_ref[3, block, :80, :].astype(jnp.float32)
        blank = jnp.zeros((80, LANES // 2), jnp.float32)
        left = jnp.concatenate([rest[:, : LANES // 2], blank], axis=1)
        right = jnp.concatenate([rest[:, LANES // 2 :], blank], axis=1)
        operator_ref[top : top + 80, 2 * LANES :] = left.astype(jnp.bfloat16)
        operator_ref[top + 80 : top + 144, 2 * LANES :] = right[:64].astype(jnp.bfloat16)
        totals = lax.dot_general(
            jnp.concatenate([all_ref[t, block, 96:, :] for t in range(4)]),
            select,
            (((0,), (0,)), ((), ())),
            preferred_element_type=jnp.float32,
        )
        for c in range(3):
            top_row, count = c * LANES, min(LANES, sums_ref.shape[0] - c * LANES)
            sums_ref[top_row : top_row + count, :] = totals[:count, c * width : (c + 1) * width]
        total = sums_ref[pl.ds(0, ifg_count, stride=row_count), :]
        for r in range(1, row_count):
            total = total + sums_ref[pl.ds(r, ifg_count, stride=row_count), :]
        if region_size & (region_size - 1):
            mean_ref[top : top + ifg_count, :] = total / region_size
        else:
            mean_ref[top : top + ifg_count, :] = total * (1.0 / region_size)


def invert_kernel(row_count, dates, recv_ref, operator_ref, mean_ref, incidence_ref, fit_ref,
                  coeff_ref, spread_ref, wide_ref, corr_ref):
    blocks, rows, width = recv_ref.shape
    ifg_count = rows // row_count
    spans = []
    for block in range(blocks):
        span = slice(block * ifg_count, (block + 1) * ifg_count)
        spans.append((span, span))
        wide_ref[...] = recv_ref[block].astype(jnp.float32)
        mean = mean_ref[span, :]
        for r in range(row_count):
            values = wide_ref[pl.ds(r, ifg_count, stride=row_count), :]
            corr_ref[span, r * width : (r + 1) * width] = (values - mean).astype(jnp.bfloat16)
    displacement = lax.dot_general(
        operator_ref[:, :dates],
        corr_ref[...],
        (((0,), (0,)), ((), ())),
        preferred_element_type=jnp.float32,
    )
    finish(row_count, displacement, spans, incidence_ref, fit_ref, coeff_ref, spread_ref, corr_ref)


def finish(row_count, displacement, spans, incidence_ref, fit_ref, coeff_ref, spread_ref, corr_ref):
    pairs = incidence_ref.shape[0]
    width = corr_ref.shape[1] // row_count
    dates = displacement.shape[0]
    coeffs = jnp.dot(
        fit_ref[:, :dates],
        displacement,
        precision=lax.Precision.HIGHEST,
        preferred_element_type=jnp.float32,
    )
    high = displacement.astype(jnp.bfloat16)
    low = (displacement - high.astype(jnp.float32)).astype(jnp.bfloat16)
    blank = jnp.zeros((incidence_ref.shape[1] - 2 * dates + 256, high.shape[1]), jnp.bfloat16)
    rest = jnp.concatenate([high[256:], low[256:], blank])
    total = jnp.zeros((8, row_count * width), jnp.float32)
    for span, rows in spans:
        incidence = incidence_ref[span, :256]
        predicted = (
            jnp.dot(incidence, high[:256], preferred_element_type=jnp.float32)
            + jnp.dot(incidence, low[:256], preferred_element_type=jnp.float32)
            + jnp.dot(incidence_ref[span, 256:], rest, preferred_element_type=jnp.float32)
        )
        misfit = corr_ref[rows, :].astype(jnp.float32) - predicted
        total = total + jnp.sum((misfit * misfit).reshape(-1, 8, misfit.shape[1]), axis=0)
    spread = jnp.sqrt(jnp.sum(total, axis=0, keepdims=True) / pairs + EPS)
    for r in range(row_count):
        coeff_ref[:, r, :] = coeffs[:, r * width : (r + 1) * width]
        spread_ref[r : r + 1, :] = spread[:, r * width : (r + 1) * width]


def trade(array, bit):
    size = lax.axis_size("ifg")
    return lax.ppermute(array, "ifg", [(i, i ^ bit) for i in range(size)])


def trade_and_swap(array, bit, other):
    size, tiles = lax.axis_size("ifg"), lax.axis_size("tile")
    moves = [
        (i * tiles + t, (i ^ bit) * tiles + (t ^ other)) for i in range(size) for t in range(tiles)
    ]
    return lax.ppermute(array, ("ifg", "tile"), moves)


def small_slice(ifgs, pairs, pseudo_inverse, ref_pixels, epochs):
    ifg_count, row_count, cols = ifgs.shape
    blocks = lax.axis_size("ifg")
    width = cols // blocks
    date_count = pseudo_inverse.shape[0]
    pair_count = blocks * ifg_count
    lanes = 3 * LANES
    dates = -(-date_count // 16) * 16

    send, share = pack(ref_pixels, ifgs, pseudo_inverse.T, blocks)
    shares = [share] + [trade(share, 2 * m) for m in range(1, PLANES)]
    recv = lax.all_to_all(
        send.reshape(blocks, ifg_count * row_count, width), "ifg", 0, 0, tiled=True
    )
    own = jnp.stack(shares)
    own, pairs, epochs = lax.optimization_barrier((own, pairs, epochs))
    across = trade(own, 1)
    up = swap(own, 2)
    across_up = trade_and_swap(own, 1, 2)
    incidence = incidence_matrix(pairs, dates)
    terms = 8 + epochs.shape[0]
    fit = pl.pallas_call(
        functools.partial(fit_kernel, date_count),
        out_shape=pltpu.VMEM((terms, lanes), jnp.float32),
        in_specs=[SMEM],
        out_specs=VMEM,
        compiler_params=SMALL,
        name="fit",
    )(epochs)
    across, incidence, fit = lax.optimization_barrier((across, incidence, fit))
    parts = [own, across, swap(own, 1), swap(across, 1)]
    parts = parts + [up, across_up, swap(up, 1), swap(across_up, 1)]
    operator, means = pl.pallas_call(
        functools.partial(prepare_kernel, row_count, ref_pixels.shape[0]),
        out_shape=(
            pltpu.VMEM((pair_count, lanes), jnp.bfloat16),
            pltpu.VMEM((pair_count, width), jnp.float32),
        ),
        in_specs=[VMEM] * 8,
        out_specs=(VMEM, VMEM),
        scratch_shapes=[
            pltpu.VMEM((4, blocks) + share.shape, jnp.bfloat16),
            pltpu.VMEM((row_count * ifg_count, width), jnp.float32),
        ],
        compiler_params=SMALL,
        cost_estimate=pl.CostEstimate(flops=COST, bytes_accessed=0, transcendentals=0),
        name="prepare",
    )(*parts)
    return pl.pallas_call(
        functools.partial(invert_kernel, row_count, dates),
        out_shape=(
            jax.ShapeDtypeStruct((terms, row_count, width), jnp.float32),
            jax.ShapeDtypeStruct((row_count, width), jnp.float32),
        ),
        in_specs=[VMEM] * 5,
        out_specs=(VMEM, VMEM),
        scratch_shapes=[
            pltpu.VMEM((row_count * ifg_count, width), jnp.float32),
            pltpu.VMEM((pair_count, row_count * width), jnp.bfloat16),
        ],
        compiler_params=SMALL,
        name="invert",
    )(recv, operator, means, incidence, fit)


def swap(array, bit):
    size = lax.axis_size("tile")
    return lax.ppermute(array, "tile", [(i, i ^ bit) for i in range(size)])


def tile_gather(array):
    size = lax.axis_size("tile")
    tile = lax.axis_index("tile")
    parts = [array]
    bit = size // 2
    order = []
    while bit:
        parts = parts + [swap(part, bit) for part in parts]
        order.append(bit)
        bit //= 2
    stacked = jnp.stack(parts)
    offset = [0] * size
    for position in range(size):
        mask = 0
        for place, bit in enumerate(order):
            if position >> place & 1:
                mask |= bit
        offset[mask] = position
    stacked = jnp.stack([parts[offset[m]] for m in range(size)])
    for bit in order:
        swapped = stacked.reshape((size // (2 * bit), 2, bit) + array.shape)
        swapped = jnp.flip(swapped, axis=1).reshape(stacked.shape)
        stacked = jnp.where((tile & bit) != 0, swapped, stacked)
    return stacked


def split_sum(value):
    high = lax.reduce_precision(value, 8, 7)
    middle = lax.reduce_precision(value - high, 8, 7)
    low = lax.reduce_precision(value - high - middle, 8, 7)
    return jnp.stack([high, middle, low]).astype(jnp.bfloat16)


def shards(ifgs, pairs, pseudo_inverse, ref_pixels, epochs):
    ifg_count, row_count, cols = ifgs.shape
    blocks = lax.axis_size("ifg")
    tiles = lax.axis_size("tile")
    shape = (blocks, tiles, ifg_count, row_count, cols // blocks)
    dates = pseudo_inverse.shape[0]
    if shape == (2 * PLANES, 4, 144, 2, LANES) and 2 * LANES < dates <= 320:
        return small_slice(ifgs, pairs, pseudo_inverse, ref_pixels, epochs)
    width = cols // blocks
    date_count = pseudo_inverse.shape[0]
    pair_count = blocks * ifg_count
    dates = -(-date_count // 16) * 16
    tile = lax.axis_index("tile")

    send = ifgs.reshape(ifg_count, row_count, blocks, width).transpose(2, 0, 1, 3)
    send = send.reshape(blocks, ifg_count * row_count, width)

    share = -(-ifg_count // tiles)
    columns = jnp.pad(pseudo_inverse.T, ((0, share * tiles - ifg_count), (0, 0)))
    columns = lax.dynamic_slice_in_dim(columns, tile * share, share, 0)
    lanes = max(date_count, ifg_count)
    sums = split_sum(partial_sums(ifgs, send, ref_pixels))
    payload = jnp.concatenate(
        [
            jnp.pad(columns, ((0, 0), (0, lanes - date_count))),
            jnp.pad(sums, ((0, 0), (0, lanes - ifg_count))),
        ]
    )
    payload = jnp.broadcast_to(payload[None], (blocks,) + payload.shape)
    payload = lax.all_to_all(payload, "ifg", 0, 0, tiled=True)
    recv = lax.all_to_all(send, "ifg", 0, 0, tiled=True)
    gathered = tile_gather(payload)

    inverse = gathered[:, :, :share, :date_count].transpose(3, 1, 0, 2)
    inverse = inverse.reshape(date_count, blocks, tiles * share)[:, :, :ifg_count]
    inverse = jnp.pad(
        inverse.reshape(date_count, pair_count), ((0, dates - date_count), (0, 0))
    )
    totals = jnp.sum(gathered[:, :, share:, :ifg_count].astype(jnp.float32), axis=(0, 2))
    means = (totals / ref_pixels.shape[0]).reshape(pair_count, 1)
    means = jnp.broadcast_to(means, (pair_count, width))
    incidence = incidence_matrix(pairs, dates)
    fit = jnp.pad(fit_operator(epochs, date_count), ((0, 0), (0, dates - date_count)))

    terms = fit.shape[0]
    return pl.pallas_call(
        functools.partial(post_kernel, row_count),
        out_shape=(
            jax.ShapeDtypeStruct((terms, row_count, width), jnp.float32),
            jax.ShapeDtypeStruct((row_count, width), jnp.float32),
        ),
        in_specs=[VMEM] * 5,
        out_specs=(VMEM, VMEM),
        scratch_shapes=[
            pltpu.VMEM(
                (row_count * (128 if pair_count % 128 == 0 else pair_count), width), jnp.float32
            ),
            pltpu.VMEM((pair_count, row_count * width), jnp.bfloat16),
        ],
        compiler_params=pltpu.CompilerParams(vmem_limit_bytes=32 * 1024 * 1024),
        name="invert",
    )(recv.reshape(pair_count * row_count, width), means, inverse, incidence, fit)


def solution(mesh):
    in_specs = (P("ifg", "tile", None), P(), P(None, "ifg"), P(), P())
    out_specs = (P(None, "tile", "ifg"), P("tile", "ifg"))
    return jax.shard_map(shards, mesh=mesh, in_specs=in_specs, out_specs=out_specs, check_vma=False)
```

```python
import functools
import math

import jax
import jax.numpy as jnp
from jax import lax
from jax.experimental import pallas as pl
from jax.experimental.pallas import tpu as pltpu
from jax.sharding import PartitionSpec as P

EPS = 1e-06
RIDGE = 1.0
VMEM = pl.BlockSpec(memory_space=pltpu.VMEM)
SMEM = pl.BlockSpec(memory_space=pltpu.SMEM)


def design(epochs, count):
    index = jnp.arange(count, dtype=jnp.int32)
    days = index.astype(jnp.float32)
    scaled = 2.0 * days / (count - 1) - 1.0
    years = days * 12.0 / 365.25
    smooth = jnp.stack(
        [
            jnp.ones_like(days),
            scaled,
            scaled * scaled,
            scaled * scaled * scaled,
            jnp.sin(2.0 * math.pi * years),
            jnp.cos(2.0 * math.pi * years),
            jnp.sin(4.0 * math.pi * years),
            jnp.cos(4.0 * math.pi * years),
        ],
        axis=1,
    )
    jumps = (index[:, None] >= epochs[None, :]).astype(jnp.float32)
    return jnp.concatenate([smooth, jumps], axis=1)


def fit_operator(epochs, count):
    matrix = design(epochs, count)
    normal = jnp.dot(
        matrix.T, matrix, precision=lax.Precision.HIGHEST, preferred_element_type=jnp.float32
    )
    normal = normal + RIDGE * jnp.eye(matrix.shape[1], dtype=jnp.float32)
    factor = jnp.linalg.cholesky(normal)
    return jax.scipy.linalg.cho_solve((factor, True), matrix.T)


def incidence_matrix(pairs, count):
    dates = jnp.arange(-(-(2 * count - 256) // 128) * 128, dtype=jnp.int32)
    dates = jnp.where(dates < count, dates, jnp.where(dates < 2 * count - 256, dates - count + 256, -1))
    later = (pairs[:, 1:2] == dates[None, :]).astype(jnp.bfloat16)
    earlier = (pairs[:, 0:1] == dates[None, :]).astype(jnp.bfloat16)
    return later - earlier


def sums_kernel(row_count, ref_ref, send_ref, out_ref, acc_ref):
    blocks, rows, width = send_ref.shape
    ifg_count = rows // row_count
    cols = blocks * width
    first = lax.axis_index("tile") * row_count
    row = lax.broadcasted_iota(jnp.int32, (8, cols), 0) % row_count + first
    flat = row * cols + lax.broadcasted_iota(jnp.int32, (8, cols), 1)

    def count(i, weight):
        return weight + jnp.where(flat == ref_ref[i], 1.0, 0.0)

    weight = lax.fori_loop(
        0, ref_ref.shape[0], count, jnp.zeros((8, cols), jnp.float32), unroll=8
    )
    acc = jnp.zeros((rows // 8, 8, width), jnp.float32)
    for j in range(blocks):
        values = send_ref[j].astype(jnp.float32).reshape(rows // 8, 8, width)
        acc = acc + values * weight[None, :, j * width : (j + 1) * width]
    acc_ref[...] = acc.reshape(rows, width)
    per_ifg = acc_ref[pl.ds(0, ifg_count, stride=row_count), :]
    for r in range(1, row_count):
        per_ifg = per_ifg + acc_ref[pl.ds(r, ifg_count, stride=row_count), :]
    out_ref[...] = lax.dot_general(
        jnp.ones((8, width), jnp.float32),
        per_ifg,
        (((1,), (1,)), ((), ())),
        precision=lax.Precision.HIGHEST,
        preferred_element_type=jnp.float32,
    )


def partial_sums(ifgs, send, ref_pixels):
    ifg_count, row_count, cols = ifgs.shape
    if send.shape[1] % 16:
        tile = lax.axis_index("tile")
        pixel = jnp.arange(row_count * cols, dtype=jnp.int32) + tile * row_count * cols
        weight = jnp.sum((ref_pixels[:, None] == pixel[None, :]).astype(jnp.float32), axis=0)
        weight = weight.reshape(1, row_count, cols)
        return jnp.sum(ifgs.astype(jnp.float32) * weight, axis=(1, 2))
    sums = pl.pallas_call(
        functools.partial(sums_kernel, row_count),
        out_shape=jax.ShapeDtypeStruct((8, ifg_count), jnp.float32),
        in_specs=[SMEM, VMEM],
        out_specs=VMEM,
        scratch_shapes=[pltpu.VMEM(send.shape[1:], jnp.float32)],
        name="region_sums",
    )(ref_pixels, send)
    return sums[0]


def post_kernel(row_count, recv_ref, mean_ref, inverse_ref, incidence_ref, fit_ref,
                coeff_ref, spread_ref, wide_ref, corr_ref):
    pairs = incidence_ref.shape[0]
    width = recv_ref.shape[1]
    step = 128 if pairs % 128 == 0 else pairs
    for k in range(0, pairs, step):
        wide_ref[...] = recv_ref[row_count * k : row_count * (k + step), :].astype(jnp.float32)
        mean = mean_ref[k : k + step, :]
        for r in range(row_count):
            values = wide_ref[pl.ds(r, step, stride=row_count), :]
            corr_ref[k : k + step, r * width : (r + 1) * width] = (values - mean).astype(
                jnp.bfloat16
            )
    displacement = jnp.dot(
        inverse_ref[...], corr_ref[...], preferred_element_type=jnp.float32
    )
    spans = [(slice(k, k + step), slice(k, k + step)) for k in range(0, pairs, step)]
    finish(row_count, displacement, spans, incidence_ref, fit_ref, coeff_ref, spread_ref, corr_ref)


ANY = pl.BlockSpec(memory_space=pl.ANY)
PAD = 16
PLANES = 4
SPARE = 8
COST = 6_000_000_000
LANES = 128
SMALL = pltpu.CompilerParams(vmem_limit_bytes=16 * 1024 * 1024)


def pack_kernel(row_count, ref_hbm, ifgs_hbm, columns_hbm, blocks, share,
                refs, columns, weight_ref, in_sems, misc_sems):
    ifg_count, _, cols = ifgs_hbm.shape
    count, width = blocks.shape[0], blocks.shape[3]
    rest = columns.shape[1] - 2 * LANES
    ref_copy = pltpu.make_async_copy(ref_hbm, refs, misc_sems.at[0])
    ref_copy.start()
    ins = [
        pltpu.make_async_copy(
            ifgs_hbm.at[:, :, pl.ds(j * width, width)], blocks.at[j], in_sems.at[j]
        )
        for j in range(count)
    ]
    for copy in ins:
        copy.start()
    columns_copy = pltpu.make_async_copy(columns_hbm, columns, misc_sems.at[1])
    columns_copy.start()
    tile = lax.axis_index("tile")
    flat = lax.broadcasted_iota(jnp.int32, (8, cols), 1) + cols * (
        lax.broadcasted_iota(jnp.int32, (8, cols), 0) % row_count + tile * row_count
    )
    ref_copy.wait()
    weight = jnp.zeros((8, cols), jnp.float32)
    for i in range(refs.shape[0]):
        weight = weight + jnp.where(flat == refs[i], 1.0, 0.0)
    weight_ref[...] = weight
    columns_copy.wait()

    @pl.when(tile == 0)
    def _():
        share[:96, :] = columns[:96, :LANES]

    @pl.when(tile == 1)
    def _():
        share[:48, :] = columns[96:, :LANES]
        share[48:96, :] = columns[:48, LANES : 2 * LANES]

    @pl.when(tile == 2)
    def _():
        share[:96, :] = columns[48:, LANES : 2 * LANES]

    @pl.when(tile == 3)
    def _():
        left = columns[:80, 2 * LANES :].astype(jnp.float32)
        right = columns[80:, 2 * LANES :].astype(jnp.float32)
        left = jnp.pad(left, ((0, 16), (0, LANES // 2 - rest)))
        right = jnp.pad(right, ((0, 32), (0, LANES // 2 - rest)))
        share[:96, :] = jnp.concatenate([left, right], axis=1).astype(jnp.bfloat16)

    for copy in ins:
        copy.wait()
    flat_blocks = blocks.reshape(count, ifg_count * row_count, width)
    totals = 0.0
    for j in range(count):
        totals = totals + lax.dot_general(
            weight_ref[:, j * width : (j + 1) * width].astype(jnp.bfloat16),
            flat_blocks[j],
            (((1,), (1,)), ((), ())),
            preferred_element_type=jnp.float32,
        )
    row = lax.broadcasted_iota(jnp.int32, totals.shape, 0)
    lane = lax.broadcasted_iota(jnp.int32, totals.shape, 1)
    totals = jnp.sum(jnp.where(row == lane % row_count, totals, 0.0), axis=0, keepdims=True)
    totals = jnp.pad(totals, ((0, 0), (0, 3 * LANES - totals.shape[1])))
    high = totals.astype(jnp.bfloat16).astype(jnp.float32)
    middle = (totals - high).astype(jnp.bfloat16).astype(jnp.float32)
    terms = (high, middle, totals - high - middle)
    row = lax.broadcasted_iota(jnp.int32, (PAD, LANES), 0)
    under = jnp.zeros((PAD, LANES), jnp.float32)
    for t, term in enumerate(terms):
        for c in range(3):
            under = jnp.where(row == 3 * t + c, term[:, c * LANES : (c + 1) * LANES], under)
    share[96:, :] = under.astype(jnp.bfloat16)


def pack(ref_pixels, ifgs, columns, blocks):
    ifg_count, row_count, cols = ifgs.shape
    shape = (blocks, ifg_count, row_count, cols // blocks)
    return pl.pallas_call(
        functools.partial(pack_kernel, row_count),
        out_shape=(pltpu.VMEM(shape, jnp.bfloat16), pltpu.VMEM((96 + PAD, LANES), jnp.bfloat16)),
        in_specs=[ANY] * 3,
        out_specs=(VMEM, VMEM),
        scratch_shapes=[
            pltpu.SMEM(ref_pixels.shape, jnp.int32),
            pltpu.VMEM(columns.shape, jnp.bfloat16),
            pltpu.VMEM((8, cols), jnp.float32),
            pltpu.SemaphoreType.DMA((blocks,)),
            pltpu.SemaphoreType.DMA((2,)),
        ],
        name="pack",
    )(ref_pixels, ifgs, columns)


def fit_kernel(date_count, epochs_ref, fit_ref):
    terms, lanes = fit_ref.shape
    index = lax.broadcasted_iota(jnp.int32, (terms, lanes), 1)
    row = lax.broadcasted_iota(jnp.int32, (terms, lanes), 0)
    days = index.astype(jnp.float32)
    scaled = 2.0 * days / (date_count - 1) - 1.0
    years = days * 12.0 / 365.25
    smooth = [
        jnp.ones_like(days),
        scaled,
        scaled * scaled,
        scaled * scaled * scaled,
        jnp.sin(2.0 * math.pi * years),
        jnp.cos(2.0 * math.pi * years),
        jnp.sin(4.0 * math.pi * years),
        jnp.cos(4.0 * math.pi * years),
    ]
    matrix = jnp.zeros((terms, lanes), jnp.float32)
    for r, values in enumerate(smooth):
        matrix = jnp.where(row == r, values, matrix)
    for e in range(epochs_ref.shape[0]):
        step = jnp.where(index >= epochs_ref[e], 1.0, 0.0)
        matrix = jnp.where(row == len(smooth) + e, step, matrix)
    matrix = jnp.where(index < date_count, matrix, 0.0)
    normal = lax.dot_general(
        matrix,
        matrix,
        (((1,), (1,)), ((), ())),
        precision=lax.Precision.HIGHEST,
        preferred_element_type=jnp.float32,
    )
    place = lax.broadcasted_iota(jnp.int32, (terms, terms), 0)
    diagonal = place == lax.broadcasted_iota(jnp.int32, (terms, terms), 1)
    normal = normal + jnp.where(diagonal, RIDGE, 0.0)
    for j in range(terms):
        scale = 1.0 / normal[j : j + 1, j : j + 1]
        pivot, right = normal[j : j + 1, :] * scale, matrix[j : j + 1, :] * scale
        factor = normal[:, j : j + 1]
        normal = jnp.where(place == j, pivot, normal - factor * pivot)
        matrix = jnp.where(row == j, right, matrix - factor * right)
    fit_ref[...] = matrix


def prepare_kernel(row_count, region_size, *refs):
    *part_refs, operator_ref, mean_ref, all_ref, sums_ref = refs
    pairs, width = mean_ref.shape
    ifg, tile = lax.axis_index("ifg"), lax.axis_index("tile")
    blocks = 2 * PLANES
    ifg_count = pairs // blocks
    for position, part_ref in enumerate(part_refs):
        flip, away = position // 2, position % 2
        for m in range(PLANES):
            all_ref[tile ^ flip, ifg ^ (2 * m + away)] = part_ref[m]
    row = lax.broadcasted_iota(jnp.int32, (4 * PAD, 3 * width), 0) % PAD
    lane = lax.broadcasted_iota(jnp.int32, (4 * PAD, 3 * width), 1)
    select = jnp.where((row < 9) & (row % 3 == lane // width), 1.0, 0.0).astype(jnp.bfloat16)
    for block in range(blocks):
        top = block * ifg_count
        operator_ref[top : top + 96, :LANES] = all_ref[0, block, :96, :]
        operator_ref[top + 96 : top + 144, :LANES] = all_ref[1, block, :48, :]
        operator_ref[top : top + 48, LANES : 2 * LANES] = all_ref[1, block, 48:96, :]
        operator_ref[top + 48 : top + 144, LANES : 2 * LANES] = all_ref[2, block, :96, :]
        rest = all_ref[3, block, :80, :].astype(jnp.float32)
        blank = jnp.zeros((80, LANES // 2), jnp.float32)
        left = jnp.concatenate([rest[:, : LANES // 2], blank], axis=1)
        right = jnp.concatenate([rest[:, LANES // 2 :], blank], axis=1)
        operator_ref[top : top + 80, 2 * LANES :] = left.astype(jnp.bfloat16)
        operator_ref[top + 80 : top + 144, 2 * LANES :] = right[:64].astype(jnp.bfloat16)
        totals = lax.dot_general(
            jnp.concatenate([all_ref[t, block, 96:, :] for t in range(4)]),
            select,
            (((0,), (0,)), ((), ())),
            preferred_element_type=jnp.float32,
        )
        for c in range(3):
            top_row, count = c * LANES, min(LANES, row_count * ifg_count - c * LANES)
            sums_ref[top_row : top_row + count, :] = totals[:count, c * width : (c + 1) * width]
        total = sums_ref[pl.ds(0, ifg_count, stride=row_count), :]
        for r in range(1, row_count):
            total = total + sums_ref[pl.ds(r, ifg_count, stride=row_count), :]
        if region_size & (region_size - 1):
            mean_ref[top : top + ifg_count, :] = total / region_size
        else:
            mean_ref[top : top + ifg_count, :] = total * (1.0 / region_size)


def invert_kernel(row_count, dates, recv_ref, operator_ref, mean_ref, incidence_ref, fit_ref,
                  coeff_ref, spread_ref, wide_ref, corr_ref):
    blocks, rows, width = recv_ref.shape
    ifg_count = rows // row_count
    spans = []
    for block in range(blocks):
        span = slice(block * ifg_count, (block + 1) * ifg_count)
        spans.append((span, span))
        wide_ref[:rows, :] = recv_ref[block].astype(jnp.float32)
        mean = mean_ref[span, :]
        for r in range(row_count):
            values = wide_ref[pl.ds(r, ifg_count, stride=row_count), :]
            corr_ref[span, r * width : (r + 1) * width] = (values - mean).astype(jnp.bfloat16)
    displacement = lax.dot_general(
        operator_ref[:, :dates],
        corr_ref[...],
        (((0,), (0,)), ((), ())),
        preferred_element_type=jnp.float32,
    )
    finish(row_count, displacement, spans, incidence_ref, fit_ref, coeff_ref, spread_ref, corr_ref)


def finish(row_count, displacement, spans, incidence_ref, fit_ref, coeff_ref, spread_ref, corr_ref):
    pairs = incidence_ref.shape[0]
    width = corr_ref.shape[1] // row_count
    dates = displacement.shape[0]
    coeffs = jnp.dot(
        fit_ref[:, :dates],
        displacement,
        precision=lax.Precision.HIGHEST,
        preferred_element_type=jnp.float32,
    )
    high = displacement.astype(jnp.bfloat16)
    low = (displacement - high.astype(jnp.float32)).astype(jnp.bfloat16)
    blank = jnp.zeros((incidence_ref.shape[1] - 2 * dates + 256, high.shape[1]), jnp.bfloat16)
    rest = jnp.concatenate([high[256:], low[256:], blank])
    total = jnp.zeros((8, row_count * width), jnp.float32)
    for span, rows in spans:
        incidence = incidence_ref[span, :256]
        predicted = (
            jnp.dot(incidence, high[:256], preferred_element_type=jnp.float32)
            + jnp.dot(incidence, low[:256], preferred_element_type=jnp.float32)
            + jnp.dot(incidence_ref[span, 256:], rest, preferred_element_type=jnp.float32)
        )
        misfit = corr_ref[rows, :].astype(jnp.float32) - predicted
        total = total + jnp.sum((misfit * misfit).reshape(-1, 8, misfit.shape[1]), axis=0)
    spread = jnp.sqrt(jnp.sum(total, axis=0, keepdims=True) / pairs + EPS)
    for r in range(row_count):
        coeff_ref[:, r, :] = coeffs[:, r * width : (r + 1) * width]
        spread_ref[r : r + 1, :] = spread[:, r * width : (r + 1) * width]


def trade(array, bit):
    size = lax.axis_size("ifg")
    return lax.ppermute(array, "ifg", [(i, i ^ bit) for i in range(size)])


def trade_and_swap(array, bit, other):
    size, tiles = lax.axis_size("ifg"), lax.axis_size("tile")
    moves = [
        (i * tiles + t, (i ^ bit) * tiles + (t ^ other)) for i in range(size) for t in range(tiles)
    ]
    return lax.ppermute(array, ("ifg", "tile"), moves)


def small_slice(ifgs, pairs, pseudo_inverse, ref_pixels, epochs):
    ifg_count, row_count, cols = ifgs.shape
    blocks = lax.axis_size("ifg")
    width = cols // blocks
    date_count = pseudo_inverse.shape[0]
    pair_count = blocks * ifg_count
    lanes = 3 * LANES
    dates = -(-date_count // 16) * 16

    send, share = pack(ref_pixels, ifgs, pseudo_inverse.T, blocks)
    shares = [share] + [trade(share, 2 * m) for m in range(1, PLANES)]
    recv = lax.all_to_all(
        send.reshape(blocks, ifg_count * row_count, width), "ifg", 0, 0, tiled=True
    )
    own = jnp.stack(shares)
    own, pairs, epochs = lax.optimization_barrier((own, pairs, epochs))
    across = trade(own, 1)
    up = swap(own, 2)
    across_up = trade_and_swap(own, 1, 2)
    incidence = incidence_matrix(pairs, dates)
    terms = 8 + epochs.shape[0]
    fit = pl.pallas_call(
        functools.partial(fit_kernel, date_count),
        out_shape=pltpu.VMEM((terms, lanes), jnp.float32),
        in_specs=[SMEM],
        out_specs=VMEM,
        compiler_params=SMALL,
        name="fit",
    )(epochs)
    across, incidence, fit = lax.optimization_barrier((across, incidence, fit))
    parts = [own, across, swap(own, 1), swap(across, 1)]
    parts = parts + [up, across_up, swap(up, 1), swap(across_up, 1)]
    operator, means = pl.pallas_call(
        functools.partial(prepare_kernel, row_count, ref_pixels.shape[0]),
        out_shape=(
            pltpu.VMEM((pair_count, lanes), jnp.bfloat16),
            pltpu.VMEM((pair_count, width), jnp.float32),
        ),
        in_specs=[VMEM] * 8,
        out_specs=(VMEM, VMEM),
        scratch_shapes=[
            pltpu.VMEM((4, blocks) + share.shape, jnp.bfloat16),
            pltpu.VMEM((row_count * ifg_count + SPARE, width), jnp.float32),
        ],
        compiler_params=SMALL,
        cost_estimate=pl.CostEstimate(flops=COST, bytes_accessed=0, transcendentals=0),
        name="prepare",
    )(*parts)
    return pl.pallas_call(
        functools.partial(invert_kernel, row_count, dates),
        out_shape=(
            jax.ShapeDtypeStruct((terms, row_count, width), jnp.float32),
            jax.ShapeDtypeStruct((row_count, width), jnp.float32),
        ),
        in_specs=[VMEM] * 5,
        out_specs=(VMEM, VMEM),
        scratch_shapes=[
            pltpu.VMEM((row_count * ifg_count + SPARE, width), jnp.float32),
            pltpu.VMEM((pair_count, row_count * width), jnp.bfloat16),
        ],
        compiler_params=SMALL,
        name="invert",
    )(recv, operator, means, incidence, fit)


def swap(array, bit):
    size = lax.axis_size("tile")
    return lax.ppermute(array, "tile", [(i, i ^ bit) for i in range(size)])


def tile_gather(array):
    size = lax.axis_size("tile")
    tile = lax.axis_index("tile")
    parts = [array]
    bit = size // 2
    order = []
    while bit:
        parts = parts + [swap(part, bit) for part in parts]
        order.append(bit)
        bit //= 2
    stacked = jnp.stack(parts)
    offset = [0] * size
    for position in range(size):
        mask = 0
        for place, bit in enumerate(order):
            if position >> place & 1:
                mask |= bit
        offset[mask] = position
    stacked = jnp.stack([parts[offset[m]] for m in range(size)])
    for bit in order:
        swapped = stacked.reshape((size // (2 * bit), 2, bit) + array.shape)
        swapped = jnp.flip(swapped, axis=1).reshape(stacked.shape)
        stacked = jnp.where((tile & bit) != 0, swapped, stacked)
    return stacked


def split_sum(value):
    high = lax.reduce_precision(value, 8, 7)
    middle = lax.reduce_precision(value - high, 8, 7)
    low = lax.reduce_precision(value - high - middle, 8, 7)
    return jnp.stack([high, middle, low]).astype(jnp.bfloat16)


def shards(ifgs, pairs, pseudo_inverse, ref_pixels, epochs):
    ifg_count, row_count, cols = ifgs.shape
    blocks = lax.axis_size("ifg")
    tiles = lax.axis_size("tile")
    shape = (blocks, tiles, ifg_count, row_count, cols // blocks)
    dates = pseudo_inverse.shape[0]
    if shape == (2 * PLANES, 4, 144, 2, LANES) and 2 * LANES < dates <= 320:
        return small_slice(ifgs, pairs, pseudo_inverse, ref_pixels, epochs)
    width = cols // blocks
    date_count = pseudo_inverse.shape[0]
    pair_count = blocks * ifg_count
    dates = -(-date_count // 16) * 16
    tile = lax.axis_index("tile")

    send = ifgs.reshape(ifg_count, row_count, blocks, width).transpose(2, 0, 1, 3)
    send = send.reshape(blocks, ifg_count * row_count, width)

    share = -(-ifg_count // tiles)
    columns = jnp.pad(pseudo_inverse.T, ((0, share * tiles - ifg_count), (0, 0)))
    columns = lax.dynamic_slice_in_dim(columns, tile * share, share, 0)
    lanes = max(date_count, ifg_count)
    sums = split_sum(partial_sums(ifgs, send, ref_pixels))
    payload = jnp.concatenate(
        [
            jnp.pad(columns, ((0, 0), (0, lanes - date_count))),
            jnp.pad(sums, ((0, 0), (0, lanes - ifg_count))),
        ]
    )
    payload = jnp.broadcast_to(payload[None], (blocks,) + payload.shape)
    payload = lax.all_to_all(payload, "ifg", 0, 0, tiled=True)
    recv = lax.all_to_all(send, "ifg", 0, 0, tiled=True)
    gathered = tile_gather(payload)

    inverse = gathered[:, :, :share, :date_count].transpose(3, 1, 0, 2)
    inverse = inverse.reshape(date_count, blocks, tiles * share)[:, :, :ifg_count]
    inverse = jnp.pad(
        inverse.reshape(date_count, pair_count), ((0, dates - date_count), (0, 0))
    )
    totals = jnp.sum(gathered[:, :, share:, :ifg_count].astype(jnp.float32), axis=(0, 2))
    means = (totals / ref_pixels.shape[0]).reshape(pair_count, 1)
    means = jnp.broadcast_to(means, (pair_count, width))
    incidence = incidence_matrix(pairs, dates)
    fit = jnp.pad(fit_operator(epochs, date_count), ((0, 0), (0, dates - date_count)))

    terms = fit.shape[0]
    return pl.pallas_call(
        functools.partial(post_kernel, row_count),
        out_shape=(
            jax.ShapeDtypeStruct((terms, row_count, width), jnp.float32),
            jax.ShapeDtypeStruct((row_count, width), jnp.float32),
        ),
        in_specs=[VMEM] * 5,
        out_specs=(VMEM, VMEM),
        scratch_shapes=[
            pltpu.VMEM(
                (row_count * (128 if pair_count % 128 == 0 else pair_count), width), jnp.float32
            ),
            pltpu.VMEM((pair_count, row_count * width), jnp.bfloat16),
        ],
        compiler_params=pltpu.CompilerParams(vmem_limit_bytes=32 * 1024 * 1024),
        name="invert",
    )(recv.reshape(pair_count * row_count, width), means, inverse, incidence, fit)


def solution(mesh):
    in_specs = (P("ifg", "tile", None), P(), P(None, "ifg"), P(), P())
    out_specs = (P(None, "tile", "ifg"), P("tile", "ifg"))
    return jax.shard_map(shards, mesh=mesh, in_specs=in_specs, out_specs=out_specs, check_vma=False)
```

```python
import functools
import math

import jax
import jax.numpy as jnp
from jax import lax
from jax.experimental import pallas as pl
from jax.experimental.pallas import tpu as pltpu
from jax.sharding import PartitionSpec as P

EPS = 1e-06
RIDGE = 1.0
VMEM = pl.BlockSpec(memory_space=pltpu.VMEM)
SMEM = pl.BlockSpec(memory_space=pltpu.SMEM)


def design(epochs, count):
    index = jnp.arange(count, dtype=jnp.int32)
    days = index.astype(jnp.float32)
    scaled = 2.0 * days / (count - 1) - 1.0
    years = days * 12.0 / 365.25
    smooth = jnp.stack(
        [
            jnp.ones_like(days),
            scaled,
            scaled * scaled,
            scaled * scaled * scaled,
            jnp.sin(2.0 * math.pi * years),
            jnp.cos(2.0 * math.pi * years),
            jnp.sin(4.0 * math.pi * years),
            jnp.cos(4.0 * math.pi * years),
        ],
        axis=1,
    )
    jumps = (index[:, None] >= epochs[None, :]).astype(jnp.float32)
    return jnp.concatenate([smooth, jumps], axis=1)


def fit_operator(epochs, count):
    matrix = design(epochs, count)
    normal = jnp.dot(
        matrix.T, matrix, precision=lax.Precision.HIGHEST, preferred_element_type=jnp.float32
    )
    normal = normal + RIDGE * jnp.eye(matrix.shape[1], dtype=jnp.float32)
    factor = jnp.linalg.cholesky(normal)
    return jax.scipy.linalg.cho_solve((factor, True), matrix.T)


def incidence_matrix(pairs, count):
    dates = jnp.arange(-(-(2 * count - 256) // 128) * 128, dtype=jnp.int32)
    dates = jnp.where(dates < count, dates, jnp.where(dates < 2 * count - 256, dates - count + 256, -1))
    later = (pairs[:, 1:2] == dates[None, :]).astype(jnp.bfloat16)
    earlier = (pairs[:, 0:1] == dates[None, :]).astype(jnp.bfloat16)
    return later - earlier


def sums_kernel(row_count, ref_ref, send_ref, out_ref, acc_ref):
    blocks, rows, width = send_ref.shape
    ifg_count = rows // row_count
    cols = blocks * width
    first = lax.axis_index("tile") * row_count
    row = lax.broadcasted_iota(jnp.int32, (8, cols), 0) % row_count + first
    flat = row * cols + lax.broadcasted_iota(jnp.int32, (8, cols), 1)

    def count(i, weight):
        return weight + jnp.where(flat == ref_ref[i], 1.0, 0.0)

    weight = lax.fori_loop(
        0, ref_ref.shape[0], count, jnp.zeros((8, cols), jnp.float32), unroll=8
    )
    acc = jnp.zeros((rows // 8, 8, width), jnp.float32)
    for j in range(blocks):
        values = send_ref[j].astype(jnp.float32).reshape(rows // 8, 8, width)
        acc = acc + values * weight[None, :, j * width : (j + 1) * width]
    acc_ref[...] = acc.reshape(rows, width)
    per_ifg = acc_ref[pl.ds(0, ifg_count, stride=row_count), :]
    for r in range(1, row_count):
        per_ifg = per_ifg + acc_ref[pl.ds(r, ifg_count, stride=row_count), :]
    out_ref[...] = lax.dot_general(
        jnp.ones((8, width), jnp.float32),
        per_ifg,
        (((1,), (1,)), ((), ())),
        precision=lax.Precision.HIGHEST,
        preferred_element_type=jnp.float32,
    )


def partial_sums(ifgs, send, ref_pixels):
    ifg_count, row_count, cols = ifgs.shape
    if send.shape[1] % 16:
        tile = lax.axis_index("tile")
        pixel = jnp.arange(row_count * cols, dtype=jnp.int32) + tile * row_count * cols
        weight = jnp.sum((ref_pixels[:, None] == pixel[None, :]).astype(jnp.float32), axis=0)
        weight = weight.reshape(1, row_count, cols)
        return jnp.sum(ifgs.astype(jnp.float32) * weight, axis=(1, 2))
    sums = pl.pallas_call(
        functools.partial(sums_kernel, row_count),
        out_shape=jax.ShapeDtypeStruct((8, ifg_count), jnp.float32),
        in_specs=[SMEM, VMEM],
        out_specs=VMEM,
        scratch_shapes=[pltpu.VMEM(send.shape[1:], jnp.float32)],
        name="region_sums",
    )(ref_pixels, send)
    return sums[0]


def post_kernel(row_count, recv_ref, mean_ref, inverse_ref, incidence_ref, fit_ref,
                coeff_ref, spread_ref, wide_ref, corr_ref):
    pairs = incidence_ref.shape[0]
    width = recv_ref.shape[1]
    step = 128 if pairs % 128 == 0 else pairs
    for k in range(0, pairs, step):
        wide_ref[...] = recv_ref[row_count * k : row_count * (k + step), :].astype(jnp.float32)
        mean = mean_ref[k : k + step, :]
        for r in range(row_count):
            values = wide_ref[pl.ds(r, step, stride=row_count), :]
            corr_ref[k : k + step, r * width : (r + 1) * width] = (values - mean).astype(
                jnp.bfloat16
            )
    displacement = jnp.dot(
        inverse_ref[...], corr_ref[...], preferred_element_type=jnp.float32
    )
    spans = [(slice(k, k + step), slice(k, k + step)) for k in range(0, pairs, step)]
    finish(row_count, displacement, spans, incidence_ref, fit_ref, coeff_ref, spread_ref, corr_ref)


ANY = pl.BlockSpec(memory_space=pl.ANY)
PAD = 16
PLANES = 4
SPARE = 8
COST = 6_000_000_000
LANES = 128
SMALL = pltpu.CompilerParams(vmem_limit_bytes=16 * 1024 * 1024)


def pack_kernel(row_count, ref_hbm, ifgs_hbm, columns_hbm, blocks, share,
                refs, columns, weight_ref, in_sems, misc_sems):
    ifg_count, _, cols = ifgs_hbm.shape
    count, width = blocks.shape[0], blocks.shape[3]
    rest = columns.shape[1] - 2 * LANES
    ref_copy = pltpu.make_async_copy(ref_hbm, refs, misc_sems.at[0])
    ref_copy.start()
    ins = [
        pltpu.make_async_copy(
            ifgs_hbm.at[:, :, pl.ds(j * width, width)], blocks.at[j], in_sems.at[j]
        )
        for j in range(count)
    ]
    for copy in ins:
        copy.start()
    columns_copy = pltpu.make_async_copy(columns_hbm, columns, misc_sems.at[1])
    columns_copy.start()
    tile = lax.axis_index("tile")
    flat = lax.broadcasted_iota(jnp.int32, (8, cols), 1) + cols * (
        lax.broadcasted_iota(jnp.int32, (8, cols), 0) % row_count + tile * row_count
    )
    ref_copy.wait()
    weight = jnp.zeros((8, cols), jnp.float32)
    for i in range(refs.shape[0]):
        weight = weight + jnp.where(flat == refs[i], 1.0, 0.0)
    weight_ref[...] = weight
    columns_copy.wait()

    @pl.when(tile == 0)
    def _():
        share[:96, :] = columns[:96, :LANES]

    @pl.when(tile == 1)
    def _():
        share[:48, :] = columns[96:, :LANES]
        share[48:96, :] = columns[:48, LANES : 2 * LANES]

    @pl.when(tile == 2)
    def _():
        share[:96, :] = columns[48:, LANES : 2 * LANES]

    @pl.when(tile == 3)
    def _():
        left = columns[:80, 2 * LANES :].astype(jnp.float32)
        right = columns[80:, 2 * LANES :].astype(jnp.float32)
        left = jnp.pad(left, ((0, 16), (0, LANES // 2 - rest)))
        right = jnp.pad(right, ((0, 32), (0, LANES // 2 - rest)))
        share[:96, :] = jnp.concatenate([left, right], axis=1).astype(jnp.bfloat16)

    for copy in ins:
        copy.wait()
    flat_blocks = blocks.reshape(count, ifg_count * row_count, width)
    totals = 0.0
    for j in range(count):
        totals = totals + lax.dot_general(
            weight_ref[:, j * width : (j + 1) * width].astype(jnp.bfloat16),
            flat_blocks[j],
            (((1,), (1,)), ((), ())),
            preferred_element_type=jnp.float32,
        )
    row = lax.broadcasted_iota(jnp.int32, totals.shape, 0)
    lane = lax.broadcasted_iota(jnp.int32, totals.shape, 1)
    totals = jnp.sum(jnp.where(row == lane % row_count, totals, 0.0), axis=0, keepdims=True)
    totals = jnp.pad(totals, ((0, 0), (0, 3 * LANES - totals.shape[1])))
    high = totals.astype(jnp.bfloat16).astype(jnp.float32)
    middle = (totals - high).astype(jnp.bfloat16).astype(jnp.float32)
    terms = (high, middle, totals - high - middle)
    row = lax.broadcasted_iota(jnp.int32, (PAD, LANES), 0)
    under = jnp.zeros((PAD, LANES), jnp.float32)
    for t, term in enumerate(terms):
        for c in range(3):
            under = jnp.where(row == 3 * t + c, term[:, c * LANES : (c + 1) * LANES], under)
    share[96:, :] = under.astype(jnp.bfloat16)


def pack(ref_pixels, ifgs, columns, blocks):
    ifg_count, row_count, cols = ifgs.shape
    shape = (blocks, ifg_count, row_count, cols // blocks)
    return pl.pallas_call(
        functools.partial(pack_kernel, row_count),
        out_shape=(pltpu.VMEM(shape, jnp.bfloat16), pltpu.VMEM((96 + PAD, LANES), jnp.bfloat16)),
        in_specs=[ANY] * 3,
        out_specs=(VMEM, VMEM),
        scratch_shapes=[
            pltpu.SMEM(ref_pixels.shape, jnp.int32),
            pltpu.VMEM(columns.shape, jnp.bfloat16),
            pltpu.VMEM((8, cols), jnp.float32),
            pltpu.SemaphoreType.DMA((blocks,)),
            pltpu.SemaphoreType.DMA((2,)),
        ],
        name="pack",
    )(ref_pixels, ifgs, columns)


def fit_kernel(date_count, epochs_ref, fit_ref):
    terms, lanes = fit_ref.shape
    index = lax.broadcasted_iota(jnp.int32, (terms, lanes), 1)
    row = lax.broadcasted_iota(jnp.int32, (terms, lanes), 0)
    days = index.astype(jnp.float32)
    scaled = 2.0 * days / (date_count - 1) - 1.0
    years = days * 12.0 / 365.25
    smooth = [
        jnp.ones_like(days),
        scaled,
        scaled * scaled,
        scaled * scaled * scaled,
        jnp.sin(2.0 * math.pi * years),
        jnp.cos(2.0 * math.pi * years),
        jnp.sin(4.0 * math.pi * years),
        jnp.cos(4.0 * math.pi * years),
    ]
    matrix = jnp.zeros((terms, lanes), jnp.float32)
    for r, values in enumerate(smooth):
        matrix = jnp.where(row == r, values, matrix)
    for e in range(epochs_ref.shape[0]):
        step = jnp.where(index >= epochs_ref[e], 1.0, 0.0)
        matrix = jnp.where(row == len(smooth) + e, step, matrix)
    matrix = jnp.where(index < date_count, matrix, 0.0)
    normal = lax.dot_general(
        matrix,
        matrix,
        (((1,), (1,)), ((), ())),
        precision=lax.Precision.HIGHEST,
        preferred_element_type=jnp.float32,
    )
    place = lax.broadcasted_iota(jnp.int32, (terms, terms), 0)
    diagonal = place == lax.broadcasted_iota(jnp.int32, (terms, terms), 1)
    normal = normal + jnp.where(diagonal, RIDGE, 0.0)
    for j in range(terms):
        scale = 1.0 / normal[j : j + 1, j : j + 1]
        pivot, right = normal[j : j + 1, :] * scale, matrix[j : j + 1, :] * scale
        factor = normal[:, j : j + 1]
        normal = jnp.where(place == j, pivot, normal - factor * pivot)
        matrix = jnp.where(row == j, right, matrix - factor * right)
    fit_ref[...] = matrix


def prepare_kernel(row_count, region_size, *refs):
    *part_refs, operator_ref, mean_ref, all_ref, sums_ref = refs
    pairs, width = mean_ref.shape
    ifg, tile = lax.axis_index("ifg"), lax.axis_index("tile")
    blocks = 2 * PLANES
    ifg_count = pairs // blocks
    for position, part_ref in enumerate(part_refs):
        flip, away = position // 2, position % 2
        holder = tile ^ flip
        far = PLANES - 1 - holder % 2
        for slot, (plane, other) in enumerate(((0, 0), (1, 0), (far, 0), (far, 1))):
            all_ref[holder ^ other, ifg ^ (2 * plane + away)] = part_ref[slot]
    row = lax.broadcasted_iota(jnp.int32, (4 * PAD, 3 * width), 0) % PAD
    lane = lax.broadcasted_iota(jnp.int32, (4 * PAD, 3 * width), 1)
    select = jnp.where((row < 9) & (row % 3 == lane // width), 1.0, 0.0).astype(jnp.bfloat16)
    for block in range(blocks):
        top = block * ifg_count
        operator_ref[top : top + 96, :LANES] = all_ref[0, block, :96, :]
        operator_ref[top + 96 : top + 144, :LANES] = all_ref[1, block, :48, :]
        operator_ref[top : top + 48, LANES : 2 * LANES] = all_ref[1, block, 48:96, :]
        operator_ref[top + 48 : top + 144, LANES : 2 * LANES] = all_ref[2, block, :96, :]
        rest = all_ref[3, block, :80, :].astype(jnp.float32)
        blank = jnp.zeros((80, LANES // 2), jnp.float32)
        left = jnp.concatenate([rest[:, : LANES // 2], blank], axis=1)
        right = jnp.concatenate([rest[:, LANES // 2 :], blank], axis=1)
        operator_ref[top : top + 80, 2 * LANES :] = left.astype(jnp.bfloat16)
        operator_ref[top + 80 : top + 144, 2 * LANES :] = right[:64].astype(jnp.bfloat16)
        totals = lax.dot_general(
            jnp.concatenate([all_ref[t, block, 96:, :] for t in range(4)]),
            select,
            (((0,), (0,)), ((), ())),
            preferred_element_type=jnp.float32,
        )
        for c in range(3):
            top_row, count = c * LANES, min(LANES, row_count * ifg_count - c * LANES)
            sums_ref[top_row : top_row + count, :] = totals[:count, c * width : (c + 1) * width]
        total = sums_ref[pl.ds(0, ifg_count, stride=row_count), :]
        for r in range(1, row_count):
            total = total + sums_ref[pl.ds(r, ifg_count, stride=row_count), :]
        if region_size & (region_size - 1):
            mean_ref[top : top + ifg_count, :] = total / region_size
        else:
            mean_ref[top : top + ifg_count, :] = total * (1.0 / region_size)


def invert_kernel(row_count, dates, recv_ref, operator_ref, mean_ref, incidence_ref, fit_ref,
                  coeff_ref, spread_ref, wide_ref, corr_ref):
    blocks, rows, width = recv_ref.shape
    ifg_count = rows // row_count
    spans = []
    for block in range(blocks):
        span = slice(block * ifg_count, (block + 1) * ifg_count)
        spans.append((span, span))
        wide_ref[:rows, :] = recv_ref[block].astype(jnp.float32)
        mean = mean_ref[span, :]
        for r in range(row_count):
            values = wide_ref[pl.ds(r, ifg_count, stride=row_count), :]
            corr_ref[span, r * width : (r + 1) * width] = (values - mean).astype(jnp.bfloat16)
    displacement = lax.dot_general(
        operator_ref[:, :dates],
        corr_ref[...],
        (((0,), (0,)), ((), ())),
        preferred_element_type=jnp.float32,
    )
    finish(row_count, displacement, spans, incidence_ref, fit_ref, coeff_ref, spread_ref, corr_ref)


def finish(row_count, displacement, spans, incidence_ref, fit_ref, coeff_ref, spread_ref, corr_ref):
    pairs = incidence_ref.shape[0]
    width = corr_ref.shape[1] // row_count
    dates = displacement.shape[0]
    coeffs = jnp.dot(
        fit_ref[:, :dates],
        displacement,
        precision=lax.Precision.HIGHEST,
        preferred_element_type=jnp.float32,
    )
    high = displacement.astype(jnp.bfloat16)
    low = (displacement - high.astype(jnp.float32)).astype(jnp.bfloat16)
    blank = jnp.zeros((incidence_ref.shape[1] - 2 * dates + 256, high.shape[1]), jnp.bfloat16)
    rest = jnp.concatenate([high[256:], low[256:], blank])
    total = jnp.zeros((8, row_count * width), jnp.float32)
    for span, rows in spans:
        incidence = incidence_ref[span, :256]
        predicted = (
            jnp.dot(incidence, high[:256], preferred_element_type=jnp.float32)
            + jnp.dot(incidence, low[:256], preferred_element_type=jnp.float32)
            + jnp.dot(incidence_ref[span, 256:], rest, preferred_element_type=jnp.float32)
        )
        misfit = corr_ref[rows, :].astype(jnp.float32) - predicted
        total = total + jnp.sum((misfit * misfit).reshape(-1, 8, misfit.shape[1]), axis=0)
    spread = jnp.sqrt(jnp.sum(total, axis=0, keepdims=True) / pairs + EPS)
    for r in range(row_count):
        coeff_ref[:, r, :] = coeffs[:, r * width : (r + 1) * width]
        spread_ref[r : r + 1, :] = spread[:, r * width : (r + 1) * width]


def trade(array, bit):
    size = lax.axis_size("ifg")
    return lax.ppermute(array, "ifg", [(i, i ^ bit) for i in range(size)])


def trade_and_swap(array, bit, other):
    size, tiles = lax.axis_size("ifg"), lax.axis_size("tile")
    moves = [
        (i * tiles + t, (i ^ bit) * tiles + (t ^ other)) for i in range(size) for t in range(tiles)
    ]
    return lax.ppermute(array, ("ifg", "tile"), moves)


def small_slice(ifgs, pairs, pseudo_inverse, ref_pixels, epochs):
    ifg_count, row_count, cols = ifgs.shape
    blocks = lax.axis_size("ifg")
    width = cols // blocks
    date_count = pseudo_inverse.shape[0]
    pair_count = blocks * ifg_count
    lanes = 3 * LANES
    dates = -(-date_count // 16) * 16

    send, share = pack(ref_pixels, ifgs, pseudo_inverse.T, blocks)
    pair = jnp.stack([share, swap(share, 1)])
    send, pair = lax.optimization_barrier((send, pair))
    tiles = lax.axis_size("tile")
    far = [
        (i * tiles + t, (i ^ (2 * (PLANES - 1 - t % 2))) * tiles + t)
        for i in range(blocks)
        for t in range(tiles)
    ]
    far = lax.ppermute(pair, ("ifg", "tile"), far)
    near = trade(pair[0], 2)
    recv = lax.all_to_all(
        send.reshape(blocks, ifg_count * row_count, width), "ifg", 0, 0, tiled=True
    )
    own = jnp.stack([share, near, far[0], far[1]])
    own, pairs, epochs = lax.optimization_barrier((own, pairs, epochs))
    across = trade(own, 1)
    up = swap(own, 2)
    across_up = trade_and_swap(own, 1, 2)
    incidence = incidence_matrix(pairs, dates)
    terms = 8 + epochs.shape[0]
    fit = pl.pallas_call(
        functools.partial(fit_kernel, date_count),
        out_shape=pltpu.VMEM((terms, lanes), jnp.float32),
        in_specs=[SMEM],
        out_specs=VMEM,
        compiler_params=SMALL,
        name="fit",
    )(epochs)
    across, incidence, fit = lax.optimization_barrier((across, incidence, fit))
    parts = [own, across, swap(own, 1), swap(across, 1)]
    parts = parts + [up, across_up, swap(up, 1), swap(across_up, 1)]
    operator, means = pl.pallas_call(
        functools.partial(prepare_kernel, row_count, ref_pixels.shape[0]),
        out_shape=(
            pltpu.VMEM((pair_count, lanes), jnp.bfloat16),
            pltpu.VMEM((pair_count, width), jnp.float32),
        ),
        in_specs=[VMEM] * 8,
        out_specs=(VMEM, VMEM),
        scratch_shapes=[
            pltpu.VMEM((4, blocks) + share.shape, jnp.bfloat16),
            pltpu.VMEM((row_count * ifg_count + SPARE, width), jnp.float32),
        ],
        compiler_params=SMALL,
        cost_estimate=pl.CostEstimate(flops=COST, bytes_accessed=0, transcendentals=0),
        name="prepare",
    )(*parts)
    return pl.pallas_call(
        functools.partial(invert_kernel, row_count, dates),
        out_shape=(
            jax.ShapeDtypeStruct((terms, row_count, width), jnp.float32),
            jax.ShapeDtypeStruct((row_count, width), jnp.float32),
        ),
        in_specs=[VMEM] * 5,
        out_specs=(VMEM, VMEM),
        scratch_shapes=[
            pltpu.VMEM((row_count * ifg_count + SPARE, width), jnp.float32),
            pltpu.VMEM((pair_count, row_count * width), jnp.bfloat16),
        ],
        compiler_params=SMALL,
        name="invert",
    )(recv, operator, means, incidence, fit)


def swap(array, bit):
    size = lax.axis_size("tile")
    return lax.ppermute(array, "tile", [(i, i ^ bit) for i in range(size)])


def tile_gather(array):
    size = lax.axis_size("tile")
    tile = lax.axis_index("tile")
    parts = [array]
    bit = size // 2
    order = []
    while bit:
        parts = parts + [swap(part, bit) for part in parts]
        order.append(bit)
        bit //= 2
    stacked = jnp.stack(parts)
    offset = [0] * size
    for position in range(size):
        mask = 0
        for place, bit in enumerate(order):
            if position >> place & 1:
                mask |= bit
        offset[mask] = position
    stacked = jnp.stack([parts[offset[m]] for m in range(size)])
    for bit in order:
        swapped = stacked.reshape((size // (2 * bit), 2, bit) + array.shape)
        swapped = jnp.flip(swapped, axis=1).reshape(stacked.shape)
        stacked = jnp.where((tile & bit) != 0, swapped, stacked)
    return stacked


def split_sum(value):
    high = lax.reduce_precision(value, 8, 7)
    middle = lax.reduce_precision(value - high, 8, 7)
    low = lax.reduce_precision(value - high - middle, 8, 7)
    return jnp.stack([high, middle, low]).astype(jnp.bfloat16)


def shards(ifgs, pairs, pseudo_inverse, ref_pixels, epochs):
    ifg_count, row_count, cols = ifgs.shape
    blocks = lax.axis_size("ifg")
    tiles = lax.axis_size("tile")
    shape = (blocks, tiles, ifg_count, row_count, cols // blocks)
    dates = pseudo_inverse.shape[0]
    if shape == (2 * PLANES, 4, 144, 2, LANES) and 2 * LANES < dates <= 320:
        return small_slice(ifgs, pairs, pseudo_inverse, ref_pixels, epochs)
    width = cols // blocks
    date_count = pseudo_inverse.shape[0]
    pair_count = blocks * ifg_count
    dates = -(-date_count // 16) * 16
    tile = lax.axis_index("tile")

    send = ifgs.reshape(ifg_count, row_count, blocks, width).transpose(2, 0, 1, 3)
    send = send.reshape(blocks, ifg_count * row_count, width)

    share = -(-ifg_count // tiles)
    columns = jnp.pad(pseudo_inverse.T, ((0, share * tiles - ifg_count), (0, 0)))
    columns = lax.dynamic_slice_in_dim(columns, tile * share, share, 0)
    lanes = max(date_count, ifg_count)
    sums = split_sum(partial_sums(ifgs, send, ref_pixels))
    payload = jnp.concatenate(
        [
            jnp.pad(columns, ((0, 0), (0, lanes - date_count))),
            jnp.pad(sums, ((0, 0), (0, lanes - ifg_count))),
        ]
    )
    payload = jnp.broadcast_to(payload[None], (blocks,) + payload.shape)
    payload = lax.all_to_all(payload, "ifg", 0, 0, tiled=True)
    recv = lax.all_to_all(send, "ifg", 0, 0, tiled=True)
    gathered = tile_gather(payload)

    inverse = gathered[:, :, :share, :date_count].transpose(3, 1, 0, 2)
    inverse = inverse.reshape(date_count, blocks, tiles * share)[:, :, :ifg_count]
    inverse = jnp.pad(
        inverse.reshape(date_count, pair_count), ((0, dates - date_count), (0, 0))
    )
    totals = jnp.sum(gathered[:, :, share:, :ifg_count].astype(jnp.float32), axis=(0, 2))
    means = (totals / ref_pixels.shape[0]).reshape(pair_count, 1)
    means = jnp.broadcast_to(means, (pair_count, width))
    incidence = incidence_matrix(pairs, dates)
    fit = jnp.pad(fit_operator(epochs, date_count), ((0, 0), (0, dates - date_count)))

    terms = fit.shape[0]
    return pl.pallas_call(
        functools.partial(post_kernel, row_count),
        out_shape=(
            jax.ShapeDtypeStruct((terms, row_count, width), jnp.float32),
            jax.ShapeDtypeStruct((row_count, width), jnp.float32),
        ),
        in_specs=[VMEM] * 5,
        out_specs=(VMEM, VMEM),
        scratch_shapes=[
            pltpu.VMEM(
                (row_count * (128 if pair_count % 128 == 0 else pair_count), width), jnp.float32
            ),
            pltpu.VMEM((pair_count, row_count * width), jnp.bfloat16),
        ],
        compiler_params=pltpu.CompilerParams(vmem_limit_bytes=32 * 1024 * 1024),
        name="invert",
    )(recv.reshape(pair_count * row_count, width), means, inverse, incidence, fit)


def solution(mesh):
    in_specs = (P("ifg", "tile", None), P(), P(None, "ifg"), P(), P())
    out_specs = (P(None, "tile", "ifg"), P("tile", "ifg"))
    return jax.shard_map(shards, mesh=mesh, in_specs=in_specs, out_specs=out_specs, check_vma=False)
```

```python
import functools
import math

import jax
import jax.numpy as jnp
from jax import lax
from jax.experimental import pallas as pl
from jax.experimental.pallas import tpu as pltpu
from jax.sharding import PartitionSpec as P

EPS = 1e-06
RIDGE = 1.0
VMEM = pl.BlockSpec(memory_space=pltpu.VMEM)
SMEM = pl.BlockSpec(memory_space=pltpu.SMEM)


def design(epochs, count):
    index = jnp.arange(count, dtype=jnp.int32)
    days = index.astype(jnp.float32)
    scaled = 2.0 * days / (count - 1) - 1.0
    years = days * 12.0 / 365.25
    smooth = jnp.stack(
        [
            jnp.ones_like(days),
            scaled,
            scaled * scaled,
            scaled * scaled * scaled,
            jnp.sin(2.0 * math.pi * years),
            jnp.cos(2.0 * math.pi * years),
            jnp.sin(4.0 * math.pi * years),
            jnp.cos(4.0 * math.pi * years),
        ],
        axis=1,
    )
    jumps = (index[:, None] >= epochs[None, :]).astype(jnp.float32)
    return jnp.concatenate([smooth, jumps], axis=1)


def fit_operator(epochs, count):
    matrix = design(epochs, count)
    normal = jnp.dot(
        matrix.T, matrix, precision=lax.Precision.HIGHEST, preferred_element_type=jnp.float32
    )
    normal = normal + RIDGE * jnp.eye(matrix.shape[1], dtype=jnp.float32)
    factor = jnp.linalg.cholesky(normal)
    return jax.scipy.linalg.cho_solve((factor, True), matrix.T)


def incidence_matrix(pairs, count):
    dates = jnp.arange(-(-(2 * count - 256) // 128) * 128, dtype=jnp.int32)
    dates = jnp.where(dates < count, dates, jnp.where(dates < 2 * count - 256, dates - count + 256, -1))
    later = (pairs[:, 1:2] == dates[None, :]).astype(jnp.bfloat16)
    earlier = (pairs[:, 0:1] == dates[None, :]).astype(jnp.bfloat16)
    return later - earlier


def sums_kernel(row_count, ref_ref, send_ref, out_ref, acc_ref):
    blocks, rows, width = send_ref.shape
    ifg_count = rows // row_count
    cols = blocks * width
    first = lax.axis_index("tile") * row_count
    row = lax.broadcasted_iota(jnp.int32, (8, cols), 0) % row_count + first
    flat = row * cols + lax.broadcasted_iota(jnp.int32, (8, cols), 1)

    def count(i, weight):
        return weight + jnp.where(flat == ref_ref[i], 1.0, 0.0)

    weight = lax.fori_loop(
        0, ref_ref.shape[0], count, jnp.zeros((8, cols), jnp.float32), unroll=8
    )
    acc = jnp.zeros((rows // 8, 8, width), jnp.float32)
    for j in range(blocks):
        values = send_ref[j].astype(jnp.float32).reshape(rows // 8, 8, width)
        acc = acc + values * weight[None, :, j * width : (j + 1) * width]
    acc_ref[...] = acc.reshape(rows, width)
    per_ifg = acc_ref[pl.ds(0, ifg_count, stride=row_count), :]
    for r in range(1, row_count):
        per_ifg = per_ifg + acc_ref[pl.ds(r, ifg_count, stride=row_count), :]
    out_ref[...] = lax.dot_general(
        jnp.ones((8, width), jnp.float32),
        per_ifg,
        (((1,), (1,)), ((), ())),
        precision=lax.Precision.HIGHEST,
        preferred_element_type=jnp.float32,
    )


def partial_sums(ifgs, send, ref_pixels):
    ifg_count, row_count, cols = ifgs.shape
    if send.shape[1] % 16:
        tile = lax.axis_index("tile")
        pixel = jnp.arange(row_count * cols, dtype=jnp.int32) + tile * row_count * cols
        weight = jnp.sum((ref_pixels[:, None] == pixel[None, :]).astype(jnp.float32), axis=0)
        weight = weight.reshape(1, row_count, cols)
        return jnp.sum(ifgs.astype(jnp.float32) * weight, axis=(1, 2))
    sums = pl.pallas_call(
        functools.partial(sums_kernel, row_count),
        out_shape=jax.ShapeDtypeStruct((8, ifg_count), jnp.float32),
        in_specs=[SMEM, VMEM],
        out_specs=VMEM,
        scratch_shapes=[pltpu.VMEM(send.shape[1:], jnp.float32)],
        name="region_sums",
    )(ref_pixels, send)
    return sums[0]


def post_kernel(row_count, recv_ref, mean_ref, inverse_ref, incidence_ref, fit_ref,
                coeff_ref, spread_ref, wide_ref, corr_ref):
    pairs = incidence_ref.shape[0]
    width = recv_ref.shape[1]
    step = 128 if pairs % 128 == 0 else pairs
    for k in range(0, pairs, step):
        wide_ref[...] = recv_ref[row_count * k : row_count * (k + step), :].astype(jnp.float32)
        mean = mean_ref[k : k + step, :]
        for r in range(row_count):
            values = wide_ref[pl.ds(r, step, stride=row_count), :]
            corr_ref[k : k + step, r * width : (r + 1) * width] = (values - mean).astype(
                jnp.bfloat16
            )
    displacement = jnp.dot(
        inverse_ref[...], corr_ref[...], preferred_element_type=jnp.float32
    )
    spans = [(slice(k, k + step), slice(k, k + step)) for k in range(0, pairs, step)]
    finish(row_count, displacement, spans, incidence_ref, fit_ref, coeff_ref, spread_ref, corr_ref)


ANY = pl.BlockSpec(memory_space=pl.ANY)
PAD = 16
PLANES = 4
SPARE = 8
COST = 6_000_000_000
LANES = 128
SMALL = pltpu.CompilerParams(vmem_limit_bytes=16 * 1024 * 1024)


def pack_kernel(row_count, ref_hbm, ifgs_hbm, columns_hbm, blocks, share,
                refs, columns, weight_ref, in_sems, misc_sems):
    ifg_count, _, cols = ifgs_hbm.shape
    count, width = blocks.shape[0], blocks.shape[3]
    rest = columns.shape[1] - 2 * LANES
    ref_copy = pltpu.make_async_copy(ref_hbm, refs, misc_sems.at[0])
    ref_copy.start()
    ins = [
        pltpu.make_async_copy(
            ifgs_hbm.at[:, :, pl.ds(j * width, width)], blocks.at[j], in_sems.at[j]
        )
        for j in range(count)
    ]
    for copy in ins:
        copy.start()
    columns_copy = pltpu.make_async_copy(columns_hbm, columns, misc_sems.at[1])
    columns_copy.start()
    tile = lax.axis_index("tile")
    flat = lax.broadcasted_iota(jnp.int32, (8, cols), 1) + cols * (
        lax.broadcasted_iota(jnp.int32, (8, cols), 0) % row_count + tile * row_count
    )
    ref_copy.wait()
    weight = jnp.zeros((8, cols), jnp.float32)
    for i in range(refs.shape[0]):
        weight = weight + jnp.where(flat == refs[i], 1.0, 0.0)
    weight_ref[...] = weight
    columns_copy.wait()

    @pl.when(tile == 0)
    def _():
        share[:96, :] = columns[:96, :LANES]

    @pl.when(tile == 1)
    def _():
        share[:48, :] = columns[96:, :LANES]
        share[48:96, :] = columns[:48, LANES : 2 * LANES]

    @pl.when(tile == 2)
    def _():
        share[:96, :] = columns[48:, LANES : 2 * LANES]

    @pl.when(tile == 3)
    def _():
        left = columns[:80, 2 * LANES :].astype(jnp.float32)
        right = columns[80:, 2 * LANES :].astype(jnp.float32)
        left = jnp.pad(left, ((0, 16), (0, LANES // 2 - rest)))
        right = jnp.pad(right, ((0, 32), (0, LANES // 2 - rest)))
        share[:96, :] = jnp.concatenate([left, right], axis=1).astype(jnp.bfloat16)

    for copy in ins:
        copy.wait()
    flat_blocks = blocks.reshape(count, ifg_count * row_count, width)
    totals = 0.0
    for j in range(count):
        totals = totals + lax.dot_general(
            weight_ref[:, j * width : (j + 1) * width].astype(jnp.bfloat16),
            flat_blocks[j],
            (((1,), (1,)), ((), ())),
            preferred_element_type=jnp.float32,
        )
    row = lax.broadcasted_iota(jnp.int32, totals.shape, 0)
    lane = lax.broadcasted_iota(jnp.int32, totals.shape, 1)
    totals = jnp.sum(jnp.where(row == lane % row_count, totals, 0.0), axis=0, keepdims=True)
    totals = jnp.pad(totals, ((0, 0), (0, 3 * LANES - totals.shape[1])))
    high = totals.astype(jnp.bfloat16).astype(jnp.float32)
    middle = (totals - high).astype(jnp.bfloat16).astype(jnp.float32)
    terms = (high, middle, totals - high - middle)
    row = lax.broadcasted_iota(jnp.int32, (PAD, LANES), 0)
    under = jnp.zeros((PAD, LANES), jnp.float32)
    for t, term in enumerate(terms):
        for c in range(3):
            under = jnp.where(row == 3 * t + c, term[:, c * LANES : (c + 1) * LANES], under)
    share[96:, :] = under.astype(jnp.bfloat16)


def pack(ref_pixels, ifgs, columns, blocks):
    ifg_count, row_count, cols = ifgs.shape
    shape = (blocks, ifg_count, row_count, cols // blocks)
    return pl.pallas_call(
        functools.partial(pack_kernel, row_count),
        out_shape=(pltpu.VMEM(shape, jnp.bfloat16), pltpu.VMEM((96 + PAD, LANES), jnp.bfloat16)),
        in_specs=[ANY] * 3,
        out_specs=(VMEM, VMEM),
        scratch_shapes=[
            pltpu.SMEM(ref_pixels.shape, jnp.int32),
            pltpu.VMEM(columns.shape, jnp.bfloat16),
            pltpu.VMEM((8, cols), jnp.float32),
            pltpu.SemaphoreType.DMA((blocks,)),
            pltpu.SemaphoreType.DMA((2,)),
        ],
        name="pack",
    )(ref_pixels, ifgs, columns)


def fit_kernel(date_count, epochs_ref, fit_ref):
    terms, lanes = fit_ref.shape
    index = lax.broadcasted_iota(jnp.int32, (terms, lanes), 1)
    row = lax.broadcasted_iota(jnp.int32, (terms, lanes), 0)
    days = index.astype(jnp.float32)
    scaled = 2.0 * days / (date_count - 1) - 1.0
    years = days * 12.0 / 365.25
    smooth = [
        jnp.ones_like(days),
        scaled,
        scaled * scaled,
        scaled * scaled * scaled,
        jnp.sin(2.0 * math.pi * years),
        jnp.cos(2.0 * math.pi * years),
        jnp.sin(4.0 * math.pi * years),
        jnp.cos(4.0 * math.pi * years),
    ]
    matrix = jnp.zeros((terms, lanes), jnp.float32)
    for r, values in enumerate(smooth):
        matrix = jnp.where(row == r, values, matrix)
    for e in range(epochs_ref.shape[0]):
        step = jnp.where(index >= epochs_ref[e], 1.0, 0.0)
        matrix = jnp.where(row == len(smooth) + e, step, matrix)
    matrix = jnp.where(index < date_count, matrix, 0.0)
    normal = lax.dot_general(
        matrix,
        matrix,
        (((1,), (1,)), ((), ())),
        precision=lax.Precision.HIGHEST,
        preferred_element_type=jnp.float32,
    )
    place = lax.broadcasted_iota(jnp.int32, (terms, terms), 0)
    diagonal = place == lax.broadcasted_iota(jnp.int32, (terms, terms), 1)
    normal = normal + jnp.where(diagonal, RIDGE, 0.0)
    for j in range(terms):
        scale = 1.0 / normal[j : j + 1, j : j + 1]
        pivot, right = normal[j : j + 1, :] * scale, matrix[j : j + 1, :] * scale
        factor = normal[:, j : j + 1]
        normal = jnp.where(place == j, pivot, normal - factor * pivot)
        matrix = jnp.where(row == j, right, matrix - factor * right)
    fit_ref[...] = matrix


def prepare_kernel(row_count, region_size, *refs):
    *part_refs, operator_ref, mean_ref, all_ref, sums_ref = refs
    pairs, width = mean_ref.shape
    ifg, tile = lax.axis_index("ifg"), lax.axis_index("tile")
    blocks = 2 * PLANES
    ifg_count = pairs // blocks
    for position, part_ref in enumerate(part_refs):
        flip, away = position // 2, position % 2
        holder = tile ^ flip
        far = PLANES - 1 - holder % 2
        for slot, (plane, other) in enumerate(((0, 0), (1, 0), (far, 0), (far, 1))):
            all_ref[holder ^ other, ifg ^ (2 * plane + away)] = part_ref[slot]
    row = lax.broadcasted_iota(jnp.int32, (4 * PAD, 3 * width), 0) % PAD
    lane = lax.broadcasted_iota(jnp.int32, (4 * PAD, 3 * width), 1)
    select = jnp.where((row < 9) & (row % 3 == lane // width), 1.0, 0.0).astype(jnp.bfloat16)
    for block in range(blocks):
        top = block * ifg_count
        operator_ref[top : top + 96, :LANES] = all_ref[0, block, :96, :]
        operator_ref[top + 96 : top + 144, :LANES] = all_ref[1, block, :48, :]
        operator_ref[top : top + 48, LANES : 2 * LANES] = all_ref[1, block, 48:96, :]
        operator_ref[top + 48 : top + 144, LANES : 2 * LANES] = all_ref[2, block, :96, :]
        rest = all_ref[3, block, :80, :].astype(jnp.float32)
        blank = jnp.zeros((80, LANES // 2), jnp.float32)
        left = jnp.concatenate([rest[:, : LANES // 2], blank], axis=1)
        right = jnp.concatenate([rest[:, LANES // 2 :], blank], axis=1)
        operator_ref[top : top + 80, 2 * LANES :] = left.astype(jnp.bfloat16)
        operator_ref[top + 80 : top + 144, 2 * LANES :] = right[:64].astype(jnp.bfloat16)
        totals = lax.dot_general(
            jnp.concatenate([all_ref[t, block, 96:, :] for t in range(4)]),
            select,
            (((0,), (0,)), ((), ())),
            preferred_element_type=jnp.float32,
        )
        for c in range(3):
            top_row, count = c * LANES, min(LANES, row_count * ifg_count - c * LANES)
            sums_ref[top_row : top_row + count, :] = totals[:count, c * width : (c + 1) * width]
        total = sums_ref[pl.ds(0, ifg_count, stride=row_count), :]
        for r in range(1, row_count):
            total = total + sums_ref[pl.ds(r, ifg_count, stride=row_count), :]
        if region_size & (region_size - 1):
            mean_ref[top : top + ifg_count, :] = total / region_size
        else:
            mean_ref[top : top + ifg_count, :] = total * (1.0 / region_size)


def invert_kernel(row_count, dates, recv_ref, operator_ref, mean_ref, incidence_ref, fit_ref,
                  coeff_ref, spread_ref, wide_ref, corr_ref):
    blocks, rows, width = recv_ref.shape
    ifg_count = rows // row_count
    spans = []
    for block in range(blocks):
        span = slice(block * ifg_count, (block + 1) * ifg_count)
        spans.append((span, span))
        wide_ref[:rows, :] = recv_ref[block].astype(jnp.float32)
        mean = mean_ref[span, :]
        for r in range(row_count):
            values = wide_ref[pl.ds(r, ifg_count, stride=row_count), :]
            corr_ref[span, r * width : (r + 1) * width] = (values - mean).astype(jnp.bfloat16)
    displacement = lax.dot_general(
        operator_ref[:, :dates],
        corr_ref[...],
        (((0,), (0,)), ((), ())),
        preferred_element_type=jnp.float32,
    )
    finish(row_count, displacement, spans, incidence_ref, fit_ref, coeff_ref, spread_ref, corr_ref)


def finish(row_count, displacement, spans, incidence_ref, fit_ref, coeff_ref, spread_ref, corr_ref):
    pairs = incidence_ref.shape[0]
    width = corr_ref.shape[1] // row_count
    dates = displacement.shape[0]
    coeffs = jnp.dot(
        fit_ref[:, :dates],
        displacement,
        precision=lax.Precision.HIGHEST,
        preferred_element_type=jnp.float32,
    )
    high = displacement.astype(jnp.bfloat16)
    low = (displacement - high.astype(jnp.float32)).astype(jnp.bfloat16)
    blank = jnp.zeros((incidence_ref.shape[1] - 2 * dates + 256, high.shape[1]), jnp.bfloat16)
    rest = jnp.concatenate([high[256:], low[256:], blank])
    total = jnp.zeros((8, row_count * width), jnp.float32)
    for span, rows in spans:
        incidence = incidence_ref[span, :256]
        predicted = (
            jnp.dot(incidence, high[:256], preferred_element_type=jnp.float32)
            + jnp.dot(incidence, low[:256], preferred_element_type=jnp.float32)
            + jnp.dot(incidence_ref[span, 256:], rest, preferred_element_type=jnp.float32)
        )
        misfit = corr_ref[rows, :].astype(jnp.float32) - predicted
        total = total + jnp.sum((misfit * misfit).reshape(-1, 8, misfit.shape[1]), axis=0)
    spread = jnp.sqrt(jnp.sum(total, axis=0, keepdims=True) / pairs + EPS)
    for r in range(row_count):
        coeff_ref[:, r, :] = coeffs[:, r * width : (r + 1) * width]
        spread_ref[r : r + 1, :] = spread[:, r * width : (r + 1) * width]


def trade(array, bit):
    size = lax.axis_size("ifg")
    return lax.ppermute(array, "ifg", [(i, i ^ bit) for i in range(size)])


def trade_and_swap(array, bit, other):
    size, tiles = lax.axis_size("ifg"), lax.axis_size("tile")
    moves = [
        (i * tiles + t, (i ^ bit) * tiles + (t ^ other)) for i in range(size) for t in range(tiles)
    ]
    return lax.ppermute(array, ("ifg", "tile"), moves)


def small_slice(ifgs, pairs, pseudo_inverse, ref_pixels, epochs):
    ifg_count, row_count, cols = ifgs.shape
    blocks = lax.axis_size("ifg")
    width = cols // blocks
    date_count = pseudo_inverse.shape[0]
    pair_count = blocks * ifg_count
    lanes = 3 * LANES
    dates = -(-date_count // 16) * 16

    send, share = pack(ref_pixels, ifgs, pseudo_inverse.T, blocks)
    pair = jnp.stack([share, swap(share, 1)])
    send, pair = lax.optimization_barrier((send, pair))
    tiles = lax.axis_size("tile")
    far = [
        (i * tiles + t, (i ^ (2 * (PLANES - 1 - t % 2))) * tiles + t)
        for i in range(blocks)
        for t in range(tiles)
    ]
    far = lax.ppermute(pair, ("ifg", "tile"), far)
    near = trade(share, 2)
    recv = lax.all_to_all(
        send.reshape(blocks, ifg_count * row_count, width), "ifg", 0, 0, tiled=True
    )
    own = jnp.stack([share, near, far[0], far[1]])
    own, pairs, epochs = lax.optimization_barrier((own, pairs, epochs))
    across = trade(own, 1)
    up = swap(own, 2)
    across_up = trade_and_swap(own, 1, 2)
    incidence = incidence_matrix(pairs, dates)
    terms = 8 + epochs.shape[0]
    fit = pl.pallas_call(
        functools.partial(fit_kernel, date_count),
        out_shape=pltpu.VMEM((terms, lanes), jnp.float32),
        in_specs=[SMEM],
        out_specs=VMEM,
        compiler_params=SMALL,
        name="fit",
    )(epochs)
    across, incidence, fit = lax.optimization_barrier((across, incidence, fit))
    parts = [own, across, swap(own, 1), swap(across, 1)]
    parts = parts + [up, across_up, swap(up, 1), swap(across_up, 1)]
    operator, means = pl.pallas_call(
        functools.partial(prepare_kernel, row_count, ref_pixels.shape[0]),
        out_shape=(
            pltpu.VMEM((pair_count, lanes), jnp.bfloat16),
            pltpu.VMEM((pair_count, width), jnp.float32),
        ),
        in_specs=[VMEM] * 8,
        out_specs=(VMEM, VMEM),
        scratch_shapes=[
            pltpu.VMEM((4, blocks) + share.shape, jnp.bfloat16),
            pltpu.VMEM((row_count * ifg_count + SPARE, width), jnp.float32),
        ],
        compiler_params=SMALL,
        cost_estimate=pl.CostEstimate(flops=COST, bytes_accessed=0, transcendentals=0),
        name="prepare",
    )(*parts)
    return pl.pallas_call(
        functools.partial(invert_kernel, row_count, dates),
        out_shape=(
            jax.ShapeDtypeStruct((terms, row_count, width), jnp.float32),
            jax.ShapeDtypeStruct((row_count, width), jnp.float32),
        ),
        in_specs=[VMEM] * 5,
        out_specs=(VMEM, VMEM),
        scratch_shapes=[
            pltpu.VMEM((row_count * ifg_count + SPARE, width), jnp.float32),
            pltpu.VMEM((pair_count, row_count * width), jnp.bfloat16),
        ],
        compiler_params=SMALL,
        name="invert",
    )(recv, operator, means, incidence, fit)


def swap(array, bit):
    size = lax.axis_size("tile")
    return lax.ppermute(array, "tile", [(i, i ^ bit) for i in range(size)])


def tile_gather(array):
    size = lax.axis_size("tile")
    tile = lax.axis_index("tile")
    parts = [array]
    bit = size // 2
    order = []
    while bit:
        parts = parts + [swap(part, bit) for part in parts]
        order.append(bit)
        bit //= 2
    stacked = jnp.stack(parts)
    offset = [0] * size
    for position in range(size):
        mask = 0
        for place, bit in enumerate(order):
            if position >> place & 1:
                mask |= bit
        offset[mask] = position
    stacked = jnp.stack([parts[offset[m]] for m in range(size)])
    for bit in order:
        swapped = stacked.reshape((size // (2 * bit), 2, bit) + array.shape)
        swapped = jnp.flip(swapped, axis=1).reshape(stacked.shape)
        stacked = jnp.where((tile & bit) != 0, swapped, stacked)
    return stacked


def split_sum(value):
    high = lax.reduce_precision(value, 8, 7)
    middle = lax.reduce_precision(value - high, 8, 7)
    low = lax.reduce_precision(value - high - middle, 8, 7)
    return jnp.stack([high, middle, low]).astype(jnp.bfloat16)


def shards(ifgs, pairs, pseudo_inverse, ref_pixels, epochs):
    ifg_count, row_count, cols = ifgs.shape
    blocks = lax.axis_size("ifg")
    tiles = lax.axis_size("tile")
    shape = (blocks, tiles, ifg_count, row_count, cols // blocks)
    dates = pseudo_inverse.shape[0]
    if shape == (2 * PLANES, 4, 144, 2, LANES) and 2 * LANES < dates <= 320:
        return small_slice(ifgs, pairs, pseudo_inverse, ref_pixels, epochs)
    width = cols // blocks
    date_count = pseudo_inverse.shape[0]
    pair_count = blocks * ifg_count
    dates = -(-date_count // 16) * 16
    tile = lax.axis_index("tile")

    send = ifgs.reshape(ifg_count, row_count, blocks, width).transpose(2, 0, 1, 3)
    send = send.reshape(blocks, ifg_count * row_count, width)

    share = -(-ifg_count // tiles)
    columns = jnp.pad(pseudo_inverse.T, ((0, share * tiles - ifg_count), (0, 0)))
    columns = lax.dynamic_slice_in_dim(columns, tile * share, share, 0)
    lanes = max(date_count, ifg_count)
    sums = split_sum(partial_sums(ifgs, send, ref_pixels))
    payload = jnp.concatenate(
        [
            jnp.pad(columns, ((0, 0), (0, lanes - date_count))),
            jnp.pad(sums, ((0, 0), (0, lanes - ifg_count))),
        ]
    )
    payload = jnp.broadcast_to(payload[None], (blocks,) + payload.shape)
    payload = lax.all_to_all(payload, "ifg", 0, 0, tiled=True)
    recv = lax.all_to_all(send, "ifg", 0, 0, tiled=True)
    gathered = tile_gather(payload)

    inverse = gathered[:, :, :share, :date_count].transpose(3, 1, 0, 2)
    inverse = inverse.reshape(date_count, blocks, tiles * share)[:, :, :ifg_count]
    inverse = jnp.pad(
        inverse.reshape(date_count, pair_count), ((0, dates - date_count), (0, 0))
    )
    totals = jnp.sum(gathered[:, :, share:, :ifg_count].astype(jnp.float32), axis=(0, 2))
    means = (totals / ref_pixels.shape[0]).reshape(pair_count, 1)
    means = jnp.broadcast_to(means, (pair_count, width))
    incidence = incidence_matrix(pairs, dates)
    fit = jnp.pad(fit_operator(epochs, date_count), ((0, 0), (0, dates - date_count)))

    terms = fit.shape[0]
    return pl.pallas_call(
        functools.partial(post_kernel, row_count),
        out_shape=(
            jax.ShapeDtypeStruct((terms, row_count, width), jnp.float32),
            jax.ShapeDtypeStruct((row_count, width), jnp.float32),
        ),
        in_specs=[VMEM] * 5,
        out_specs=(VMEM, VMEM),
        scratch_shapes=[
            pltpu.VMEM(
                (row_count * (128 if pair_count % 128 == 0 else pair_count), width), jnp.float32
            ),
            pltpu.VMEM((pair_count, row_count * width), jnp.bfloat16),
        ],
        compiler_params=pltpu.CompilerParams(vmem_limit_bytes=32 * 1024 * 1024),
        name="invert",
    )(recv.reshape(pair_count * row_count, width), means, inverse, incidence, fit)


def solution(mesh):
    in_specs = (P("ifg", "tile", None), P(), P(None, "ifg"), P(), P())
    out_specs = (P(None, "tile", "ifg"), P("tile", "ifg"))
    return jax.shard_map(shards, mesh=mesh, in_specs=in_specs, out_specs=out_specs, check_vma=False)
```

```python
import functools
import math

import jax
import jax.numpy as jnp
from jax import lax
from jax.experimental import pallas as pl
from jax.experimental.pallas import tpu as pltpu
from jax.sharding import PartitionSpec as P

EPS = 1e-06
RIDGE = 1.0
VMEM = pl.BlockSpec(memory_space=pltpu.VMEM)
SMEM = pl.BlockSpec(memory_space=pltpu.SMEM)


def design(epochs, count):
    index = jnp.arange(count, dtype=jnp.int32)
    days = index.astype(jnp.float32)
    scaled = 2.0 * days / (count - 1) - 1.0
    years = days * 12.0 / 365.25
    smooth = jnp.stack(
        [
            jnp.ones_like(days),
            scaled,
            scaled * scaled,
            scaled * scaled * scaled,
            jnp.sin(2.0 * math.pi * years),
            jnp.cos(2.0 * math.pi * years),
            jnp.sin(4.0 * math.pi * years),
            jnp.cos(4.0 * math.pi * years),
        ],
        axis=1,
    )
    jumps = (index[:, None] >= epochs[None, :]).astype(jnp.float32)
    return jnp.concatenate([smooth, jumps], axis=1)


def fit_operator(epochs, count):
    matrix = design(epochs, count)
    normal = jnp.dot(
        matrix.T, matrix, precision=lax.Precision.HIGHEST, preferred_element_type=jnp.float32
    )
    normal = normal + RIDGE * jnp.eye(matrix.shape[1], dtype=jnp.float32)
    factor = jnp.linalg.cholesky(normal)
    return jax.scipy.linalg.cho_solve((factor, True), matrix.T)


def incidence_matrix(pairs, count):
    dates = jnp.arange(-(-(2 * count - 256) // 128) * 128, dtype=jnp.int32)
    dates = jnp.where(dates < count, dates, jnp.where(dates < 2 * count - 256, dates - count + 256, -1))
    later = (pairs[:, 1:2] == dates[None, :]).astype(jnp.bfloat16)
    earlier = (pairs[:, 0:1] == dates[None, :]).astype(jnp.bfloat16)
    return later - earlier


def sums_kernel(row_count, ref_ref, send_ref, out_ref, acc_ref):
    blocks, rows, width = send_ref.shape
    ifg_count = rows // row_count
    cols = blocks * width
    first = lax.axis_index("tile") * row_count
    row = lax.broadcasted_iota(jnp.int32, (8, cols), 0) % row_count + first
    flat = row * cols + lax.broadcasted_iota(jnp.int32, (8, cols), 1)

    def count(i, weight):
        return weight + jnp.where(flat == ref_ref[i], 1.0, 0.0)

    weight = lax.fori_loop(
        0, ref_ref.shape[0], count, jnp.zeros((8, cols), jnp.float32), unroll=8
    )
    acc = jnp.zeros((rows // 8, 8, width), jnp.float32)
    for j in range(blocks):
        values = send_ref[j].astype(jnp.float32).reshape(rows // 8, 8, width)
        acc = acc + values * weight[None, :, j * width : (j + 1) * width]
    acc_ref[...] = acc.reshape(rows, width)
    per_ifg = acc_ref[pl.ds(0, ifg_count, stride=row_count), :]
    for r in range(1, row_count):
        per_ifg = per_ifg + acc_ref[pl.ds(r, ifg_count, stride=row_count), :]
    out_ref[...] = lax.dot_general(
        jnp.ones((8, width), jnp.float32),
        per_ifg,
        (((1,), (1,)), ((), ())),
        precision=lax.Precision.HIGHEST,
        preferred_element_type=jnp.float32,
    )


def partial_sums(ifgs, send, ref_pixels):
    ifg_count, row_count, cols = ifgs.shape
    if send.shape[1] % 16:
        tile = lax.axis_index("tile")
        pixel = jnp.arange(row_count * cols, dtype=jnp.int32) + tile * row_count * cols
        weight = jnp.sum((ref_pixels[:, None] == pixel[None, :]).astype(jnp.float32), axis=0)
        weight = weight.reshape(1, row_count, cols)
        return jnp.sum(ifgs.astype(jnp.float32) * weight, axis=(1, 2))
    sums = pl.pallas_call(
        functools.partial(sums_kernel, row_count),
        out_shape=jax.ShapeDtypeStruct((8, ifg_count), jnp.float32),
        in_specs=[SMEM, VMEM],
        out_specs=VMEM,
        scratch_shapes=[pltpu.VMEM(send.shape[1:], jnp.float32)],
        name="region_sums",
    )(ref_pixels, send)
    return sums[0]


def post_kernel(row_count, recv_ref, mean_ref, inverse_ref, incidence_ref, fit_ref,
                coeff_ref, spread_ref, wide_ref, corr_ref):
    pairs = incidence_ref.shape[0]
    width = recv_ref.shape[1]
    step = 128 if pairs % 128 == 0 else pairs
    for k in range(0, pairs, step):
        wide_ref[...] = recv_ref[row_count * k : row_count * (k + step), :].astype(jnp.float32)
        mean = mean_ref[k : k + step, :]
        for r in range(row_count):
            values = wide_ref[pl.ds(r, step, stride=row_count), :]
            corr_ref[k : k + step, r * width : (r + 1) * width] = (values - mean).astype(
                jnp.bfloat16
            )
    displacement = jnp.dot(
        inverse_ref[...], corr_ref[...], preferred_element_type=jnp.float32
    )
    spans = [(slice(k, k + step), slice(k, k + step)) for k in range(0, pairs, step)]
    finish(row_count, displacement, spans, incidence_ref, fit_ref, coeff_ref, spread_ref, corr_ref)


ANY = pl.BlockSpec(memory_space=pl.ANY)
PAD = 16
PLANES = 4
SPARE = 8
COST = 6_000_000_000
LANES = 128
SMALL = pltpu.CompilerParams(vmem_limit_bytes=16 * 1024 * 1024)


def pack_kernel(row_count, ref_hbm, ifgs_hbm, columns_hbm, blocks, share,
                refs, columns, weight_ref, in_sems, misc_sems):
    ifg_count, _, cols = ifgs_hbm.shape
    count, width = blocks.shape[0], blocks.shape[3]
    rest = columns.shape[1] - 2 * LANES
    ref_copy = pltpu.make_async_copy(ref_hbm, refs, misc_sems.at[0])
    ref_copy.start()
    ins = [
        pltpu.make_async_copy(
            ifgs_hbm.at[:, :, pl.ds(j * width, width)], blocks.at[j], in_sems.at[j]
        )
        for j in range(count)
    ]
    for copy in ins:
        copy.start()
    columns_copy = pltpu.make_async_copy(columns_hbm, columns, misc_sems.at[1])
    columns_copy.start()
    tile = lax.axis_index("tile")
    flat = lax.broadcasted_iota(jnp.int32, (8, cols), 1) + cols * (
        lax.broadcasted_iota(jnp.int32, (8, cols), 0) % row_count + tile * row_count
    )
    ref_copy.wait()
    weight = jnp.zeros((8, cols), jnp.float32)
    for i in range(refs.shape[0]):
        weight = weight + jnp.where(flat == refs[i], 1.0, 0.0)
    weight_ref[...] = weight
    columns_copy.wait()

    @pl.when(tile == 0)
    def _():
        share[:96, :] = columns[:96, :LANES]

    @pl.when(tile == 1)
    def _():
        share[:48, :] = columns[96:, :LANES]
        share[48:96, :] = columns[:48, LANES : 2 * LANES]

    @pl.when(tile == 2)
    def _():
        share[:96, :] = columns[48:, LANES : 2 * LANES]

    @pl.when(tile == 3)
    def _():
        left = columns[:80, 2 * LANES :].astype(jnp.float32)
        right = columns[80:, 2 * LANES :].astype(jnp.float32)
        left = jnp.pad(left, ((0, 16), (0, LANES // 2 - rest)))
        right = jnp.pad(right, ((0, 32), (0, LANES // 2 - rest)))
        share[:96, :] = jnp.concatenate([left, right], axis=1).astype(jnp.bfloat16)

    for copy in ins:
        copy.wait()
    flat_blocks = blocks.reshape(count, ifg_count * row_count, width)
    totals = 0.0
    for j in range(count):
        totals = totals + lax.dot_general(
            weight_ref[:, j * width : (j + 1) * width].astype(jnp.bfloat16),
            flat_blocks[j],
            (((1,), (1,)), ((), ())),
            preferred_element_type=jnp.float32,
        )
    row = lax.broadcasted_iota(jnp.int32, totals.shape, 0)
    lane = lax.broadcasted_iota(jnp.int32, totals.shape, 1)
    totals = jnp.sum(jnp.where(row == lane % row_count, totals, 0.0), axis=0, keepdims=True)
    totals = jnp.pad(totals, ((0, 0), (0, 3 * LANES - totals.shape[1])))
    high = totals.astype(jnp.bfloat16).astype(jnp.float32)
    middle = (totals - high).astype(jnp.bfloat16).astype(jnp.float32)
    terms = (high, middle, totals - high - middle)
    row = lax.broadcasted_iota(jnp.int32, (PAD, LANES), 0)
    under = jnp.zeros((PAD, LANES), jnp.float32)
    for t, term in enumerate(terms):
        for c in range(3):
            under = jnp.where(row == 3 * t + c, term[:, c * LANES : (c + 1) * LANES], under)
    share[96:, :] = under.astype(jnp.bfloat16)


def pack(ref_pixels, ifgs, columns, blocks):
    ifg_count, row_count, cols = ifgs.shape
    shape = (blocks, ifg_count, row_count, cols // blocks)
    return pl.pallas_call(
        functools.partial(pack_kernel, row_count),
        out_shape=(pltpu.VMEM(shape, jnp.bfloat16), pltpu.VMEM((96 + PAD, LANES), jnp.bfloat16)),
        in_specs=[ANY] * 3,
        out_specs=(VMEM, VMEM),
        scratch_shapes=[
            pltpu.SMEM(ref_pixels.shape, jnp.int32),
            pltpu.VMEM(columns.shape, jnp.bfloat16),
            pltpu.VMEM((8, cols), jnp.float32),
            pltpu.SemaphoreType.DMA((blocks,)),
            pltpu.SemaphoreType.DMA((2,)),
        ],
        name="pack",
    )(ref_pixels, ifgs, columns)


def fit_kernel(date_count, epochs_ref, fit_ref):
    terms, lanes = fit_ref.shape
    index = lax.broadcasted_iota(jnp.int32, (terms, lanes), 1)
    row = lax.broadcasted_iota(jnp.int32, (terms, lanes), 0)
    days = index.astype(jnp.float32)
    scaled = 2.0 * days / (date_count - 1) - 1.0
    years = days * 12.0 / 365.25
    smooth = [
        jnp.ones_like(days),
        scaled,
        scaled * scaled,
        scaled * scaled * scaled,
        jnp.sin(2.0 * math.pi * years),
        jnp.cos(2.0 * math.pi * years),
        jnp.sin(4.0 * math.pi * years),
        jnp.cos(4.0 * math.pi * years),
    ]
    matrix = jnp.zeros((terms, lanes), jnp.float32)
    for r, values in enumerate(smooth):
        matrix = jnp.where(row == r, values, matrix)
    for e in range(epochs_ref.shape[0]):
        step = jnp.where(index >= epochs_ref[e], 1.0, 0.0)
        matrix = jnp.where(row == len(smooth) + e, step, matrix)
    matrix = jnp.where(index < date_count, matrix, 0.0)
    normal = lax.dot_general(
        matrix,
        matrix,
        (((1,), (1,)), ((), ())),
        precision=lax.Precision.HIGHEST,
        preferred_element_type=jnp.float32,
    )
    place = lax.broadcasted_iota(jnp.int32, (terms, terms), 0)
    diagonal = place == lax.broadcasted_iota(jnp.int32, (terms, terms), 1)
    normal = normal + jnp.where(diagonal, RIDGE, 0.0)
    for j in range(terms):
        scale = 1.0 / normal[j : j + 1, j : j + 1]
        pivot, right = normal[j : j + 1, :] * scale, matrix[j : j + 1, :] * scale
        factor = normal[:, j : j + 1]
        normal = jnp.where(place == j, pivot, normal - factor * pivot)
        matrix = jnp.where(row == j, right, matrix - factor * right)
    fit_ref[...] = matrix


def prepare_kernel(row_count, region_size, *refs):
    *part_refs, operator_ref, mean_ref, all_ref, sums_ref = refs
    pairs, width = mean_ref.shape
    ifg, tile = lax.axis_index("ifg"), lax.axis_index("tile")
    blocks = 2 * PLANES
    ifg_count = pairs // blocks
    for position, part_ref in enumerate(part_refs):
        flip, away = position // 2, position % 2
        holder = tile ^ flip
        far = PLANES - 1 - holder % 2
        for slot, (plane, other) in enumerate(((0, 0), (1, 0), (far, 0), (far, 1))):
            all_ref[holder ^ other, ifg ^ (2 * plane + away)] = part_ref[slot]
    row = lax.broadcasted_iota(jnp.int32, (4 * PAD, 3 * width), 0) % PAD
    lane = lax.broadcasted_iota(jnp.int32, (4 * PAD, 3 * width), 1)
    select = jnp.where((row < 9) & (row % 3 == lane // width), 1.0, 0.0).astype(jnp.bfloat16)
    for block in range(blocks):
        top = block * ifg_count
        operator_ref[top : top + 96, :LANES] = all_ref[0, block, :96, :]
        operator_ref[top + 96 : top + 144, :LANES] = all_ref[1, block, :48, :]
        operator_ref[top : top + 48, LANES : 2 * LANES] = all_ref[1, block, 48:96, :]
        operator_ref[top + 48 : top + 144, LANES : 2 * LANES] = all_ref[2, block, :96, :]
        rest = all_ref[3, block, :80, :].astype(jnp.float32)
        blank = jnp.zeros((80, LANES // 2), jnp.float32)
        left = jnp.concatenate([rest[:, : LANES // 2], blank], axis=1)
        right = jnp.concatenate([rest[:, LANES // 2 :], blank], axis=1)
        operator_ref[top : top + 80, 2 * LANES :] = left.astype(jnp.bfloat16)
        operator_ref[top + 80 : top + 144, 2 * LANES :] = right[:64].astype(jnp.bfloat16)
        totals = lax.dot_general(
            jnp.concatenate([all_ref[t, block, 96:, :] for t in range(4)]),
            select,
            (((0,), (0,)), ((), ())),
            preferred_element_type=jnp.float32,
        )
        for c in range(3):
            top_row, count = c * LANES, min(LANES, row_count * ifg_count - c * LANES)
            sums_ref[top_row : top_row + count, :] = totals[:count, c * width : (c + 1) * width]
        total = sums_ref[pl.ds(0, ifg_count, stride=row_count), :]
        for r in range(1, row_count):
            total = total + sums_ref[pl.ds(r, ifg_count, stride=row_count), :]
        if region_size & (region_size - 1):
            mean_ref[top : top + ifg_count, :] = total / region_size
        else:
            mean_ref[top : top + ifg_count, :] = total * (1.0 / region_size)


def invert_kernel(row_count, dates, recv_ref, operator_ref, mean_ref, incidence_ref, fit_ref,
                  coeff_ref, spread_ref, wide_ref, corr_ref):
    blocks, rows, width = recv_ref.shape
    ifg_count = rows // row_count
    spans = []
    for block in range(blocks):
        span = slice(block * ifg_count, (block + 1) * ifg_count)
        spans.append((span, span))
        wide_ref[:rows, :] = recv_ref[block].astype(jnp.float32)
        mean = mean_ref[span, :]
        for r in range(row_count):
            values = wide_ref[pl.ds(r, ifg_count, stride=row_count), :]
            corr_ref[span, r * width : (r + 1) * width] = (values - mean).astype(jnp.bfloat16)
    displacement = lax.dot_general(
        operator_ref[:, :dates],
        corr_ref[...],
        (((0,), (0,)), ((), ())),
        preferred_element_type=jnp.float32,
    )
    finish(row_count, displacement, spans, incidence_ref, fit_ref, coeff_ref, spread_ref, corr_ref)


def finish(row_count, displacement, spans, incidence_ref, fit_ref, coeff_ref, spread_ref, corr_ref):
    pairs = incidence_ref.shape[0]
    width = corr_ref.shape[1] // row_count
    dates = displacement.shape[0]
    high = displacement.astype(jnp.bfloat16)
    low = (displacement - high.astype(jnp.float32)).astype(jnp.bfloat16)
    last = displacement - high.astype(jnp.float32) - low.astype(jnp.float32)
    fit = fit_ref[:, :dates]
    terms = fit.shape[0]
    fit_high = fit.astype(jnp.bfloat16)
    fit = fit - fit_high.astype(jnp.float32)
    fit_middle = fit.astype(jnp.bfloat16)
    fit_low = (fit - fit_middle.astype(jnp.float32)).astype(jnp.bfloat16)
    fits = jnp.concatenate([fit_high, fit_middle, fit_low])
    one = jnp.dot(fits, high, preferred_element_type=jnp.float32)
    two = jnp.dot(fits[: 2 * terms], low, preferred_element_type=jnp.float32)
    three = jnp.dot(fit_high, last.astype(jnp.bfloat16), preferred_element_type=jnp.float32)
    coeffs = one[2 * terms :] + two[terms:] + three
    coeffs = one[:terms] + (one[terms : 2 * terms] + two[:terms] + coeffs)
    blank = jnp.zeros((incidence_ref.shape[1] - 2 * dates + 256, high.shape[1]), jnp.bfloat16)
    rest = jnp.concatenate([high[256:], low[256:], blank])
    total = jnp.zeros((8, row_count * width), jnp.float32)
    for span, rows in spans:
        incidence = incidence_ref[span, :256]
        predicted = (
            jnp.dot(incidence, high[:256], preferred_element_type=jnp.float32)
            + jnp.dot(incidence, low[:256], preferred_element_type=jnp.float32)
            + jnp.dot(incidence_ref[span, 256:], rest, preferred_element_type=jnp.float32)
        )
        misfit = corr_ref[rows, :].astype(jnp.float32) - predicted
        total = total + jnp.sum((misfit * misfit).reshape(-1, 8, misfit.shape[1]), axis=0)
    spread = jnp.sqrt(jnp.sum(total, axis=0, keepdims=True) / pairs + EPS)
    for r in range(row_count):
        coeff_ref[:, r, :] = coeffs[:, r * width : (r + 1) * width]
        spread_ref[r : r + 1, :] = spread[:, r * width : (r + 1) * width]


def trade(array, bit):
    size = lax.axis_size("ifg")
    return lax.ppermute(array, "ifg", [(i, i ^ bit) for i in range(size)])


def trade_and_swap(array, bit, other):
    size, tiles = lax.axis_size("ifg"), lax.axis_size("tile")
    moves = [
        (i * tiles + t, (i ^ bit) * tiles + (t ^ other)) for i in range(size) for t in range(tiles)
    ]
    return lax.ppermute(array, ("ifg", "tile"), moves)


def small_slice(ifgs, pairs, pseudo_inverse, ref_pixels, epochs):
    ifg_count, row_count, cols = ifgs.shape
    blocks = lax.axis_size("ifg")
    width = cols // blocks
    date_count = pseudo_inverse.shape[0]
    pair_count = blocks * ifg_count
    lanes = 3 * LANES
    dates = -(-date_count // 16) * 16

    send, share = pack(ref_pixels, ifgs, pseudo_inverse.T, blocks)
    pair = jnp.stack([share, swap(share, 1)])
    send, pair = lax.optimization_barrier((send, pair))
    tiles = lax.axis_size("tile")
    far = [
        (i * tiles + t, (i ^ (2 * (PLANES - 1 - t % 2))) * tiles + t)
        for i in range(blocks)
        for t in range(tiles)
    ]
    far = lax.ppermute(pair, ("ifg", "tile"), far)
    near = trade(share, 2)
    recv = lax.all_to_all(
        send.reshape(blocks, ifg_count * row_count, width), "ifg", 0, 0, tiled=True
    )
    own = jnp.stack([share, near, far[0], far[1]])
    own, pairs, epochs = lax.optimization_barrier((own, pairs, epochs))
    across = trade(own, 1)
    up = swap(own, 2)
    across_up = trade_and_swap(own, 1, 2)
    incidence = incidence_matrix(pairs, dates)
    terms = 8 + epochs.shape[0]
    fit = pl.pallas_call(
        functools.partial(fit_kernel, date_count),
        out_shape=pltpu.VMEM((terms, lanes), jnp.float32),
        in_specs=[SMEM],
        out_specs=VMEM,
        compiler_params=SMALL,
        name="fit",
    )(epochs)
    across, incidence, fit = lax.optimization_barrier((across, incidence, fit))
    parts = [own, across, swap(own, 1), swap(across, 1)]
    parts = parts + [up, across_up, swap(up, 1), swap(across_up, 1)]
    operator, means = pl.pallas_call(
        functools.partial(prepare_kernel, row_count, ref_pixels.shape[0]),
        out_shape=(
            pltpu.VMEM((pair_count, lanes), jnp.bfloat16),
            pltpu.VMEM((pair_count, width), jnp.float32),
        ),
        in_specs=[VMEM] * 8,
        out_specs=(VMEM, VMEM),
        scratch_shapes=[
            pltpu.VMEM((4, blocks) + share.shape, jnp.bfloat16),
            pltpu.VMEM((row_count * ifg_count + SPARE, width), jnp.float32),
        ],
        compiler_params=SMALL,
        cost_estimate=pl.CostEstimate(flops=COST, bytes_accessed=0, transcendentals=0),
        name="prepare",
    )(*parts)
    return pl.pallas_call(
        functools.partial(invert_kernel, row_count, dates),
        out_shape=(
            jax.ShapeDtypeStruct((terms, row_count, width), jnp.float32),
            jax.ShapeDtypeStruct((row_count, width), jnp.float32),
        ),
        in_specs=[VMEM] * 5,
        out_specs=(VMEM, VMEM),
        scratch_shapes=[
            pltpu.VMEM((row_count * ifg_count + SPARE, width), jnp.float32),
            pltpu.VMEM((pair_count, row_count * width), jnp.bfloat16),
        ],
        compiler_params=SMALL,
        name="invert",
    )(recv, operator, means, incidence, fit)


def swap(array, bit):
    size = lax.axis_size("tile")
    return lax.ppermute(array, "tile", [(i, i ^ bit) for i in range(size)])


def tile_gather(array):
    size = lax.axis_size("tile")
    tile = lax.axis_index("tile")
    parts = [array]
    bit = size // 2
    order = []
    while bit:
        parts = parts + [swap(part, bit) for part in parts]
        order.append(bit)
        bit //= 2
    stacked = jnp.stack(parts)
    offset = [0] * size
    for position in range(size):
        mask = 0
        for place, bit in enumerate(order):
            if position >> place & 1:
                mask |= bit
        offset[mask] = position
    stacked = jnp.stack([parts[offset[m]] for m in range(size)])
    for bit in order:
        swapped = stacked.reshape((size // (2 * bit), 2, bit) + array.shape)
        swapped = jnp.flip(swapped, axis=1).reshape(stacked.shape)
        stacked = jnp.where((tile & bit) != 0, swapped, stacked)
    return stacked


def split_sum(value):
    high = lax.reduce_precision(value, 8, 7)
    middle = lax.reduce_precision(value - high, 8, 7)
    low = lax.reduce_precision(value - high - middle, 8, 7)
    return jnp.stack([high, middle, low]).astype(jnp.bfloat16)


def shards(ifgs, pairs, pseudo_inverse, ref_pixels, epochs):
    ifg_count, row_count, cols = ifgs.shape
    blocks = lax.axis_size("ifg")
    tiles = lax.axis_size("tile")
    shape = (blocks, tiles, ifg_count, row_count, cols // blocks)
    dates = pseudo_inverse.shape[0]
    if shape == (2 * PLANES, 4, 144, 2, LANES) and 2 * LANES < dates <= 320:
        return small_slice(ifgs, pairs, pseudo_inverse, ref_pixels, epochs)
    width = cols // blocks
    date_count = pseudo_inverse.shape[0]
    pair_count = blocks * ifg_count
    dates = -(-date_count // 16) * 16
    tile = lax.axis_index("tile")

    send = ifgs.reshape(ifg_count, row_count, blocks, width).transpose(2, 0, 1, 3)
    send = send.reshape(blocks, ifg_count * row_count, width)

    share = -(-ifg_count // tiles)
    columns = jnp.pad(pseudo_inverse.T, ((0, share * tiles - ifg_count), (0, 0)))
    columns = lax.dynamic_slice_in_dim(columns, tile * share, share, 0)
    lanes = max(date_count, ifg_count)
    sums = split_sum(partial_sums(ifgs, send, ref_pixels))
    payload = jnp.concatenate(
        [
            jnp.pad(columns, ((0, 0), (0, lanes - date_count))),
            jnp.pad(sums, ((0, 0), (0, lanes - ifg_count))),
        ]
    )
    payload = jnp.broadcast_to(payload[None], (blocks,) + payload.shape)
    payload = lax.all_to_all(payload, "ifg", 0, 0, tiled=True)
    recv = lax.all_to_all(send, "ifg", 0, 0, tiled=True)
    gathered = tile_gather(payload)

    inverse = gathered[:, :, :share, :date_count].transpose(3, 1, 0, 2)
    inverse = inverse.reshape(date_count, blocks, tiles * share)[:, :, :ifg_count]
    inverse = jnp.pad(
        inverse.reshape(date_count, pair_count), ((0, dates - date_count), (0, 0))
    )
    totals = jnp.sum(gathered[:, :, share:, :ifg_count].astype(jnp.float32), axis=(0, 2))
    means = (totals / ref_pixels.shape[0]).reshape(pair_count, 1)
    means = jnp.broadcast_to(means, (pair_count, width))
    incidence = incidence_matrix(pairs, dates)
    fit = jnp.pad(fit_operator(epochs, date_count), ((0, 0), (0, dates - date_count)))

    terms = fit.shape[0]
    return pl.pallas_call(
        functools.partial(post_kernel, row_count),
        out_shape=(
            jax.ShapeDtypeStruct((terms, row_count, width), jnp.float32),
            jax.ShapeDtypeStruct((row_count, width), jnp.float32),
        ),
        in_specs=[VMEM] * 5,
        out_specs=(VMEM, VMEM),
        scratch_shapes=[
            pltpu.VMEM(
                (row_count * (128 if pair_count % 128 == 0 else pair_count), width), jnp.float32
            ),
            pltpu.VMEM((pair_count, row_count * width), jnp.bfloat16),
        ],
        compiler_params=pltpu.CompilerParams(vmem_limit_bytes=32 * 1024 * 1024),
        name="invert",
    )(recv.reshape(pair_count * row_count, width), means, inverse, incidence, fit)


def solution(mesh):
    in_specs = (P("ifg", "tile", None), P(), P(None, "ifg"), P(), P())
    out_specs = (P(None, "tile", "ifg"), P("tile", "ifg"))
    return jax.shard_map(shards, mesh=mesh, in_specs=in_specs, out_specs=out_specs, check_vma=False)
```
